128 devices in a mesh: dp: 32 (over x_lo, y, z), tensor: 4 (over x_hi, core).
Axes of the slice: x: 4 (x_hi: 2, x_lo: 2; x = x_hi * 2 + x_lo), y: 4, z: 4, core: 2. Of those that a mesh axis runs over, the one named last changes fastest.
Arguments:
- tokens_in: bfloat16 [150528, 384], P('dp'), may hold values from -6 to 6
- attn_gain: bfloat16 [384], replicated, may hold values from 0.5 to 1.5
- attn_shift: bfloat16 [384], replicated, may hold values from -1.25 to 1.25
- qkv_weight: bfloat16 [3, 384, 384], P(None, None, 'tensor'), may hold values from -0.3125 to 0.3125
- qv_bias: bfloat16 [2, 384], P(None, 'tensor'), may hold values from -1.25 to 1.25
- rel_table: bfloat16 [169, 12], P(None, 'tensor'), may hold values from -6 to 6
- proj_weight: bfloat16 [384, 384], P('tensor'), may hold values from -0.875 to 0.875
- proj_bias: bfloat16 [384], replicated, may hold values from -1.25 to 1.25
- moe_gain: bfloat16 [384], replicated, may hold values from 0.5 to 1.5
- moe_shift: bfloat16 [384], replicated, may hold values from -1.25 to 1.25
- router_weight: bfloat16 [384, 8], replicated, may hold values from -0.21875 to 0.21875
- expert_in: bfloat16 [8, 384, 1536], P(None, None, 'tensor'), may hold values from -0.3125 to 0.3125
- expert_in_bias: bfloat16 [8, 1536], P(None, 'tensor'), may hold values from -0.625 to 0.625
- expert_out: bfloat16 [8, 1536, 384], P(None, 'tensor'), may hold values from -1.25 to 1.25
- expert_out_bias: bfloat16 [8, 384], replicated, may hold values from -3 to 3
- expert_ids: int32 [150528, 1], P('dp'), may hold values from 0 to 7; in each aligned block of 4704 rows (0 to 4703, 4704 to 9407, ...) at most 735 rows name the same one
- cotangent: bfloat16 [150528, 384], P('dp'), may hold values from -6 to 6
Outputs:
- block_out: bfloat16 [150528, 384], P('dp')
- input_grad: float32 [150528, 384], P('dp')
- grad_attn_gain: float32 [384], replicated
- grad_attn_shift: float32 [384], replicated
- grad_qkv_weight: float32 [3, 384, 384], P(None, None, 'tensor')
- grad_qv_bias: float32 [2, 384], P(None, 'tensor')
- grad_rel_table: float32 [169, 12], P(None, 'tensor')
- grad_proj_weight: float32 [384, 384], P('tensor')
- grad_proj_bias: float32 [384], replicated
- grad_moe_gain: float32 [384], replicated
- grad_moe_shift: float32 [384], replicated
- grad_router: float32 [384, 8], replicated
- grad_expert_in: float32 [8, 384, 1536], P(None, None, 'tensor')
- grad_expert_in_bias: float32 [8, 1536], P(None, 'tensor')
- grad_expert_out: float32 [8, 1536, 384], P(None, 'tensor')
- grad_expert_out_bias: float32 [8, 384], replicated
The draws below stay inside these ranges and needn't reach their ends.
Inputs may be any that keep to these rules, and one draw needn't show every extreme that they name: `expert_ids`: in each aligned block of 4704 rows (the tokens of one index of dp) no expert is named by more than 735 rows, and in some block one expert is named by exactly 735 rows.
All inputs are finite; a program needn't handle non-finite values.
Results may differ from the reference program's by a relative error of at most 0.012.
The reference program's roundings to bfloat16 on the way count: a program that leaves them out, or rounds other values in their place, can miss the bound.
Values sent between devices are 32-bit elements; how exact they have to be, the bound alone decides.
No kernel may reach another device: no remote copies, remote signals or barrier semaphores. Data moves between devices by JAX's collectives and lax.ppermute only.
A program may use at most 256 MiB of HBM per device.

```python
import math
import jax
import jax.numpy as jnp
import numpy as np
from jax import lax

D = 384
HEADS = 12
HEAD_DIM = 32
FF = 1536
EXPERTS = 8
SIDE = 14
WINDOW = 7
IMAGE = 196
TABLE = 169
TOKG = 4704
TOKENS = 150528
CAP = 735


def levels(stream_key, extent, pieces, low, high):
    gain = 1.0
    for dim, parts in pieces:
        heights = jax.random.uniform(jax.random.fold_in(jax.random.fold_in(stream_key, 6), dim), (parts,), jnp.float32, low / len(pieces), high / len(pieces))
        gain = gain * jnp.repeat(jnp.exp(heights), extent[dim] // parts).reshape((-1,) + (1,) * (len(extent) - 1 - dim))
    return gain


def assign_block(rng, own, number, rows, number_of, top, most, skew):
    sequence = jax.random.permutation(rng, number_of)
    packed, ordinary = shares(number_of, rows * top, most, skew, True), shares(number_of, rows * top, most, skew, False)
    places = jnp.arange(number_of)

    def named(lengths, offset_by):
        used = int((lengths > 0).sum())
        fixed = max(1, used // 4)
        shifted = fixed + (places - fixed + offset_by * (used - fixed)) % max(1, number_of - fixed)
        return jnp.zeros((number_of,), jnp.int32).at[sequence[jnp.where(places < fixed, places, shifted)]].set(jnp.asarray(lengths, jnp.int32))

    lengths = jnp.where(number % 4 == 0, named(packed, number // 4), named(ordinary, number - number // 4 - 1))
    mixed = jax.random.permutation(jax.random.fold_in(own, 3), number_of)
    giver, receiver = mixed[0:number_of // 2 * 2:2], mixed[1:number_of // 2 * 2:2]
    slack = jnp.minimum(lengths[giver] - 1, most - lengths[receiver]) // 2
    slack = jnp.where((giver == sequence[0]) | (receiver == sequence[0]) | (lengths[receiver] == 0), 0, jnp.maximum(slack, 0))
    shifted = jax.random.randint(jax.random.fold_in(own, 4), (number_of // 2,), 0, 1 << 20) % (slack + 1)
    lengths = lengths.at[giver].add(-shifted).at[receiver].add(shifted)
    items = jnp.searchsorted(jnp.cumsum(lengths), jnp.arange(rows * top), side="right").astype(jnp.int32)
    table = items.reshape(top, rows).T
    table = table[jax.random.permutation(jax.random.fold_in(own, 1), rows)]
    offset_by = jax.random.randint(jax.random.fold_in(own, 2), (rows, 1), 0, top)
    return jnp.take_along_axis(table, (jnp.arange(top)[None, :] + offset_by) % top, axis=1)


def shares(amount, total, limit, slope, full):
    loads = [(1 << 20) // math.isqrt(standing ** slope) + 1 for standing in range(1, amount + 1)]
    largest = limit if full else min(limit, max(-(-total // amount), total * loads[0] // sum(loads)))
    least = 1 if total - largest >= amount - 1 else 0
    given, spare = [largest] + [least] * (amount - 1), total - largest - least * (amount - 1)
    while spare > 0:
        movable = [i for i in range(1, amount) if given[i] < largest] or [i for i in range(1, amount) if given[i] < limit]
        whole, remaining = sum([loads[i] for i in movable]), spare
        for i in movable:
            more = min(limit - given[i], max(1, remaining * loads[i] // whole), spare)
            given[i] = given[i] + more
            spare = spare - more
    return np.array(given)


def noise(stream_key, shape, scale, reach, cuts=(), kind=jnp.bfloat16):
    values = jax.random.normal(stream_key, shape, jnp.float32) * scale
    if len(cuts) > 0:
        values = levels(stream_key, shape, cuts, -0.22, 0.18) * values
    return jnp.clip(values, min=-reach, max=reach).astype(kind)


def setup_inputs(seed: int = 0) -> dict:
    keys = jax.random.split(jax.random.key(seed), 18)
    tokens_in = noise(keys[0], (TOKENS, D), 1.0, 6.0, ((0, 32),))
    attn_gain = jnp.clip(1.0 + 0.1 * jax.random.normal(keys[1], (D,), jnp.float32), 0.5, 1.5).astype(jnp.bfloat16)
    attn_shift = noise(keys[2], (D,), 0.2, 1.25)
    qkv_weight = noise(keys[3], (3, D, D), D ** -0.5, 0.3125, ((2, 4),))
    qv_bias = noise(keys[4], (2, D), 0.2, 1.25, ((1, 4),))
    rel_table = noise(keys[5], (TABLE, HEADS), 1.0, 6.0, ((1, 4),))
    proj_weight = noise(keys[6], (D, D), (D // 8) ** -0.5, 0.875, ((0, 4),))
    proj_bias = noise(keys[7], (D,), 0.2, 1.25)
    moe_gain = jnp.clip(1.0 + 0.1 * jax.random.normal(keys[8], (D,), jnp.float32), 0.5, 1.5).astype(jnp.bfloat16)
    moe_shift = noise(keys[9], (D,), 0.2, 1.25)
    router_weight = noise(keys[10], (D, EXPERTS), (2 * D) ** -0.5, 0.21875)
    expert_in = noise(keys[11], (EXPERTS, D, FF), D ** -0.5, 0.3125, ((2, 4),))
    expert_in_bias = noise(keys[12], (EXPERTS, FF), 0.1, 0.625, ((1, 4),))
    expert_out = noise(keys[13], (EXPERTS, FF, D), (FF // 64) ** -0.5, 1.25, ((1, 4),))
    expert_out_bias = noise(keys[14], (EXPERTS, D), 0.5, 3.0)
    expert_ids_keys = jax.random.split(jax.random.fold_in(keys[15], 1), TOKENS // TOKG)
    expert_ids_turns = jax.random.permutation(jax.random.fold_in(keys[15], 3), TOKENS // TOKG)
    expert_ids = jax.vmap(lambda own, number: assign_block(jax.random.fold_in(keys[15], 2), own, number, TOKG, EXPERTS, 1, CAP, 1))(expert_ids_keys, expert_ids_turns).reshape((TOKENS, 1))
    cotangent = noise(keys[16], (TOKENS, D), 1.0, 6.0, ((0, 32),))
    return dict(tokens_in=tokens_in, attn_gain=attn_gain, attn_shift=attn_shift, qkv_weight=qkv_weight, qv_bias=qv_bias, rel_table=rel_table, proj_weight=proj_weight, proj_bias=proj_bias, moe_gain=moe_gain, moe_shift=moe_shift, router_weight=router_weight, expert_in=expert_in, expert_in_bias=expert_in_bias, expert_out=expert_out, expert_out_bias=expert_out_bias, expert_ids=expert_ids, cotangent=cotangent)


@jax.custom_vjp
def low(v):
    return lax.optimization_barrier(v.astype(jnp.bfloat16)).astype(jnp.float32)

@jax.custom_vjp
def low_back(v):
    return v

def low_keep(v):
    return (low(v), None)

def low_pass(kept, grad):
    return (grad,)

def back_keep(v):
    return (v, None)

def back_low(kept, grad):
    return (low(grad),)
low.defvjp(low_keep, low_pass)
low_back.defvjp(back_keep, back_low)
HIGHEST_MODE = lax.Precision.HIGHEST
MASK_FILL = -1e+30

def region(coordinate):
    return (coordinate >= SIDE - WINDOW).astype(jnp.int32) + (coordinate >= SIDE - WINDOW // 2).astype(jnp.int32)

def window_layout():
    cell_ids = jnp.arange(SIDE * SIDE, dtype=jnp.int32)
    offset = WINDOW // 2
    row_pos = (cell_ids // SIDE - offset) % SIDE
    col_pos = (cell_ids % SIDE - offset) % SIDE
    labels = (row_pos // WINDOW * SIDE + col_pos // WINDOW) * 9 + region(row_pos) * 3 + region(col_pos)
    allowed = labels[:, None] == labels[None, :]
    return (allowed, row_pos % WINDOW, col_pos % WINDOW)

def layer_norm(values, gain_vec, shift_vec):
    centre = values - lax.optimization_barrier(jnp.mean(values, axis=-1, keepdims=True))
    spread = lax.optimization_barrier(jnp.mean(centre * centre, axis=-1, keepdims=True))
    return centre * lax.rsqrt(spread + 1e-05) * gain_vec + shift_vec

def softmax_last(scores):
    row_max = lax.optimization_barrier(jnp.max(scores, axis=-1, keepdims=True))
    powers = jnp.exp(scores - row_max)
    return powers / lax.optimization_barrier(jnp.sum(powers, axis=-1, keepdims=True))

def gelu_exact(values):
    return 0.5 * values * (1.0 + jax.scipy.special.erf(values * (1.0 / math.sqrt(2.0))))

def forward(tokens_in, attn_gain, attn_shift, qkv_weight, qv_bias, rel_table, proj_weight, proj_bias, moe_gain, moe_shift, router_weight, expert_in, expert_in_bias, expert_out, expert_out_bias, expert_ids):
    images = tokens_in.shape[0] // IMAGE
    normed = low(layer_norm(tokens_in, attn_gain, attn_shift))
    queries = low(low_back(jnp.dot(normed, qkv_weight[0], precision=HIGHEST_MODE) + qv_bias[0]))
    keys_all = low(low_back(jnp.dot(normed, qkv_weight[1], precision=HIGHEST_MODE)))
    values_all = low(low_back(jnp.dot(normed, qkv_weight[2], precision=HIGHEST_MODE) + qv_bias[1]))
    head_shape = (images, IMAGE, HEADS, HEAD_DIM)
    allowed, inner_row, inner_col = window_layout()
    rel_index = (inner_row[:, None] - inner_row[None, :] + WINDOW - 1) * (2 * WINDOW - 1) + inner_col[:, None] - inner_col[None, :] + WINDOW - 1
    position_bias = jnp.transpose(rel_table[rel_index], (2, 0, 1))
    products = low_back(jnp.einsum('bihd,bjhd->bhij', queries.reshape(head_shape), keys_all.reshape(head_shape), precision=HIGHEST_MODE))
    scores = jnp.where(allowed, products * HEAD_DIM ** (-0.5) + position_bias, MASK_FILL)
    attention = low(softmax_last(scores))
    mixed_heads = jnp.einsum('bhij,bjhd->bihd', attention, values_all.reshape(head_shape), precision=HIGHEST_MODE).reshape(tokens_in.shape)
    mixed_heads = low(low_back(mixed_heads))
    hidden_one = tokens_in + low_back(jnp.dot(mixed_heads, proj_weight, precision=HIGHEST_MODE) + proj_bias)
    second = low(layer_norm(hidden_one, moe_gain, moe_shift))
    router_probs = softmax_last(jnp.dot(second, router_weight, precision=HIGHEST_MODE))
    chosen = expert_ids == jnp.arange(EXPERTS, dtype=jnp.int32)[None, :]
    gate_value = lax.optimization_barrier(jnp.sum(jnp.where(chosen, router_probs, 0.0), axis=-1, keepdims=True))
    rank_run = jnp.cumsum(chosen.astype(jnp.int32), axis=0, dtype=jnp.int32) - 1
    slot_ids = lax.optimization_barrier(jnp.sum(jnp.where(chosen, rank_run, 0), axis=-1, dtype=jnp.int32))
    position = (expert_ids[:, 0] * CAP + slot_ids).astype(jnp.int32)
    buffer = jnp.zeros((EXPERTS * CAP, second.shape[1]), second.dtype).at[position].set(second).reshape(EXPERTS, CAP, second.shape[1])
    preact = low_back(jnp.einsum('ecd,edf->ecf', buffer, expert_in, precision=HIGHEST_MODE) + expert_in_bias[:, None, :])
    activated = low(gelu_exact(preact))
    expert_res = jnp.einsum('ecf,efd->ecd', activated, expert_out, precision=HIGHEST_MODE) + expert_out_bias[:, None, :]
    per_token = low_back(expert_res.reshape(EXPERTS * CAP, second.shape[1])[position])
    return hidden_one + gate_value * per_token

def reference(tokens_in, attn_gain, attn_shift, qkv_weight, qv_bias, rel_table, proj_weight, proj_bias, moe_gain, moe_shift, router_weight, expert_in, expert_in_bias, expert_out, expert_out_bias, expert_ids, cotangent):
    params = tuple((member.astype(jnp.float32) for member in (attn_gain, attn_shift, qkv_weight, qv_bias, rel_table, proj_weight, proj_bias, moe_gain, moe_shift, router_weight, expert_in, expert_in_bias, expert_out, expert_out_bias)))
    groups = tokens_in.shape[0] // TOKG
    features = tokens_in.shape[1]
    inputs = (tokens_in.astype(jnp.float32).reshape(groups, TOKG, features), expert_ids.reshape(groups, TOKG, 1), cotangent.astype(jnp.float32).reshape(groups, TOKG, features))

    def group_step(totals, group_data):
        group_tokens, group_ids, group_cot = group_data

        def apply_block(tokens_group, *weights):
            return forward(tokens_group, *weights, group_ids)
        result, pullback = jax.vjp(apply_block, group_tokens, *params)
        gradients = pullback(group_cot)
        totals = tuple((running + addend for running, addend in zip(totals, gradients[1:])))
        return (totals, (result.astype(jnp.bfloat16), gradients[0]))
    totals, (results, input_grads) = lax.scan(group_step, tuple((jnp.zeros_like(member) for member in params)), inputs)
    return (results.reshape(tokens_in.shape), input_grads.reshape(tokens_in.shape), totals[0], totals[1], totals[2], totals[3], totals[4], totals[5], totals[6], totals[7], totals[8], totals[9], totals[10], totals[11], totals[12], totals[13])
```

```python
import functools
import math

import jax
import jax.numpy as jnp
import numpy as np
from jax import lax
from jax.experimental import pallas as pl
from jax.experimental.pallas import tpu as pltpu
from jax.sharding import PartitionSpec as P

F32 = jnp.float32
LOW = jnp.bfloat16
D = 384
HEADS = 12
EXPERTS = 8
SIDE = 14
WINDOW = 7
IMAGE = 196
HALF = 2352
BLOCK = 784
BLOCKS = 3
PADDED = 256
SLICE = 208
TILE = 168
TILES = 28
HALF_TILES = 14
GROUPS = 28
SORTED = 224
SLOTS = 960
CHUNK = 240
STORE = EXPERTS * SLOTS + 8
MASK_FILL = -1e30
SCALE = 32 ** (-0.5)
VMEM = 60 * 1024 * 1024


def layout_consts():
    cell = np.arange(IMAGE)
    row = (cell // SIDE - WINDOW // 2) % SIDE
    col = (cell % SIDE - WINDOW // 2) % SIDE
    slot = (row // WINDOW * 2 + col // WINDOW) * 64 + row % WINDOW * WINDOW + col % WINDOW
    place = np.zeros((4, PADDED, SLICE), np.float32)
    for k in range(4):
        place[k, slot, 4 * k + cell] = 1.0
    part = lambda v: (v >= SIDE - WINDOW) * 1 + (v >= SIDE - WINDOW // 2) * 1
    label = np.full((PADDED,), -1)
    label[slot] = part(row) * 3 + part(col)
    label = label.reshape(4, 64)
    real = np.arange(64) < WINDOW * WINDOW
    meet = (label[:, :, None] == label[:, None, :]) | ~real[None, :, None]
    fill = np.where(meet & real[None, None, :], 0.0, MASK_FILL).astype(np.float32)
    fill = np.tile(fill, (1, 1, 4))
    spot = np.arange(49)
    entry = (spot[:, None] // 7 - spot[None, :] // 7 + 6) * 13 + spot[:, None] % 7 - spot[None, :] % 7 + 6
    lookup = np.zeros((64, 64, 169), np.float32)
    lookup[spot[:, None], spot[None, :], entry] = 1.0
    heads = (np.arange(256)[:, None] // 64 == np.arange(128)[None, :] // 32).astype(np.float32)
    segment = (np.arange(256)[:, None] // 64 == np.arange(256)[None, :] // 64).astype(np.float32)
    return place, fill, lookup.reshape(4096, 169), heads, segment


def nn(a, b):
    return lax.dot_general(a, b, (((1,), (0,)), ((), ())), preferred_element_type=F32)


def nt(a, b):
    return lax.dot_general(a, b, (((1,), (1,)), ((), ())), preferred_element_type=F32)


def tn(a, b):
    return lax.dot_general(a, b, (((0,), (0,)), ((), ())), preferred_element_type=F32)


def norm_parts(values):
    centre = values - jnp.mean(values, axis=-1, keepdims=True)
    inverse = lax.rsqrt(jnp.mean(centre * centre, axis=-1, keepdims=True) + 1e-5)
    return centre * inverse, inverse


def norm_back(upstream, unit, inverse, gain):
    scaled = upstream * gain
    return inverse * (
        scaled
        - jnp.mean(scaled, axis=-1, keepdims=True)
        - unit * jnp.mean(scaled * unit, axis=-1, keepdims=True)
    )


def column_sum(values):
    return jnp.sum(values, axis=0, keepdims=True)


def router_softmax(second, router):
    logits = nn(second, router)
    lane = lax.broadcasted_iota(jnp.int32, logits.shape, 1)
    logits = jnp.where(lane < EXPERTS, logits, MASK_FILL)
    power = jnp.exp(logits - jnp.max(logits, axis=-1, keepdims=True))
    return power / jnp.sum(power, axis=-1, keepdims=True), lane


def expand(part, heads):
    return jnp.concatenate([part] * 4, axis=0) * heads


def attention_kernel(
    core, x_ref, ids_ref, attn_gain, attn_shift, wqkv_wide, bqkv, bias, place, place_t, heads, segment,
    wproj_wide, bproj, moe_gain, moe_shift, router, out_bias,
    hidden_ref, base_ref, second_ref, gate_ref, mixed_ref, qkv_ref, prob_ref,
    low_scr, raster_scr, wqkv, wproj,
):
    @pl.when(pl.program_id(0) == 0)
    def _():
        wqkv[...] = wqkv_wide[...].T.astype(LOW)
        wproj[...] = wproj_wide[...].astype(LOW)

    x = x_ref[...].astype(F32)
    unit, _ = norm_parts(x)
    low_scr[...] = (unit * attn_gain[...] + attn_shift[...]).astype(LOW)
    raster_scr[...] = jnp.zeros_like(raster_scr)
    lane = lax.broadcasted_iota(jnp.int32, (64, 128), 1)
    left = lane < 64

    def image(k, carry):
        start = pl.multiple_of(k * 192, 64)
        rows = nn(place[k], low_scr[pl.ds(start, SLICE), :]).astype(LOW)
        qkv = (nn(rows, wqkv[...]) + bqkv[...]).astype(LOW)
        qkv_ref[pl.ds(pl.multiple_of(k * PADDED, PADDED), PADDED), :] = qkv
        outs = []
        for w in range(4):
            row = slice(w * 64, w * 64 + 64)
            parts = []
            for g in range(3):
                q = qkv[row, g * 128 : g * 128 + 128]
                kx = expand(qkv[row, D + g * 128 : D + g * 128 + 128], heads[...])
                vx = expand(qkv[row, 2 * D + g * 128 : 2 * D + g * 128 + 128], heads[...])
                scores = nt(q, kx) * SCALE + bias[w * 3 + g]
                power = []
                for c in range(2):
                    piece = scores[:, c * 128 : c * 128 + 128]
                    first = jnp.max(jnp.where(left, piece, 2 * MASK_FILL), axis=-1, keepdims=True)
                    other = jnp.max(jnp.where(left, 2 * MASK_FILL, piece), axis=-1, keepdims=True)
                    power.append(jnp.exp(piece - jnp.where(left, first, other)))
                power = jnp.concatenate(power, axis=1)
                total = nn(power.astype(LOW), segment[...])
                prob = (power / total).astype(LOW)
                spot = pl.multiple_of(((k * 4 + w) * 3 + g) * 64, 64)
                prob_ref[pl.ds(spot, 64), :] = prob
                parts.append(nn(prob, vx).astype(LOW))
            outs.append(jnp.concatenate(parts, axis=1))
        mixed = jnp.concatenate(outs, axis=0)
        raster_scr[pl.ds(start, SLICE), :] += nn(place_t[k], mixed)
        return carry

    lax.fori_loop(0, 4, image, 0)
    mixed = raster_scr[...].astype(LOW)
    mixed_ref[...] = mixed
    hidden = x + (nn(mixed, wproj[...]) + bproj[...])
    hidden_ref[...] = hidden
    unit, _ = norm_parts(hidden)
    second = (unit * moe_gain[...] + moe_shift[...]).astype(LOW)
    second_ref[...] = second.astype(F32)
    probs, lanes = router_softmax(second, router[...])
    chosen = lanes == ids_ref[...]
    gate = jnp.sum(jnp.where(chosen, probs, 0.0), axis=-1, keepdims=True)
    gate_ref[...] = gate
    base_ref[...] = hidden + gate * nn(chosen.astype(F32).astype(LOW), out_bias[...])


def whole(shape):
    return pl.BlockSpec(shape, lambda *_: (0,) * len(shape))


def attention_forward(core, x, ids, consts, weights, bias):
    place, place_t, heads, segment = consts
    at_block = lambda width: pl.BlockSpec((BLOCK, width), lambda i, s: (s[0] * BLOCKS + i, 0))
    rows = lambda height, width: pl.BlockSpec((height, width), lambda i, s: (i, 0))
    fixed = [weights[n] for n in ("attn_gain", "attn_shift", "wqkv", "bqkv")]
    tail = [weights[n] for n in ("wproj", "bproj", "moe_gain", "moe_shift", "router", "out_bias_pad")]
    operands = fixed + [bias, place, place_t, heads, segment] + tail
    return pl.pallas_call(
        attention_kernel,
        grid_spec=pltpu.PrefetchScalarGridSpec(
            num_scalar_prefetch=1,
            grid=(BLOCKS,),
            in_specs=[at_block(D), at_block(1)] + [whole(v.shape) for v in operands],
            out_specs=[
                rows(BLOCK, D),
                rows(BLOCK, D),
                rows(BLOCK, D),
                rows(BLOCK, 1),
                rows(BLOCK, D),
                rows(4 * PADDED, 3 * D),
                rows(48 * 64, 256),
            ],
            scratch_shapes=[
                pltpu.VMEM((BLOCK, D), LOW),
                pltpu.VMEM((BLOCK, D), F32),
                pltpu.VMEM((D, 3 * D), LOW),
                pltpu.VMEM((D, D), LOW),
            ],
        ),
        out_shape=[
            jax.ShapeDtypeStruct((HALF, D), F32),
            jax.ShapeDtypeStruct((HALF, D), F32),
            jax.ShapeDtypeStruct((HALF, D), F32),
            jax.ShapeDtypeStruct((HALF, 1), F32),
            jax.ShapeDtypeStruct((HALF, D), LOW),
            jax.ShapeDtypeStruct((BLOCKS * 4 * PADDED, 3 * D), LOW),
            jax.ShapeDtypeStruct((BLOCKS * 48 * 64, 256), LOW),
        ],
        compiler_params=pltpu.CompilerParams(vmem_limit_bytes=VMEM),
        cost_estimate=pl.CostEstimate(flops=8_000_000_000, bytes_accessed=40_000_000, transcendentals=4_000_000),
        name="attention_forward",
    )(core, x, ids, *operands)


def gelu_parts(values):
    size = jnp.abs(values)
    decay = jnp.exp(-0.5 * values * values)
    t = 1.0 / (1.0 + (0.3275911 / math.sqrt(2.0)) * size)
    poly = t * (0.254829592 + t * (-0.284496736 + t * (1.421413741 + t * (-1.453152027 + t * 1.061405429))))
    half = 0.5 * poly * decay
    cdf = jnp.where(values >= 0.0, 1.0 - half, half)
    return values * cdf, cdf + values * decay * (1.0 / math.sqrt(2.0 * math.pi))


def experts_kernel(
    core, dest, chunks,
    own_ref, other_ref, g_ref, ids_ref, pos_row, pos_col, router, w_in, b_in, w_out,
    grad_in, grad_out, in_bias, out_bias, gs_theirs, ep_theirs, gg_theirs, gs_mine, ep_mine, gg_mine,
    store,
):
    step = pl.program_id(0)

    @pl.when(step == 0)
    def _():
        def clear(j, carry):
            store[pl.ds(pl.multiple_of(j * 248, 8), 248), :] = jnp.zeros((248, 2 * D), F32)
            return carry

        lax.fori_loop(0, STORE // 248, clear, 0)

    def tile_of():
        undo = step >= TILES + EXPERTS
        j = jnp.where(undo, step - TILES - EXPERTS, step)
        flip = jnp.where(undo, 1 - core[0], core[0])
        half = jnp.where(j < HALF_TILES, flip, 1 - flip)
        return half * HALF_TILES + j % HALF_TILES

    @pl.when(step < TILES)
    def _():
        tile = tile_of()
        second = jnp.where(step < HALF_TILES, own_ref[...], other_ref[...]).astype(LOW)
        probs, lanes = router_softmax(second, router[...])
        gate = jnp.sum(jnp.where(lanes == ids_ref[...], probs, 0.0), axis=-1, keepdims=True)
        grad = (gate * g_ref[...].astype(F32)).astype(LOW)
        spot = lax.broadcasted_iota(jnp.int32, (SORTED, TILE), 0)
        pick = (spot == pos_row[0]).astype(F32).astype(LOW)
        moved = nn(pick, jnp.concatenate([second, grad], axis=1))
        for j in range(GROUPS):
            at = pl.multiple_of(dest[tile * GROUPS + j] * 8, 8)
            store[pl.ds(at, 8), :] = moved[j * 8 : j * 8 + 8, :]

    @pl.when((step >= TILES) & (step < TILES + EXPERTS))
    def _():
        e = step - TILES
        grad_in[...] = jnp.zeros_like(grad_in)
        grad_out[...] = jnp.zeros_like(grad_out)

        def chunk(c, sums):
            at = pl.ds(pl.multiple_of(e * SLOTS + c * CHUNK, 16), CHUNK)
            buffer = store[at, :D].astype(LOW)
            grad = store[at, D:].astype(LOW)
            act, slope = gelu_parts(nn(buffer, w_in[0]) + b_in[pl.ds(e, 1), :].astype(F32))
            act = act.astype(LOW)
            grad_pre = (nt(grad, w_out[0]) * slope).astype(LOW)
            store[at, :D] = nt(grad_pre, w_in[0])
            store[at, D:] = nn(act, w_out[0])
            grad_in[...] += tn(buffer, grad_pre)
            grad_out[...] += tn(act, grad)
            return sums[0] + column_sum(grad_pre.astype(F32)), sums[1] + column_sum(grad.astype(F32))

        zero = jnp.zeros((1, D), F32)
        sums = lax.fori_loop(0, chunks[e], chunk, (zero, zero))
        in_bias[pl.ds(e, 1), :] = sums[0]
        out_bias[pl.ds(e, 1), :] = sums[1]

    def collect():
        tile = tile_of()
        rows = [store[pl.ds(pl.multiple_of(dest[tile * GROUPS + j] * 8, 8), 8), :] for j in range(GROUPS)]
        rows = jnp.concatenate(rows, axis=0).astype(LOW)
        spot = lax.broadcasted_iota(jnp.int32, (TILE, SORTED), 1)
        pick = (spot == pos_col[...]).astype(F32).astype(LOW)
        back = nn(pick, rows)
        gate_grad = jnp.sum(g_ref[...].astype(F32) * back[:, D:], axis=-1, keepdims=True)
        return back[:, :D], back[:, D:], gate_grad

    @pl.when((step >= TILES + EXPERTS) & (step < TILES + EXPERTS + HALF_TILES))
    def _():
        gs_theirs[...], ep_theirs[...], gg_theirs[...] = collect()

    @pl.when(step >= TILES + EXPERTS + HALF_TILES)
    def _():
        gs_mine[...], ep_mine[...], gg_mine[...] = collect()


def experts(core, dest, chunks, own, other, g, ids, pos_row, pos_col, router, w_in, b_in, w_out):
    steps = TILES + EXPERTS + TILES
    last = HALF_TILES - 1

    def tile(i, c, *_):
        undo = i >= TILES + EXPERTS
        j = jnp.where(undo, i - TILES - EXPERTS, jnp.minimum(i, TILES - 1))
        flip = jnp.where(undo, 1 - c[0], c[0])
        half = jnp.where(j < HALF_TILES, flip, 1 - flip)
        return half * HALF_TILES + j % HALF_TILES

    def run(begin):
        return lambda i, *_: (jnp.clip(i - begin, 0, last), 0)

    expert = lambda i, *_: (jnp.clip(i - TILES, 0, EXPERTS - 1), 0, 0)
    flat = lambda i, *_: (jnp.clip(i - TILES, 0, EXPERTS - 1), 0)
    by_tile = lambda width: pl.BlockSpec((TILE, width), lambda i, *s: (tile(i, *s), 0))
    undo = TILES + EXPERTS
    half = lambda width: jax.ShapeDtypeStruct((HALF, width), F32)
    out_half = lambda begin: [pl.BlockSpec((TILE, w), run(begin)) for w in (D, D, 1)]
    return pl.pallas_call(
        experts_kernel,
        grid_spec=pltpu.PrefetchScalarGridSpec(
            num_scalar_prefetch=3,
            grid=(steps,),
            in_specs=[
                pl.BlockSpec((TILE, D), run(0)),
                pl.BlockSpec((TILE, D), run(HALF_TILES)),
                by_tile(D),
                by_tile(1),
                pl.BlockSpec((1, 1, TILE), lambda i, *s: (tile(i, *s), 0, 0)),
                by_tile(1),
                whole((D, 128)),
                pl.BlockSpec((1, D, D), expert),
                whole((EXPERTS, D)),
                pl.BlockSpec((1, D, D), expert),
            ],
            out_specs=[
                pl.BlockSpec((D, D), flat),
                pl.BlockSpec((D, D), flat),
                whole((EXPERTS, D)),
                whole((EXPERTS, D)),
            ]
            + out_half(undo)
            + out_half(undo + HALF_TILES),
            scratch_shapes=[pltpu.VMEM((STORE, 2 * D), F32)],
        ),
        out_shape=[
            jax.ShapeDtypeStruct((EXPERTS * D, D), F32),
            jax.ShapeDtypeStruct((EXPERTS * D, D), F32),
            jax.ShapeDtypeStruct((EXPERTS, D), F32),
            jax.ShapeDtypeStruct((EXPERTS, D), F32),
        ]
        + [half(D), half(D), half(1)] * 2,
        compiler_params=pltpu.CompilerParams(vmem_limit_bytes=VMEM),
        cost_estimate=pl.CostEstimate(flops=25_000_000_000, bytes_accessed=60_000_000, transcendentals=6_000_000),
        name="experts",
    )(core, dest, chunks, own, other, g, ids, pos_row, pos_col, router, w_in, b_in, w_out)


def sort_plan(ids):
    named = ids.reshape(TILES, TILE)
    kinds = jnp.arange(EXPERTS, dtype=jnp.int32)
    chosen = (named[:, :, None] == kinds).astype(F32)
    before = jnp.asarray(np.tril(np.ones((TILE, TILE), np.float32), -1))
    rank = jnp.einsum("ij,tje->tie", before, chosen)
    count = jnp.sum(chosen, axis=1).astype(jnp.int32)
    groups = (count + 7) // 8
    ahead = jnp.asarray(np.tril(np.ones((EXPERTS, EXPERTS), np.int32), -1))
    first = jnp.sum(groups[:, None, :] * ahead[None], axis=-1)
    spot = jnp.sum(chosen * (rank + 8.0 * first[:, None, :].astype(F32)), axis=-1).astype(jnp.int32)
    earlier = jnp.asarray(np.tril(np.ones((TILES, TILES), np.int32), -1))
    offset = jnp.sum(earlier[:, :, None] * groups[None], axis=1)
    j = jnp.arange(GROUPS, dtype=jnp.int32)[None, :, None]
    inside = (j >= first[:, None, :]) & (j < (first + groups)[:, None, :])
    target = kinds * (SLOTS // 8) + offset[:, None, :] + j - first[:, None, :]
    dest = jnp.sum(jnp.where(inside, target, 0), axis=-1)
    dest = jnp.where(jnp.any(inside, axis=-1), dest, EXPERTS * SLOTS // 8).astype(jnp.int32)
    used = jnp.sum(groups, axis=0) * 8
    chunks = (used + CHUNK - 1) // CHUNK
    return spot, dest.reshape(-1), chunks.astype(jnp.int32)


def backward_kernel(
    first, core, gs_a, gs_b, gg_ref, hidden_ref, g_ref, x_ref, ids_ref, mixed_ref, qkv_ref, prob_ref,
    attn_gain, attn_shift, wqkv, place, place_t, heads, segment, wproj, moe_gain, moe_shift, router, out_bias_t,
    *refs,
):
    if first:
        input_grad, grad_wqkv, grad_wproj, small, table, raster_scr, mixed_scr = refs
        grad_wqkv[...] = jnp.zeros_like(grad_wqkv)
        grad_wproj[...] = jnp.zeros_like(grad_wproj)
        small[...] = jnp.zeros_like(small)
        table[...] = jnp.zeros_like(table)
    else:
        before, (input_grad, grad_wqkv, grad_wproj, small, table, raster_scr, mixed_scr) = refs[:4], refs[4:]
        for was, now in zip(before, (grad_wqkv, grad_wproj, small, table)):
            now[...] = was[...]

    g_low = g_ref[...]
    g = g_low.astype(F32)
    unit, inverse = norm_parts(hidden_ref[...])
    second = (unit * moe_gain[...] + moe_shift[...]).astype(LOW)
    probs, lanes = router_softmax(second, router[...])
    chosen = lanes == ids_ref[...]
    gate = jnp.sum(jnp.where(chosen, probs, 0.0), axis=-1, keepdims=True)
    with_bias = jnp.sum(jnp.where(chosen, nn(g_low, out_bias_t[...]), 0.0), axis=-1, keepdims=True)
    grad_gate = gg_ref[...] + with_bias
    grad_logit = grad_gate * gate * (chosen.astype(F32) - probs)
    logit_high = grad_logit.astype(LOW)
    logit_rest = (grad_logit - logit_high.astype(F32)).astype(LOW)
    grad_router = tn(logit_high, second) + tn(logit_rest, second)
    grad_second = gs_a[...] + gs_b[...] + nt(logit_high, router[...]) + nt(logit_rest, router[...])
    small[3:4, :] += column_sum(grad_second * unit)
    small[4:5, :] += column_sum(grad_second)
    small[8:16, :] += grad_router[:EXPERTS, :]
    grad_hidden = g + norm_back(grad_second, unit, inverse, moe_gain[...])
    grad_low = grad_hidden.astype(LOW)
    small[2:3, :] += column_sum(grad_low.astype(F32))
    grad_wproj[...] += tn(mixed_ref[...], grad_low)
    mixed_scr[...] = nt(grad_low, wproj[...].astype(LOW)).astype(LOW)
    raster_scr[...] = jnp.zeros_like(raster_scr)

    def image(k, carry):
        start = pl.multiple_of(k * 192, 64)
        grad_mixed = nn(place[k], mixed_scr[pl.ds(start, SLICE), :]).astype(LOW)
        outs = []
        for w in range(4):
            row = slice(w * 64, w * 64 + 64)
            at = pl.ds(pl.multiple_of(k * PADDED + w * 64, 64), 64)
            parts = [[], [], []]
            for c in range(3):
                q = qkv_ref[at, c * 128 : c * 128 + 128]
                kx = expand(qkv_ref[at, D + c * 128 : D + c * 128 + 128], heads[...])
                vx = expand(qkv_ref[at, 2 * D + c * 128 : 2 * D + c * 128 + 128], heads[...])
                prob_low = prob_ref[pl.ds(pl.multiple_of(((k * 4 + w) * 3 + c) * 64, 64), 64), :]
                prob = prob_low.astype(F32)
                upstream = grad_mixed[row, c * 128 : c * 128 + 128]
                grad_prob = nt(upstream, vx)
                weighted = nn((prob * grad_prob).astype(LOW), segment[...])
                grad_score = prob * (grad_prob - weighted)
                table[c * 64 : c * 64 + 64, :] += grad_score
                low = (grad_score * SCALE).astype(LOW)
                parts[0].append(nn(low, kx).astype(LOW))
                for slot, left, right in ((1, low, q), (2, prob_low, upstream)):
                    full = tn(left, right)
                    kept = [full[h * 64 : h * 64 + 64] * heads[h * 64 : h * 64 + 64, :].astype(F32) for h in range(4)]
                    parts[slot].append((kept[0] + kept[1] + kept[2] + kept[3]).astype(LOW))
            outs.append(jnp.concatenate(parts[0] + parts[1] + parts[2], axis=1))
        grads = jnp.concatenate(outs, axis=0)
        raster_scr[pl.ds(start, SLICE), :] += nn(place_t[k], grads)
        return carry

    lax.fori_loop(0, 4, image, 0)
    unit, inverse = norm_parts(x_ref[...].astype(F32))
    attn_low = (unit * attn_gain[...] + attn_shift[...]).astype(LOW)
    raster = raster_scr[...]
    small[5:6, :] += column_sum(raster[:, :D])
    small[6:7, :] += column_sum(raster[:, 2 * D :])
    grads = raster.astype(LOW)
    grad_wqkv[...] += tn(grads, attn_low)
    grad_in = nn(grads, wqkv[...].astype(LOW))
    small[0:1, :] += column_sum(grad_in * unit)
    small[1:2, :] += column_sum(grad_in)
    input_grad[...] = grad_hidden + norm_back(grad_in, unit, inverse, attn_gain[...])


def attention_backward(block, core, gs_a, gs_b, gg, hidden, g, x, ids, mixed, qkv, prob, consts, weights, sums):
    place, place_t, heads, segment = consts
    at_block = lambda width: pl.BlockSpec((BLOCK, width), lambda i, s: (s[0] * BLOCKS + block, 0))
    rows = lambda height, width: pl.BlockSpec((height, width), lambda i, s: (block, 0))
    fixed = [weights[n] for n in ("attn_gain", "attn_shift", "wqkv")] + [place, place_t, heads, segment]
    fixed = fixed + [weights[n] for n in ("wproj", "moe_gain", "moe_shift", "router", "out_bias_t")]
    totals = [(3 * D, D), (D, D), (16, D), (192, 256)]
    before = [] if sums is None else list(sums)
    return pl.pallas_call(
        functools.partial(backward_kernel, sums is None),
        grid_spec=pltpu.PrefetchScalarGridSpec(
            num_scalar_prefetch=1,
            grid=(1,),
            in_specs=[
                whole((BLOCK, D)),
                whole((BLOCK, D)),
                rows(BLOCK, 1),
                rows(BLOCK, D),
                at_block(D),
                at_block(D),
                at_block(1),
                rows(BLOCK, D),
                rows(4 * PADDED, 3 * D),
                rows(48 * 64, 256),
            ]
            + [whole(v.shape) for v in fixed + before],
            out_specs=[whole((BLOCK, D))] + [whole(v) for v in totals],
            scratch_shapes=[pltpu.VMEM((BLOCK, 3 * D), F32), pltpu.VMEM((BLOCK, D), LOW)],
        ),
        out_shape=[jax.ShapeDtypeStruct(v, F32) for v in [(BLOCK, D)] + totals],
        compiler_params=pltpu.CompilerParams(vmem_limit_bytes=VMEM),
        cost_estimate=pl.CostEstimate(flops=20_000_000_000, bytes_accessed=50_000_000, transcendentals=100_000),
        name="attention_backward",
    )(core, gs_a, gs_b, gg, hidden, g, x, ids, mixed, qkv, prob, *fixed, *before)


def position_bias(table, fill, lookup):
    rows = jnp.dot(lookup, table, precision=lax.Precision.HIGHEST)
    rows = rows.T.reshape(3, 4, 64, 64).transpose(0, 2, 1, 3).reshape(1, 3, 64, 256)
    return (rows + fill[:, None]).reshape(12, 64, 256)


def table_gradient(sums, lookup):
    rows = sums.reshape(3, 64, 4, 64).transpose(1, 3, 0, 2).reshape(4096, HEADS)
    return lax.dot_general(lookup, rows, (((0,), (0,)), ((), ())), precision=lax.Precision.HIGHEST)


AXES = ("dp", "tensor")


def device_index(x, y, z, core):
    return (x % 2 * 16 + y % 4 * 4 + z % 4) * 4 + x // 2 % 2 * 2 + core


def pairs(move):
    places = [(x, y, z, c) for x in range(4) for y in range(4) for z in range(4) for c in range(2)]
    return [(device_index(*p), device_index(*move(*p))) for p in places]


CORE_SWAP = pairs(lambda x, y, z, c: (x, y, z, 1 - c))
FAR_SWAP = pairs(lambda x, y, z, c: ((x + 2) % 4, y, z, c))
NEAR_SWAP = pairs(lambda x, y, z, c: (x ^ 1, y, z, c))
TURN = {
    "y": [pairs(lambda x, y, z, c, s=s: (x, y + s, z, c)) for s in range(4)],
    "z": [pairs(lambda x, y, z, c, s=s: (x, y, z + s, c)) for s in range(4)],
}


def send(values, table):
    return lax.ppermute(values, AXES, table)


def after(values, *others):
    return lax.optimization_barrier((values,) + others)[0]


def scatter_sums(parts):
    got = []
    for shift in (1, 3, 2):
        for n, (values, axis, place) in enumerate(parts):
            rows = values.shape[0] // 4
            piece = lax.dynamic_slice_in_dim(values, (place + shift) % 4 * rows, rows, 0)
            if shift == 2:
                piece = after(piece, got[n])
            got.append(send(piece, TURN[axis][shift]))
    sums = []
    for n, (values, axis, place) in enumerate(parts):
        rows = values.shape[0] // 4
        own = lax.dynamic_slice_in_dim(values, place * rows, rows, 0)
        sums.append(own + got[n] + got[n + len(parts)] + got[n + 2 * len(parts)])
    return sums


def gather_rows(parts):
    got = []
    for shift in (1, 3, 2):
        for n, (values, axis, place) in enumerate(parts):
            piece = after(values, got[n]) if shift == 2 else values
            got.append(send(piece, TURN[axis][shift]))
    fulls = []
    for n, (values, axis, place) in enumerate(parts):
        rows = values.shape[0]
        full = jnp.zeros((4 * rows,) + values.shape[1:], values.dtype)
        for shift, piece in ((0, values), (1, got[n]), (3, got[n + len(parts)]), (2, got[n + 2 * len(parts)])):
            full = lax.dynamic_update_slice_in_dim(full, piece, (place - shift) % 4 * rows, 0)
        fulls.append(full)
    return fulls


def assemble_kernel(core, mine, other, out):
    half = pl.program_id(0) // BLOCKS
    out[...] = jnp.where(half == core[0], mine[...], other[...]).astype(out.dtype)


def assemble(core, mine, other, kind):
    def spot(is_mine):
        def index(i, c):
            here = (i // BLOCKS == c[0]) == is_mine
            return (jnp.where(here, i % BLOCKS, jnp.where(i < BLOCKS, 0, BLOCKS - 1)), 0)

        return index

    return pl.pallas_call(
        assemble_kernel,
        grid_spec=pltpu.PrefetchScalarGridSpec(
            num_scalar_prefetch=1,
            grid=(2 * BLOCKS,),
            in_specs=[pl.BlockSpec((BLOCK, D), spot(True)), pl.BlockSpec((BLOCK, D), spot(False))],
            out_specs=pl.BlockSpec((BLOCK, D), lambda i, c: (i, 0)),
        ),
        out_shape=jax.ShapeDtypeStruct((2 * HALF, D), kind),
        cost_estimate=pl.CostEstimate(flops=10_000_000, bytes_accessed=15_000_000, transcendentals=0),
        name="assemble",
    )(core, mine, other)


def gather_weights(far, core, qkv_weight, qv_bias, rel_table, proj_weight):
    few = jnp.concatenate([qv_bias.astype(F32).reshape(-1), rel_table.astype(F32).reshape(-1)])
    few = jnp.pad(few, (0, 8 * D - few.shape[0])).reshape(8, D)
    own = jnp.concatenate(
        [
            qkv_weight.astype(F32).transpose(0, 2, 1).reshape(3 * 96, D),
            proj_weight.astype(F32),
            few,
        ]
    )
    near = send(own, CORE_SWAP)
    over = send(own, FAR_SWAP)
    last = send(over, CORE_SWAP)
    pick = lambda flag, a, b: jnp.where(flag == 1, a, b)
    low = (pick(core, near, own), pick(core, own, near))
    high = (pick(core, last, over), pick(core, over, last))
    shards = [pick(far, high[i], low[i]) for i in (0, 1)] + [pick(far, low[i], high[i]) for i in (0, 1)]
    wqkv = jnp.stack([v[:288].reshape(3, 96, D) for v in shards], axis=1).reshape(3 * D, D)
    wproj = jnp.concatenate([v[288:384] for v in shards])
    few = jnp.stack([v[384:392].reshape(-1) for v in shards])
    bias = few[:, :192].reshape(4, 2, 96).transpose(1, 0, 2).reshape(2, D)
    table = few[:, 192:699].reshape(4, 169, 3).transpose(1, 0, 2).reshape(169, HEADS)
    return wqkv, wproj, bias, table


def shards(
    tokens_in, attn_gain, attn_shift, qkv_weight, qv_bias, rel_table, proj_weight, proj_bias, moe_gain, moe_shift,
    router_weight, expert_in, expert_in_bias, expert_out, expert_out_bias, expert_ids, cotangent,
):
    group, shard = lax.axis_index("dp"), lax.axis_index("tensor")
    at_x, at_y, at_z = group // 16, group // 4 % 4, group % 4
    far, side = shard // 2, shard % 2
    core = side.astype(jnp.int32).reshape(1)
    place, fill, lookup, heads, segment = layout_consts()
    consts = tuple(jnp.asarray(v).astype(LOW) for v in (place, place.transpose(0, 2, 1), heads, segment))
    lookup = jnp.asarray(lookup)
    wide = lambda v: v.astype(F32).reshape(1, -1)

    wqkv, wproj, bias_qv, table = gather_weights(far, side, qkv_weight, qv_bias, rel_table, proj_weight)
    weights = dict(
        attn_gain=wide(attn_gain),
        attn_shift=wide(attn_shift),
        wqkv=wqkv,
        bqkv=jnp.concatenate([bias_qv[0:1], jnp.zeros((1, D), F32), bias_qv[1:2]], axis=1),
        wproj=wproj,
        bproj=wide(proj_bias),
        moe_gain=wide(moe_gain),
        moe_shift=wide(moe_shift),
        router=jnp.pad(router_weight, ((0, 0), (0, 128 - EXPERTS))),
        out_bias_pad=jnp.pad(expert_out_bias, ((0, 128 - EXPERTS), (0, 0))),
        out_bias_t=jnp.pad(expert_out_bias, ((0, 128 - EXPERTS), (0, 0))).T,
    )
    bias = position_bias(table, jnp.asarray(fill), lookup)
    spot, dest, chunks = sort_plan(expert_ids)
    hidden, base, second, gate, mixed, qkv, prob = attention_forward(
        core, tokens_in, expert_ids, consts, weights, bias
    )
    second_other = send(second, CORE_SWAP)
    (grad_in, grad_out, in_bias, out_bias, gs_theirs, ep_theirs, gg_theirs, gs_mine, ep_mine, gg_mine) = experts(
        core, dest, chunks, second, second_other, cotangent, expert_ids,
        spot.reshape(TILES, 1, TILE), spot.reshape(-1, 1), weights["router"],
        expert_in, expert_in_bias.astype(F32), expert_out,
    )

    gs_theirs = send(gs_theirs, CORE_SWAP)
    gg = gg_mine[:, 0] + send(gg_theirs[:, 0], CORE_SWAP)
    gg = (gg + send(gg, FAR_SWAP)).reshape(HALF, 1)
    gs, gs_far = [], []
    for b in range(BLOCKS):
        block = slice(b * BLOCK, (b + 1) * BLOCK)
        gs.append(gs_mine[block] + gs_theirs[block])
        gs_far.append(send(after(gs[b], gs_far[-1]) if b else gs[b], FAR_SWAP))

    ep = ep_mine + send(ep_theirs, CORE_SWAP)
    ep = ep + send(after(ep, gs_far[-1]), FAR_SWAP)
    block_half = base + gate * ep
    block_out = assemble(core, block_half, send(block_half, CORE_SWAP), LOW)

    sum_in, sum_out = scatter_sums([(grad_in, "y", at_y), (grad_out, "z", at_z)])
    sum_in, sum_out = scatter_sums([(sum_in, "z", at_z), (sum_out, "y", at_y)])
    sum_in, sum_out = sum_in + send(sum_in, NEAR_SWAP), sum_out + send(sum_out, NEAR_SWAP)
    sum_in, sum_out = gather_rows([(sum_in, "z", at_z), (sum_out, "y", at_y)])
    sum_in, sum_out = gather_rows([(sum_in, "y", at_y), (sum_out, "z", at_z)])

    sums, grads = None, []
    for b in range(BLOCKS):
        grad, *sums = attention_backward(
            b, core, gs[b], gs_far[b], gg, hidden, cotangent, tokens_in, expert_ids, mixed, qkv, prob,
            consts, weights, sums,
        )
        grads.append(grad)
    others = [send(v, CORE_SWAP) for v in grads]
    input_grad = assemble(core, jnp.concatenate(grads), jnp.concatenate(others), F32)

    grad_wqkv, grad_wproj, small, pair_sums = sums
    rows = jnp.pad(table_gradient(pair_sums, lookup).reshape(-1), (0, 8 * D - 169 * HEADS)).reshape(8, D)
    by_shard = jnp.concatenate([grad_wqkv.reshape(3, 4, 96, D), grad_wproj.reshape(1, 4, 96, D)])

    def pack(index):
        return jnp.concatenate([lax.dynamic_index_in_dim(by_shard, index, 1, False).reshape(D, D), small, rows])

    packed = pack(shard) + send(pack(shard ^ 1), CORE_SWAP)
    packed = jnp.concatenate([packed, in_bias, out_bias, jnp.zeros((88, D), F32)])
    (packed,) = scatter_sums([(packed, "y", at_y)])
    (packed,) = scatter_sums([(packed, "z", at_z)])
    packed = packed + send(packed, NEAR_SWAP)
    (packed,) = gather_rows([(packed, "z", at_z)])
    (packed,) = gather_rows([(packed, "y", at_y)])
    few = packed[D : D + 24]
    grad_table = few[16:24].reshape(-1)[: 169 * HEADS].reshape(169, HEADS)
    return (
        block_out,
        input_grad,
        few[0],
        few[1],
        packed[:288].reshape(3, 96, D).transpose(0, 2, 1),
        lax.dynamic_slice_in_dim(few[5:7], shard * 96, 96, 1),
        lax.dynamic_slice_in_dim(grad_table, shard * 3, 3, 1),
        packed[288:384],
        few[2],
        few[3],
        few[4],
        few[8:16].T,
        sum_in.reshape(EXPERTS, D, D),
        packed[408:416],
        sum_out.reshape(EXPERTS, D, D),
        packed[416:424],
    )


def solution(mesh):
    placed = (
        P("dp", None),
        P(),
        P(),
        P(None, None, "tensor"),
        P(None, "tensor"),
        P(None, "tensor"),
        P("tensor", None),
        P(),
        P(),
        P(),
        P(),
        P(None, None, "tensor"),
        P(None, "tensor"),
        P(None, "tensor", None),
        P(),
        P("dp", None),
        P("dp", None),
    )
    return jax.shard_map(
        shards,
        mesh=mesh,
        in_specs=placed,
        out_specs=(
            P("dp", None),
            P("dp", None),
            P(),
            P(),
            P(None, None, "tensor"),
            P(None, "tensor"),
            P(None, "tensor"),
            P("tensor", None),
            P(),
            P(),
            P(),
            P(),
            P(None, None, "tensor"),
            P(None, "tensor"),
            P(None, "tensor", None),
            P(),
        ),
        check_vma=False,
    )
```

```python
import functools
import math

import jax
import jax.numpy as jnp
import numpy as np
from jax import lax
from jax.experimental import pallas as pl
from jax.experimental.pallas import tpu as pltpu
from jax.sharding import PartitionSpec as P

F32 = jnp.float32
LOW = jnp.bfloat16
D = 384
HEADS = 12
EXPERTS = 8
SIDE = 14
WINDOW = 7
IMAGE = 196
HALF = 2352
BLOCK = 784
BLOCKS = 3
PADDED = 256
SLICE = 208
TILE = 168
TILES = 28
HALF_TILES = 14
GROUPS = 28
SORTED = 224
RUN = 7
STEPS_HALF = HALF_TILES // RUN
DISPATCH = 2 * STEPS_HALF
SLOTS = 960
CHUNK = 240
STORE = EXPERTS * SLOTS + 8
CLEAR = 248
MASK_FILL = -1e30
SCALE = 32 ** (-0.5)
VMEM = 60 * 1024 * 1024


def layout_consts():
    cell = np.arange(IMAGE)
    row = (cell // SIDE - WINDOW // 2) % SIDE
    col = (cell % SIDE - WINDOW // 2) % SIDE
    slot = (row // WINDOW * 2 + col // WINDOW) * 64 + row % WINDOW * WINDOW + col % WINDOW
    place = np.zeros((4, PADDED, SLICE), np.float32)
    for k in range(4):
        place[k, slot, 4 * k + cell] = 1.0
    part = lambda v: (v >= SIDE - WINDOW) * 1 + (v >= SIDE - WINDOW // 2) * 1
    label = np.full((PADDED,), -1)
    label[slot] = part(row) * 3 + part(col)
    label = label.reshape(4, 64)
    real = np.arange(64) < WINDOW * WINDOW
    meet = (label[:, :, None] == label[:, None, :]) | ~real[None, :, None]
    fill = np.where(meet & real[None, None, :], 0.0, MASK_FILL).astype(np.float32)
    fill = np.tile(fill, (1, 1, 4))
    spot = np.arange(49)
    entry = (spot[:, None] // 7 - spot[None, :] // 7 + 6) * 13 + spot[:, None] % 7 - spot[None, :] % 7 + 6
    lookup = np.zeros((64, 64, 169), np.float32)
    lookup[spot[:, None], spot[None, :], entry] = 1.0
    heads = (np.arange(256)[:, None] // 64 == np.arange(128)[None, :] // 32).astype(np.float32)
    segment = (np.arange(256)[:, None] // 64 == np.arange(256)[None, :] // 64).astype(np.float32)
    return place, fill, lookup.reshape(4096, 169), heads, segment


def nn(a, b):
    return lax.dot_general(a, b, (((1,), (0,)), ((), ())), preferred_element_type=F32)


def nt(a, b):
    return lax.dot_general(a, b, (((1,), (1,)), ((), ())), preferred_element_type=F32)


def tn(a, b):
    return lax.dot_general(a, b, (((0,), (0,)), ((), ())), preferred_element_type=F32)


def norm_parts(values):
    centre = values - jnp.mean(values, axis=-1, keepdims=True)
    inverse = lax.rsqrt(jnp.mean(centre * centre, axis=-1, keepdims=True) + 1e-5)
    return centre * inverse, inverse


def norm_back(upstream, unit, inverse, gain):
    scaled = upstream * gain
    return inverse * (
        scaled
        - jnp.mean(scaled, axis=-1, keepdims=True)
        - unit * jnp.mean(scaled * unit, axis=-1, keepdims=True)
    )


def column_sum(values):
    return jnp.sum(values, axis=0, keepdims=True)


def router_softmax(second, router):
    logits = nn(second, router)
    lane = lax.broadcasted_iota(jnp.int32, logits.shape, 1)
    logits = jnp.where(lane < EXPERTS, logits, MASK_FILL)
    power = jnp.exp(logits - jnp.max(logits, axis=-1, keepdims=True))
    return power / jnp.sum(power, axis=-1, keepdims=True), lane


def expand(part, heads):
    return jnp.concatenate([part] * 4, axis=0) * heads


def attention_kernel(
    core, x_ref, ids_ref, attn_gain, attn_shift, wqkv_wide, bqkv, bias, place, place_t, heads, segment,
    wproj_wide, bproj, moe_gain, moe_shift, router, out_bias,
    hidden_ref, base_ref, second_ref, gate_ref, mixed_ref, qkv_ref, prob_ref, window_ref,
    low_scr, raster_scr, wqkv, wproj, power_scr,
):
    @pl.when(pl.program_id(0) == 0)
    def _():
        wqkv[...] = wqkv_wide[...].T.astype(LOW)
        wproj[...] = wproj_wide[...].astype(LOW)

    x = x_ref[...].astype(F32)
    unit, _ = norm_parts(x)
    low_scr[...] = (unit * attn_gain[...] + attn_shift[...]).astype(LOW)
    raster_scr[...] = jnp.zeros_like(raster_scr)
    lane = lax.broadcasted_iota(jnp.int32, (64, 128), 1)
    left = lane < 64

    def project(k, carry):
        start = pl.multiple_of(k * 192, 64)
        rows = nn(place[k], low_scr[pl.ds(start, SLICE), :]).astype(LOW)
        qkv = (nn(rows, wqkv[...]) + bqkv[...]).astype(LOW)
        qkv_ref[pl.ds(pl.multiple_of(k * PADDED, PADDED), PADDED), :] = qkv
        return carry

    def scores_of(k, w, g):
        at = pl.ds(pl.multiple_of(k * PADDED + w * 64, 64), 64)
        q = qkv_ref[at, g * 128 : g * 128 + 128]
        kx = expand(qkv_ref[at, D + g * 128 : D + g * 128 + 128], heads[...])
        return nt(q, kx) * SCALE + bias[w * 3 + g]

    def finish(k):
        spot = pl.multiple_of(k * 768, 64)
        total = nn(power_scr[...], segment[...])
        prob_ref[pl.ds(spot, 768), :] = (power_scr[...].astype(F32) / total).astype(LOW)
        for w in range(4):
            at = pl.ds(pl.multiple_of(k * PADDED + w * 64, 64), 64)
            parts = []
            for g in range(3):
                vx = expand(qkv_ref[at, 2 * D + g * 128 : 2 * D + g * 128 + 128], heads[...])
                prob = prob_ref[pl.ds(pl.multiple_of(spot + (w * 3 + g) * 64, 64), 64), :]
                parts.append(nn(prob, vx).astype(LOW))
            window_ref[at, :] = jnp.concatenate(parts, axis=1)
        mixed = window_ref[pl.ds(pl.multiple_of(k * PADDED, PADDED), PADDED), :]
        raster_scr[pl.ds(pl.multiple_of(k * 192, 64), SLICE), :] += nn(place_t[k], mixed)
        return total

    def image(k, bounds):
        project(k, 0)
        for w in range(4):
            for g in range(3):
                power_scr[(w * 3 + g) * 64 : (w * 3 + g) * 64 + 64, :] = jnp.exp(scores_of(k, w, g)).astype(LOW)
        total = finish(k).reshape(96, 8, 256)
        return jnp.minimum(bounds[0], jnp.min(total, axis=0)), jnp.maximum(bounds[1], jnp.max(total, axis=0))

    def image_shifted(k, carry):
        for w in range(4):
            for g in range(3):
                scores = scores_of(k, w, g)
                power = []
                for c in range(2):
                    piece = scores[:, c * 128 : c * 128 + 128]
                    first = jnp.max(jnp.where(left, piece, 2 * MASK_FILL), axis=-1, keepdims=True)
                    other = jnp.max(jnp.where(left, 2 * MASK_FILL, piece), axis=-1, keepdims=True)
                    power.append(jnp.exp(piece - jnp.where(left, first, other)))
                power_scr[(w * 3 + g) * 64 : (w * 3 + g) * 64 + 64, :] = jnp.concatenate(power, axis=1).astype(LOW)
        finish(k)
        return carry

    least, most = lax.fori_loop(0, 4, image, (jnp.full((8, 256), 1.0, F32), jnp.full((8, 256), 1.0, F32)))
    safe = (jnp.min(least) > 1e-25) & (jnp.max(most) < 1e25)

    @pl.when(jnp.logical_not(safe))
    def _():
        raster_scr[...] = jnp.zeros_like(raster_scr)
        lax.fori_loop(0, 4, image_shifted, 0)

    mixed = raster_scr[...].astype(LOW)
    mixed_ref[...] = mixed
    hidden = x + (nn(mixed, wproj[...]) + bproj[...])
    hidden_ref[...] = hidden
    unit, _ = norm_parts(hidden)
    second = (unit * moe_gain[...] + moe_shift[...]).astype(LOW)
    second_ref[...] = second.astype(F32)
    probs, lanes = router_softmax(second, router[...])
    chosen = lanes == ids_ref[...]
    gate = jnp.sum(jnp.where(chosen, probs, 0.0), axis=-1, keepdims=True)
    gate_ref[...] = gate
    base_ref[...] = hidden + gate * nn(chosen.astype(F32).astype(LOW), out_bias[...])


def whole(shape):
    return pl.BlockSpec(shape, lambda *_: (0,) * len(shape))


def attention_forward(core, x, ids, consts, weights, bias):
    place, place_t, heads, segment, _ = consts
    at_block = lambda width: pl.BlockSpec((BLOCK, width), lambda i, s: (s[0] * BLOCKS + i, 0))
    rows = lambda height, width: pl.BlockSpec((height, width), lambda i, s: (i, 0))
    fixed = [weights[n] for n in ("attn_gain", "attn_shift", "wqkv", "bqkv")]
    tail = [weights[n] for n in ("wproj", "bproj", "moe_gain", "moe_shift", "router", "out_bias_pad")]
    operands = fixed + [bias, place, place_t, heads, segment] + tail
    return pl.pallas_call(
        attention_kernel,
        grid_spec=pltpu.PrefetchScalarGridSpec(
            num_scalar_prefetch=1,
            grid=(BLOCKS,),
            in_specs=[at_block(D), at_block(1)] + [whole(v.shape) for v in operands],
            out_specs=[
                rows(BLOCK, D),
                rows(BLOCK, D),
                rows(BLOCK, D),
                rows(BLOCK, 1),
                rows(BLOCK, D),
                rows(4 * PADDED, 3 * D),
                rows(48 * 64, 256),
                rows(4 * PADDED, D),
            ],
            scratch_shapes=[
                pltpu.VMEM((BLOCK, D), LOW),
                pltpu.VMEM((BLOCK, D), F32),
                pltpu.VMEM((D, 3 * D), LOW),
                pltpu.VMEM((D, D), LOW),
                pltpu.VMEM((768, 256), LOW),
            ],
        ),
        out_shape=[
            jax.ShapeDtypeStruct((HALF, D), F32),
            jax.ShapeDtypeStruct((HALF, D), F32),
            jax.ShapeDtypeStruct((HALF, D), F32),
            jax.ShapeDtypeStruct((HALF, 1), F32),
            jax.ShapeDtypeStruct((HALF, D), LOW),
            jax.ShapeDtypeStruct((BLOCKS * 4 * PADDED, 3 * D), LOW),
            jax.ShapeDtypeStruct((BLOCKS * 48 * 64, 256), LOW),
            jax.ShapeDtypeStruct((BLOCKS * 4 * PADDED, D), LOW),
        ],
        compiler_params=pltpu.CompilerParams(vmem_limit_bytes=VMEM),
        cost_estimate=pl.CostEstimate(flops=1_000_000, bytes_accessed=100_000, transcendentals=0),
        name="attention_forward",
    )(core, x, ids, *operands)


def gelu_parts(values):
    size = jnp.abs(values)
    decay = jnp.exp(-0.5 * values * values)
    t = 1.0 / (1.0 + (0.3275911 / math.sqrt(2.0)) * size)
    poly = t * (0.254829592 + t * (-0.284496736 + t * (1.421413741 + t * (-1.453152027 + t * 1.061405429))))
    half = 0.5 * poly * decay
    cdf = jnp.where(values >= 0.0, 1.0 - half, half)
    return values * cdf, cdf + values * decay * (1.0 / math.sqrt(2.0 * math.pi))


def experts_kernel(
    core, dest, chunks,
    own_ref, other_ref, g_ref, meta_ref, router_t, w_in, b_in, w_out,
    grad_in, grad_out, in_bias, out_bias, act_ref, gs_theirs, gg_theirs, gs_mine, gg_mine,
    store,
):
    step = pl.program_id(0)
    undo = DISPATCH + EXPERTS

    def first_tile(j, flip):
        half = jnp.where(j < STEPS_HALF, flip, 1 - flip)
        return half * HALF_TILES + j % STEPS_HALF * RUN

    @pl.when(step == 0)
    def _():
        def clear(j, carry):
            store[pl.ds(pl.multiple_of(j * CLEAR, 8), CLEAR), :] = jnp.zeros((CLEAR, 2 * D), F32)
            return carry

        lax.fori_loop(0, STORE // CLEAR, clear, 0)

    @pl.when(step < DISPATCH)
    def _():
        begin = first_tile(step, core[0])
        for r in range(RUN):
            second = jnp.where(step < STEPS_HALF, own_ref[r], other_ref[r]).astype(LOW)
            logits = nt(router_t[...], second)
            kind = lax.broadcasted_iota(jnp.int32, logits.shape, 0)
            logits = jnp.where(kind < EXPERTS, logits, MASK_FILL)
            power = jnp.exp(logits - jnp.max(logits, axis=0, keepdims=True))
            chosen = jnp.where(kind == meta_ref[r, 1:2, :], power, 0.0)
            gate = jnp.sum(chosen, axis=0, keepdims=True) / jnp.sum(power, axis=0, keepdims=True)
            high = gate.astype(LOW).astype(F32)
            spot = lax.broadcasted_iota(jnp.int32, (SORTED, TILE), 0)
            here = spot == meta_ref[r, 0:1, :]
            pick = jnp.where(here, 1.0, 0.0).astype(LOW)
            pick_high = jnp.where(here, high, 0.0).astype(LOW)
            pick_rest = jnp.where(here, gate - high, 0.0).astype(LOW)
            moved = jnp.concatenate([nn(pick, second), nn(pick_high, g_ref[r]) + nn(pick_rest, g_ref[r])], axis=1)
            for j in range(GROUPS):
                at = pl.multiple_of(dest[(begin + r) * GROUPS + j] * 8, 8)
                store[pl.ds(at, 8), :] = moved[j * 8 : j * 8 + 8, :]

    @pl.when((step >= DISPATCH) & (step < undo))
    def _():
        e = step - DISPATCH
        grad_in[...] = jnp.zeros_like(grad_in)
        grad_out[...] = jnp.zeros_like(grad_out)
        lane = lax.broadcasted_iota(jnp.int32, (CHUNK, 128), 1)

        def chunk(c, sums):
            at = pl.ds(pl.multiple_of(e * SLOTS + c * CHUNK, 16), CHUNK)
            buffer = store[at, :D].astype(LOW)
            grad = store[at, D:].astype(LOW)
            act, slope = gelu_parts(nn(buffer, w_in[0]) + b_in[pl.ds(e, 1), :].astype(F32))
            act = act.astype(LOW)
            act_ref[pl.ds(pl.multiple_of(c * CHUNK, 16), CHUNK), :] = act
            grad_act = nt(grad, w_out[0])
            gate_grad = jnp.sum(act.astype(F32) * grad_act, axis=-1, keepdims=True)
            high = gate_grad.astype(LOW).astype(F32)
            grad_pre = (grad_act * slope).astype(LOW)
            store[at, :D] = nt(grad_pre, w_in[0])
            store[at, D : D + 128] = jnp.where(lane == 0, high, gate_grad - high)
            grad_in[...] += tn(buffer, grad_pre)
            grad_out[...] += tn(act, grad)
            return sums[0] + column_sum(grad_pre.astype(F32)), sums[1] + column_sum(grad.astype(F32))

        zero = jnp.zeros((1, D), F32)
        sums = lax.fori_loop(0, chunks[e], chunk, (zero, zero))
        in_bias[pl.ds(e, 1), :] = sums[0]
        out_bias[pl.ds(e, 1), :] = sums[1]

    def collect(gs_ref, gg_ref):
        begin = first_tile(step - undo, 1 - core[0])
        ones = jnp.where(lax.broadcasted_iota(jnp.int32, (8, 128), 1) < 2, 1.0, 0.0).astype(LOW)
        for r in range(RUN):
            tile = (begin + r) * GROUPS
            rows = [store[pl.ds(pl.multiple_of(dest[tile + j] * 8, 8), 8), : D + 128] for j in range(GROUPS)]
            rows = jnp.concatenate(rows, axis=0).astype(LOW)
            spot = lax.broadcasted_iota(jnp.int32, (SORTED, TILE), 0)
            pick = jnp.where(spot == meta_ref[r, 0:1, :], 1.0, 0.0).astype(LOW)
            back = tn(pick, rows)
            gs_ref[r] = back[:, :D]
            gg_ref[r] = nt(ones, back[:, D:].astype(LOW))[0:1, :]

    @pl.when((step >= undo) & (step < undo + STEPS_HALF))
    def _():
        collect(gs_theirs, gg_theirs)

    @pl.when(step >= undo + STEPS_HALF)
    def _():
        collect(gs_mine, gg_mine)


def tile_blocks(begin, undo):
    def index(i, c, *_):
        back = i >= undo
        j = jnp.where(back, i - undo, jnp.clip(i - begin, 0, DISPATCH - 1))
        flip = jnp.where(back, 1 - c[0], c[0])
        half = jnp.where(j < STEPS_HALF, flip, 1 - flip)
        return half * STEPS_HALF + j % STEPS_HALF

    return index


def run_from(begin):
    return lambda i, *_: (jnp.clip(i - begin, 0, STEPS_HALF - 1), 0, 0)


def experts(core, dest, chunks, own, other, g, meta, router_t, w_in, b_in, w_out):
    undo = DISPATCH + EXPERTS
    tile = tile_blocks(0, undo)
    expert = lambda i, *_: (jnp.clip(i - DISPATCH, 0, EXPERTS - 1), 0, 0)
    flat = lambda i, *_: (jnp.clip(i - DISPATCH, 0, EXPERTS - 1), 0)
    out_half = lambda begin: [
        pl.BlockSpec((RUN, TILE, D), run_from(begin)),
        pl.BlockSpec((RUN, 1, TILE), run_from(begin)),
    ]
    half = [
        jax.ShapeDtypeStruct((HALF_TILES, TILE, D), F32),
        jax.ShapeDtypeStruct((HALF_TILES, 1, TILE), F32),
    ]
    return pl.pallas_call(
        experts_kernel,
        grid_spec=pltpu.PrefetchScalarGridSpec(
            num_scalar_prefetch=3,
            grid=(undo + DISPATCH,),
            in_specs=[
                pl.BlockSpec((RUN, TILE, D), run_from(0)),
                pl.BlockSpec((RUN, TILE, D), run_from(STEPS_HALF)),
                pl.BlockSpec((RUN, TILE, D), lambda i, *s: (tile(jnp.minimum(i, undo - 1), *s), 0, 0)),
                pl.BlockSpec((RUN, 2, TILE), lambda i, *s: (tile(i, *s), 0, 0)),
                whole((16, D)),
                pl.BlockSpec((1, D, D), expert),
                whole((EXPERTS, D)),
                pl.BlockSpec((1, D, D), expert),
            ],
            out_specs=[
                pl.BlockSpec((D, D), flat),
                pl.BlockSpec((D, D), flat),
                whole((EXPERTS, D)),
                whole((EXPERTS, D)),
                pl.BlockSpec((SLOTS, D), flat),
            ]
            + out_half(undo)
            + out_half(undo + STEPS_HALF),
            scratch_shapes=[pltpu.VMEM((STORE, 2 * D), F32)],
        ),
        out_shape=[
            jax.ShapeDtypeStruct((EXPERTS * D, D), F32),
            jax.ShapeDtypeStruct((EXPERTS * D, D), F32),
            jax.ShapeDtypeStruct((EXPERTS, D), F32),
            jax.ShapeDtypeStruct((EXPERTS, D), F32),
            jax.ShapeDtypeStruct((EXPERTS * SLOTS, D), LOW),
        ]
        + half
        + half,
        compiler_params=pltpu.CompilerParams(vmem_limit_bytes=VMEM),
        cost_estimate=pl.CostEstimate(flops=1_000_000, bytes_accessed=100_000, transcendentals=0),
        name="experts",
    )(core, dest, chunks, own, other, g, meta, router_t, w_in, b_in, w_out)


def output_kernel(core, dest, chunks, act_ref, meta_ref, w_out, ep_theirs, ep_mine, store):
    step = pl.program_id(0)

    @pl.when(step == 0)
    def _():
        store[EXPERTS * SLOTS :, :] = jnp.zeros((8, D), F32)

    @pl.when(step < EXPERTS)
    def _():
        def chunk(c, carry):
            rows = act_ref[pl.ds(pl.multiple_of(c * CHUNK, 16), CHUNK), :]
            store[pl.ds(pl.multiple_of(step * SLOTS + c * CHUNK, 16), CHUNK), :] = nn(rows, w_out[0])
            return carry

        lax.fori_loop(0, chunks[step], chunk, 0)

    def collect(ep_ref):
        j = step - EXPERTS
        half = jnp.where(j < STEPS_HALF, 1 - core[0], core[0])
        begin = half * HALF_TILES + j % STEPS_HALF * RUN
        for r in range(RUN):
            tile = (begin + r) * GROUPS
            rows = [store[pl.ds(pl.multiple_of(dest[tile + j] * 8, 8), 8), :] for j in range(GROUPS)]
            rows = jnp.concatenate(rows, axis=0).astype(LOW)
            spot = lax.broadcasted_iota(jnp.int32, (SORTED, TILE), 0)
            pick = jnp.where(spot == meta_ref[r, 0:1, :], 1.0, 0.0).astype(LOW)
            ep_ref[r] = tn(pick, rows)

    @pl.when((step >= EXPERTS) & (step < EXPERTS + STEPS_HALF))
    def _():
        collect(ep_theirs)

    @pl.when(step >= EXPERTS + STEPS_HALF)
    def _():
        collect(ep_mine)


def experts_output(core, dest, chunks, act, meta, w_out):
    tile = tile_blocks(-DISPATCH, EXPERTS)
    half = jax.ShapeDtypeStruct((HALF_TILES, TILE, D), F32)
    return pl.pallas_call(
        output_kernel,
        grid_spec=pltpu.PrefetchScalarGridSpec(
            num_scalar_prefetch=3,
            grid=(EXPERTS + DISPATCH,),
            in_specs=[
                pl.BlockSpec((SLOTS, D), lambda i, *_: (jnp.minimum(i, EXPERTS - 1), 0)),
                pl.BlockSpec((RUN, 2, TILE), lambda i, *s: (tile(i, *s), 0, 0)),
                pl.BlockSpec((1, D, D), lambda i, *_: (jnp.minimum(i, EXPERTS - 1), 0, 0)),
            ],
            out_specs=[
                pl.BlockSpec((RUN, TILE, D), run_from(EXPERTS)),
                pl.BlockSpec((RUN, TILE, D), run_from(EXPERTS + STEPS_HALF)),
            ],
            scratch_shapes=[pltpu.VMEM((STORE, D), F32)],
        ),
        out_shape=[half, half],
        compiler_params=pltpu.CompilerParams(vmem_limit_bytes=VMEM),
        cost_estimate=pl.CostEstimate(flops=1_000_000, bytes_accessed=100_000, transcendentals=0),
        name="experts_output",
    )(core, dest, chunks, act, meta, w_out)


def sort_plan(ids):
    named = ids.reshape(TILES, TILE)
    kinds = jnp.arange(EXPERTS, dtype=jnp.int32)
    chosen = (named[:, :, None] == kinds).astype(F32)
    before = jnp.asarray(np.tril(np.ones((TILE, TILE), np.float32), -1))
    rank = jnp.einsum("ij,tje->tie", before, chosen)
    count = jnp.sum(chosen, axis=1).astype(jnp.int32)
    groups = (count + 7) // 8
    ahead = jnp.asarray(np.tril(np.ones((EXPERTS, EXPERTS), np.int32), -1))
    first = jnp.sum(groups[:, None, :] * ahead[None], axis=-1)
    spot = jnp.sum(chosen * (rank + 8.0 * first[:, None, :].astype(F32)), axis=-1).astype(jnp.int32)
    earlier = jnp.asarray(np.tril(np.ones((TILES, TILES), np.int32), -1))
    offset = jnp.sum(earlier[:, :, None] * groups[None], axis=1)
    j = jnp.arange(GROUPS, dtype=jnp.int32)[None, :, None]
    inside = (j >= first[:, None, :]) & (j < (first + groups)[:, None, :])
    target = kinds * (SLOTS // 8) + offset[:, None, :] + j - first[:, None, :]
    dest = jnp.sum(jnp.where(inside, target, 0), axis=-1)
    dest = jnp.where(jnp.any(inside, axis=-1), dest, EXPERTS * SLOTS // 8).astype(jnp.int32)
    used = jnp.sum(groups, axis=0) * 8
    chunks = (used + CHUNK - 1) // CHUNK
    return spot, dest.reshape(-1), chunks.astype(jnp.int32)


def backward_kernel(
    first, core, gs_a, gs_b, hidden_ref, g_ref, x_ref, ids_ref, mixed_ref, qkv_ref, prob_ref, window_ref,
    attn_gain, attn_shift, wqkv, place, place_t, heads, spread, wproj, moe_gain, moe_shift, router, out_bias_t,
    *refs,
):
    if first:
        input_grad, grad_wqkv, grad_wproj, small, table, raster_scr, mixed_scr = refs
        grad_wqkv[...] = jnp.zeros_like(grad_wqkv)
        grad_wproj[...] = jnp.zeros_like(grad_wproj)
        small[...] = jnp.zeros_like(small)
        table[...] = jnp.zeros_like(table)
    else:
        before, (input_grad, grad_wqkv, grad_wproj, small, table, raster_scr, mixed_scr) = refs[:4], refs[4:]
        for was, now in zip(before, (grad_wqkv, grad_wproj, small, table)):
            now[...] = was[...]

    g_low = g_ref[...]
    g = g_low.astype(F32)
    unit, inverse = norm_parts(hidden_ref[...])
    second = (unit * moe_gain[...] + moe_shift[...]).astype(LOW)
    probs, lanes = router_softmax(second, router[...])
    chosen = lanes == ids_ref[...]
    gate = jnp.sum(jnp.where(chosen, probs, 0.0), axis=-1, keepdims=True)
    with_bias = jnp.sum(jnp.where(chosen, nn(g_low, out_bias_t[...]), 0.0), axis=-1, keepdims=True)
    sums = gs_a[BLOCK:, :] + gs_b[BLOCK:, :]
    columns = []
    for piece in range(3):
        count = min(D, BLOCK - piece * D)
        same = lax.broadcasted_iota(jnp.int32, (count, D), 0) == lax.broadcasted_iota(jnp.int32, (count, D), 1)
        columns.append(jnp.sum(jnp.where(same, sums[piece : piece + 1, :], 0.0), axis=-1, keepdims=True))
    gated = jnp.concatenate(columns, axis=0)
    grad_logit = (gated + gate * with_bias) * (chosen.astype(F32) - probs)
    logit_high = grad_logit.astype(LOW)
    logit_rest = (grad_logit - logit_high.astype(F32)).astype(LOW)
    grad_router = tn(logit_high, second) + tn(logit_rest, second)
    grad_second = gs_a[:BLOCK, :] + gs_b[:BLOCK, :] + nt(logit_high, router[...]) + nt(logit_rest, router[...])
    small[3:4, :] += column_sum(grad_second * unit)
    small[4:5, :] += column_sum(grad_second)
    small[8:16, :] += grad_router[:EXPERTS, :]
    grad_hidden = g + norm_back(grad_second, unit, inverse, moe_gain[...])
    grad_low = grad_hidden.astype(LOW)
    small[2:3, :] += column_sum(grad_low.astype(F32))
    grad_wproj[...] += tn(mixed_ref[...], grad_low)
    mixed_scr[...] = nt(grad_low, wproj[...].astype(LOW)).astype(LOW)
    raster_scr[...] = jnp.zeros_like(raster_scr)

    def image(k, carry):
        start = pl.multiple_of(k * 192, 64)
        grad_mixed = nn(place[k], mixed_scr[pl.ds(start, SLICE), :])
        dots = (grad_mixed * window_ref[pl.ds(pl.multiple_of(k * PADDED, PADDED), PADDED), :].astype(F32)).astype(LOW)
        grad_mixed = grad_mixed.astype(LOW)
        weighted = [nn(dots[:, c * 128 : c * 128 + 128], spread[...]) for c in range(3)]
        outs = []
        for w in range(4):
            row = slice(w * 64, w * 64 + 64)
            at = pl.ds(pl.multiple_of(k * PADDED + w * 64, 64), 64)
            parts = [[], [], []]
            for c in range(3):
                q = qkv_ref[at, c * 128 : c * 128 + 128]
                kx = expand(qkv_ref[at, D + c * 128 : D + c * 128 + 128], heads[...])
                vx = expand(qkv_ref[at, 2 * D + c * 128 : 2 * D + c * 128 + 128], heads[...])
                prob_low = prob_ref[pl.ds(pl.multiple_of(((k * 4 + w) * 3 + c) * 64, 64), 64), :]
                prob = prob_low.astype(F32)
                upstream = grad_mixed[row, c * 128 : c * 128 + 128]
                grad_prob = nt(upstream, vx)
                grad_score = prob * (grad_prob - weighted[c][row])
                table[c * 64 : c * 64 + 64, :] += grad_score
                low = (grad_score * SCALE).astype(LOW)
                parts[0].append(nn(low, kx).astype(LOW))
                for slot, left, right in ((1, low, q), (2, prob_low, upstream)):
                    full = tn(left, right)
                    kept = [full[h * 64 : h * 64 + 64] * heads[h * 64 : h * 64 + 64, :].astype(F32) for h in range(4)]
                    parts[slot].append((kept[0] + kept[1] + kept[2] + kept[3]).astype(LOW))
            outs.append(jnp.concatenate(parts[0] + parts[1] + parts[2], axis=1))
        grads = jnp.concatenate(outs, axis=0)
        raster_scr[pl.ds(start, SLICE), :] += nn(place_t[k], grads)
        return carry

    lax.fori_loop(0, 4, image, 0)
    unit, inverse = norm_parts(x_ref[...].astype(F32))
    attn_low = (unit * attn_gain[...] + attn_shift[...]).astype(LOW)
    raster = raster_scr[...]
    small[5:6, :] += column_sum(raster[:, :D])
    small[6:7, :] += column_sum(raster[:, 2 * D :])
    grads = raster.astype(LOW)
    grad_wqkv[...] += tn(grads, attn_low)
    grad_in = nn(grads, wqkv[...].astype(LOW))
    small[0:1, :] += column_sum(grad_in * unit)
    small[1:2, :] += column_sum(grad_in)
    input_grad[...] = grad_hidden + norm_back(grad_in, unit, inverse, attn_gain[...])


def attention_backward(block, core, gs_a, gs_b, hidden, g, x, ids, mixed, qkv, prob, window, consts, weights, sums):
    place, place_t, heads, _, spread = consts
    at_block = lambda width: pl.BlockSpec((BLOCK, width), lambda i, s: (s[0] * BLOCKS + block, 0))
    rows = lambda height, width: pl.BlockSpec((height, width), lambda i, s: (block, 0))
    fixed = [weights[n] for n in ("attn_gain", "attn_shift", "wqkv")] + [place, place_t, heads, spread]
    fixed = fixed + [weights[n] for n in ("wproj", "moe_gain", "moe_shift", "router", "out_bias_t")]
    totals = [(3 * D, D), (D, D), (16, D), (192, 256)]
    before = [] if sums is None else list(sums)
    return pl.pallas_call(
        functools.partial(backward_kernel, sums is None),
        grid_spec=pltpu.PrefetchScalarGridSpec(
            num_scalar_prefetch=1,
            grid=(1,),
            in_specs=[
                whole((BLOCK + 8, D)),
                whole((BLOCK + 8, D)),
                rows(BLOCK, D),
                at_block(D),
                at_block(D),
                at_block(1),
                rows(BLOCK, D),
                rows(4 * PADDED, 3 * D),
                rows(48 * 64, 256),
                rows(4 * PADDED, D),
            ]
            + [whole(v.shape) for v in fixed + before],
            out_specs=[whole((BLOCK, D))] + [whole(v) for v in totals],
            scratch_shapes=[pltpu.VMEM((BLOCK, 3 * D), F32), pltpu.VMEM((BLOCK, D), LOW)],
        ),
        out_shape=[jax.ShapeDtypeStruct(v, F32) for v in [(BLOCK, D)] + totals],
        compiler_params=pltpu.CompilerParams(vmem_limit_bytes=VMEM),
        cost_estimate=pl.CostEstimate(flops=1_000_000, bytes_accessed=100_000, transcendentals=0),
        name="attention_backward",
    )(core, gs_a, gs_b, hidden, g, x, ids, mixed, qkv, prob, window, *fixed, *before)


def head_bias(table, lookup):
    rows = lax.dot_general(table.astype(LOW), lookup.astype(LOW), (((0,), (1,)), ((), ())), preferred_element_type=F32)
    return rows.reshape(96, 128)


def position_bias(heads, fill):
    rows = heads.reshape(3, 4, 64, 64).transpose(0, 2, 1, 3).reshape(1, 3, 64, 256)
    return (rows + fill[:, None]).reshape(12, 64, 256)


def table_gradient(sums, lookup):
    rows = sums.reshape(3, 64, 4, 64).transpose(1, 3, 0, 2).reshape(4096, HEADS)
    return lax.dot_general(lookup, rows, (((0,), (0,)), ((), ())), precision=lax.Precision.HIGHEST)


AXES = ("dp", "tensor")


def device_index(x, y, z, core):
    return (x % 2 * 16 + y % 4 * 4 + z % 4) * 4 + x // 2 % 2 * 2 + core


def pairs(move):
    places = [(x, y, z, c) for x in range(4) for y in range(4) for z in range(4) for c in range(2)]
    return [(device_index(*p), device_index(*move(*p))) for p in places]


CORE_SWAP = pairs(lambda x, y, z, c: (x, y, z, 1 - c))
FAR_SWAP = pairs(lambda x, y, z, c: ((x + 2) % 4, y, z, c))
NEAR_SWAP = pairs(lambda x, y, z, c: (x ^ 1, y, z, c))
TURN = {
    "y": [pairs(lambda x, y, z, c, s=s: (x, y + s, z, c)) for s in range(4)],
    "z": [pairs(lambda x, y, z, c, s=s: (x, y, z + s, c)) for s in range(4)],
}


def send(values, table):
    return lax.ppermute(values, AXES, table)


def after(values, *others):
    return lax.optimization_barrier((values,) + others)[0]


def scatter_near(parts):
    return [send(quarter(v, at + shift, dim), TURN[axis][shift]) for shift in (1, 3) for v, axis, at, dim in parts]


def quarter(values, index, dim):
    return lax.dynamic_index_in_dim(values, index % 4, dim, False)


def scatter_across(parts, near):
    return [
        send(after(quarter(v, at + 2, dim), near[n]), TURN[axis][2]) for n, (v, axis, at, dim) in enumerate(parts)
    ]


def scatter_total(parts, near, across):
    return [
        quarter(v, at, dim) + near[n] + near[n + len(parts)] + across[n]
        for n, (v, axis, at, dim) in enumerate(parts)
    ]


def scatter_sums(parts):
    near = [send(quarter(v, at + shift, dim), TURN[axis][shift]) for shift in (1, 3, 2) for v, axis, at, dim in parts]
    sums = scatter_total(parts, near, near[2 * len(parts) :])
    return [v.reshape((4, v.shape[0] // 4) + v.shape[1:]) for v in sums]


def gather_rows(parts):
    got = []
    for shift in (1, 3, 2):
        for n, (values, axis, place) in enumerate(parts):
            piece = after(values, got[n]) if shift == 2 and len(parts) > 1 else values
            got.append(send(piece, TURN[axis][shift]))
    fulls = []
    for n, (values, axis, place) in enumerate(parts):
        rows = values.shape[0]
        full = jnp.zeros((4 * rows,) + values.shape[1:], values.dtype)
        for shift, piece in ((0, values), (1, got[n]), (3, got[n + len(parts)]), (2, got[n + 2 * len(parts)])):
            full = lax.dynamic_update_slice_in_dim(full, piece, (place - shift) % 4 * rows, 0)
        fulls.append(full)
    return fulls


def assemble_kernel(core, mine, other, *refs):
    refs[-1][...] = jnp.where(pl.program_id(0) == 0, mine[...], other[...]).astype(refs[-1].dtype)


def assemble(core, b, mine, other, kind, before):
    def spot(i, c):
        return (jnp.where(i == 0, c[0], 1 - c[0]) * BLOCKS + b, 0)

    kept = [] if before is None else [before]
    return pl.pallas_call(
        assemble_kernel,
        grid_spec=pltpu.PrefetchScalarGridSpec(
            num_scalar_prefetch=1,
            grid=(2,),
            in_specs=[whole((BLOCK, D)), whole((BLOCK, D))] + [pl.BlockSpec(memory_space=pl.ANY)] * len(kept),
            out_specs=pl.BlockSpec((BLOCK, D), spot),
        ),
        out_shape=jax.ShapeDtypeStruct((2 * HALF, D), kind),
        input_output_aliases={3: 0} if kept else {},
        cost_estimate=pl.CostEstimate(flops=1_000_000, bytes_accessed=100_000, transcendentals=0),
        name="assemble",
    )(core, mine, other, *kept)


def gather_shards(far, core, own):
    near = send(own, CORE_SWAP)
    over = send(own, FAR_SWAP)
    last = send(over, CORE_SWAP)
    pick = lambda flag, a, b: jnp.where(flag == 1, a, b)
    low = (pick(core, near, own), pick(core, own, near))
    high = (pick(core, last, over), pick(core, over, last))
    return [pick(far, high[i], low[i]) for i in (0, 1)] + [pick(far, low[i], high[i]) for i in (0, 1)]


def gather_weights(far, core, qkv_weight, qv_bias, rel_table, proj_weight, lookup):
    own = jnp.concatenate(
        [
            qkv_weight.astype(F32).transpose(0, 2, 1).reshape(3 * 96, D),
            proj_weight.astype(F32),
        ]
    )
    shards = gather_shards(far, core, own)
    wqkv = jnp.stack([v[:288].reshape(3, 96, D) for v in shards], axis=1).reshape(3 * D, D)
    wproj = jnp.concatenate([v[288:384] for v in shards])
    few = jnp.pad(qv_bias.astype(F32), ((0, 6), (0, 32)))
    shards = gather_shards(far, core, jnp.concatenate([head_bias(after(rel_table, own), lookup), few]))
    heads = jnp.stack([v[:96].reshape(3, 64, 64) for v in shards]).reshape(HEADS, 64, 64)
    bias = jnp.concatenate([v[96:98, :96] for v in shards], axis=1)
    return wqkv, wproj, bias, heads


def pack_rest(shard, sums, in_bias, out_bias, lookup):
    grad_wqkv, grad_wproj, small, pair_sums = sums
    rows = jnp.pad(table_gradient(pair_sums, lookup).reshape(-1), (0, 8 * D - 169 * HEADS)).reshape(8, D)
    by_shard = jnp.concatenate([grad_wqkv.reshape(3, 4, 96, D), grad_wproj.reshape(1, 4, 96, D)])

    def pack(index):
        return jnp.concatenate([lax.dynamic_index_in_dim(by_shard, index, 1, False).reshape(D, D), small, rows])

    packed = pack(shard) + send(pack(shard ^ 1), CORE_SWAP)
    return jnp.concatenate([packed, in_bias, out_bias, jnp.zeros((88, D), F32)]).reshape(4, 128, D)


def shards(
    tokens_in, attn_gain, attn_shift, qkv_weight, qv_bias, rel_table, proj_weight, proj_bias, moe_gain, moe_shift,
    router_weight, expert_in, expert_in_bias, expert_out, expert_out_bias, expert_ids, cotangent,
):
    group, shard = lax.axis_index("dp"), lax.axis_index("tensor")
    at_x, at_y, at_z = group // 16, group // 4 % 4, group % 4
    far, side = shard // 2, shard % 2
    core = side.astype(jnp.int32).reshape(1)
    place, fill, lookup, heads, segment = layout_consts()
    consts = (place, place.transpose(0, 2, 1), heads, segment, heads.T)
    consts = tuple(jnp.asarray(v).astype(LOW) for v in consts)
    lookup = jnp.asarray(lookup)
    wide = lambda v: v.astype(F32).reshape(1, -1)

    wqkv, wproj, bias_qv, table = gather_weights(
        far, side, qkv_weight, qv_bias, rel_table, proj_weight, lookup
    )
    router = jnp.pad(router_weight, ((0, 0), (0, 128 - EXPERTS)))
    weights = dict(
        attn_gain=wide(attn_gain),
        attn_shift=wide(attn_shift),
        wqkv=wqkv,
        bqkv=jnp.concatenate([bias_qv[0:1], jnp.zeros((1, D), F32), bias_qv[1:2]], axis=1),
        wproj=wproj,
        bproj=wide(proj_bias),
        moe_gain=wide(moe_gain),
        moe_shift=wide(moe_shift),
        router=router,
        out_bias_pad=jnp.pad(expert_out_bias, ((0, 128 - EXPERTS), (0, 0))),
        out_bias_t=jnp.pad(expert_out_bias, ((0, 128 - EXPERTS), (0, 0))).T,
    )
    bias = position_bias(table, jnp.asarray(fill))
    spot, dest, chunks = sort_plan(expert_ids)
    meta = jnp.stack([spot, expert_ids.reshape(TILES, TILE)], axis=1)
    hidden, base, second, gate, mixed, qkv, prob, window = attention_forward(
        core, tokens_in, expert_ids, consts, weights, bias
    )
    second = second.reshape(HALF_TILES, TILE, D)
    grad_in, grad_out, in_bias, out_bias, act, gs_theirs, gg_theirs, gs_mine, gg_mine = experts(
        core, dest, chunks, second, send(second, CORE_SWAP), cotangent.reshape(TILES, TILE, D), meta,
        router[:, :16].T, expert_in, expert_in_bias.astype(F32), expert_out,
    )

    gs_theirs = send(gs_theirs, CORE_SWAP).reshape(HALF, D)
    gs_mine = gs_mine.reshape(HALF, D)
    gg = gg_mine.reshape(HALF) + send(gg_theirs.reshape(HALF), CORE_SWAP)
    gg = jnp.pad(gg.reshape(BLOCKS, BLOCK), ((0, 0), (0, 8 * D - BLOCK))).reshape(BLOCKS, 8, D)
    gs = [
        jnp.concatenate([gs_mine[b * BLOCK : (b + 1) * BLOCK] + gs_theirs[b * BLOCK : (b + 1) * BLOCK], gg[b]])
        for b in range(BLOCKS)
    ]
    gs_far = [send(gs[0], FAR_SWAP)]

    def attend(b, sums):
        return attention_backward(
            b, core, gs[b], gs_far[b], hidden, cotangent, tokens_in, expert_ids, mixed, qkv, prob, window,
            consts, weights, sums,
        )

    sixteen = [[i * 16 + j for j in range(16)] for i in range(2)]
    gather = lambda v: lax.all_gather(v, "dp", axis=0, axis_index_groups=sixteen, tiled=True)
    sum_out = lax.psum_scatter(grad_out, "dp", scatter_dimension=0, axis_index_groups=sixteen, tiled=True)
    cells = grad_in.reshape(4, 4, 2, 96, D)
    first = [(cells[:, :, 0], "y", at_y, 0), (cells[:, :, 1], "z", at_z, 1)]
    near = scatter_near(first)
    ep_theirs, ep_mine = experts_output(core, dest, chunks, after(act, gs[0]), meta, expert_out)
    ep_mine, near = lax.optimization_barrier((ep_mine, near))
    across = scatter_across(first, near)
    gs_far.append(send(gs[1], FAR_SWAP))
    ep_mine, ep_theirs, gs_far[0] = lax.optimization_barrier((ep_mine, ep_theirs, gs_far[0]))
    ep_theirs = send(ep_theirs, CORE_SWAP)
    gs_far.append(send(after(gs[2], gs_far[0]), FAR_SWAP))
    grad_0, *sums = attend(0, None)
    across, gs_far[1], grad_0, ep_theirs = lax.optimization_barrier((across, gs_far[1], grad_0, ep_theirs))
    halves = scatter_total(first, near, across)
    second = [(halves[0], "z", at_z, 0), (halves[1], "y", at_y, 0)]
    near = scatter_near(second)
    grad_1, *sums = attend(1, sums)
    ep = (ep_mine + ep_theirs).reshape(HALF, D)
    ep = [ep[b * BLOCK : (b + 1) * BLOCK] for b in range(BLOCKS)]
    near, sum_out, gs_far[2], grad_1, ep[0] = lax.optimization_barrier((near, sum_out, gs_far[2], grad_1, ep[0]))
    near_out = send(sum_out, NEAR_SWAP)
    across = scatter_across(second, near)
    ep_far = [send(after(ep[0], gs_far[2]), FAR_SWAP)]
    grad_2, *sums = attend(2, sums)
    near_out, across, grad_2, sums, ep_far[0] = lax.optimization_barrier((near_out, across, grad_2, sums, ep_far[0]))
    sum_out = gather(sum_out + near_out)
    sum_in = jnp.concatenate(scatter_total(second, near, across))
    sum_in = gather(sum_in + send(sum_in, NEAR_SWAP))
    ep_far.append(send(after(ep[1], ep_far[0]), FAR_SWAP))
    packed = pack_rest(shard, sums, in_bias, out_bias, lookup)
    (packed,) = scatter_sums([(packed, "y", at_y, 0)])
    (packed,) = scatter_sums([(packed, "z", at_z, 0)])
    packed, ep_far[1] = lax.optimization_barrier((packed.reshape(32, D), ep_far[1]))
    packed = packed + send(packed, NEAR_SWAP)
    ep_far.append(send(after(ep[2], ep_far[1]), FAR_SWAP))

    block_out, input_grad = None, None
    for b, grad in enumerate((grad_0, grad_1, grad_2)):
        block = slice(b * BLOCK, (b + 1) * BLOCK)
        block_half = base[block] + gate[block] * (ep[b] + ep_far[b])
        block_out = assemble(core, b, block_half, send(block_half, CORE_SWAP), LOW, block_out)
        input_grad = assemble(core, b, grad, send(grad, CORE_SWAP), F32, input_grad)

    (packed,) = gather_rows([(packed, "z", at_z)])
    (packed,) = gather_rows([(packed, "y", at_y)])
    few = packed[D : D + 24]
    grad_table = few[16:24].reshape(-1)[: 169 * HEADS].reshape(169, HEADS)
    return (
        block_out,
        input_grad,
        few[0],
        few[1],
        packed[:288].reshape(3, 96, D).transpose(0, 2, 1),
        lax.dynamic_slice_in_dim(few[5:7], shard * 96, 96, 1),
        lax.dynamic_slice_in_dim(grad_table, shard * 3, 3, 1),
        packed[288:384],
        few[2],
        few[3],
        few[4],
        few[8:16].T,
        sum_in.reshape(EXPERTS, D, D),
        packed[408:416],
        sum_out.reshape(EXPERTS, D, D),
        packed[416:424],
    )


def solution(mesh):
    placed = (
        P("dp", None),
        P(),
        P(),
        P(None, None, "tensor"),
        P(None, "tensor"),
        P(None, "tensor"),
        P("tensor", None),
        P(),
        P(),
        P(),
        P(),
        P(None, None, "tensor"),
        P(None, "tensor"),
        P(None, "tensor", None),
        P(),
        P("dp", None),
        P("dp", None),
    )
    return jax.shard_map(
        shards,
        mesh=mesh,
        in_specs=placed,
        out_specs=(
            P("dp", None),
            P("dp", None),
            P(),
            P(),
            P(None, None, "tensor"),
            P(None, "tensor"),
            P(None, "tensor"),
            P("tensor", None),
            P(),
            P(),
            P(),
            P(),
            P(None, None, "tensor"),
            P(None, "tensor"),
            P(None, "tensor", None),
            P(),
        ),
        check_vma=False,
    )
```

```python
import functools
import math

import jax
import jax.numpy as jnp
import numpy as np
from jax import lax
from jax.experimental import pallas as pl
from jax.experimental.pallas import tpu as pltpu
from jax.sharding import PartitionSpec as P

F32 = jnp.float32
LOW = jnp.bfloat16
D = 384
HEADS = 12
EXPERTS = 8
SIDE = 14
WINDOW = 7
IMAGE = 196
HALF = 2352
BLOCK = 784
BLOCKS = 3
PADDED = 256
SLICE = 208
TILE = 168
TILES = 28
HALF_TILES = 14
GROUPS = 28
SORTED = 224
RUN = 7
STEPS_HALF = HALF_TILES // RUN
DISPATCH = 2 * STEPS_HALF
SLOTS = 960
CHUNK = 240
STORE = EXPERTS * SLOTS + 8
CLEAR = 248
CUTS = (0, 336, 1008, 1568, 2352)
PIECES = (336, 336, 112, 784)
MASK_FILL = -1e30
SCALE = 32 ** (-0.5)
VMEM = 60 * 1024 * 1024


def layout_consts():
    cell = np.arange(IMAGE)
    row = (cell // SIDE - WINDOW // 2) % SIDE
    col = (cell % SIDE - WINDOW // 2) % SIDE
    slot = (row // WINDOW * 2 + col // WINDOW) * 64 + row % WINDOW * WINDOW + col % WINDOW
    place = np.zeros((4, PADDED, SLICE), np.float32)
    for k in range(4):
        place[k, slot, 4 * k + cell] = 1.0
    part = lambda v: (v >= SIDE - WINDOW) * 1 + (v >= SIDE - WINDOW // 2) * 1
    label = np.full((PADDED,), -1)
    label[slot] = part(row) * 3 + part(col)
    label = label.reshape(4, 64)
    real = np.arange(64) < WINDOW * WINDOW
    meet = (label[:, :, None] == label[:, None, :]) | ~real[None, :, None]
    fill = np.where(meet & real[None, None, :], 0.0, MASK_FILL).astype(np.float32)
    fill = np.tile(fill, (1, 1, 4))
    spot = np.arange(49)
    entry = (spot[:, None] // 7 - spot[None, :] // 7 + 6) * 13 + spot[:, None] % 7 - spot[None, :] % 7 + 6
    lookup = np.zeros((64, 64, 169), np.float32)
    lookup[spot[:, None], spot[None, :], entry] = 1.0
    heads = (np.arange(256)[:, None] // 64 == np.arange(128)[None, :] // 32).astype(np.float32)
    segment = (np.arange(256)[:, None] // 64 == np.arange(256)[None, :] // 64).astype(np.float32)
    return place, fill, lookup.reshape(4096, 169), heads, segment


def nn(a, b):
    return lax.dot_general(a, b, (((1,), (0,)), ((), ())), preferred_element_type=F32)


def nt(a, b):
    return lax.dot_general(a, b, (((1,), (1,)), ((), ())), preferred_element_type=F32)


def tn(a, b):
    return lax.dot_general(a, b, (((0,), (0,)), ((), ())), preferred_element_type=F32)


def norm_parts(values):
    centre = values - jnp.mean(values, axis=-1, keepdims=True)
    inverse = lax.rsqrt(jnp.mean(centre * centre, axis=-1, keepdims=True) + 1e-5)
    return centre * inverse, inverse


def norm_back(upstream, unit, inverse, gain):
    scaled = upstream * gain
    return inverse * (
        scaled
        - jnp.mean(scaled, axis=-1, keepdims=True)
        - unit * jnp.mean(scaled * unit, axis=-1, keepdims=True)
    )


def column_sum(values):
    return jnp.sum(values, axis=0, keepdims=True)


def router_softmax(second, router):
    logits = nn(second, router)
    lane = lax.broadcasted_iota(jnp.int32, logits.shape, 1)
    logits = jnp.where(lane < EXPERTS, logits, MASK_FILL)
    power = jnp.exp(logits - jnp.max(logits, axis=-1, keepdims=True))
    return power / jnp.sum(power, axis=-1, keepdims=True), lane


def expand(part, heads):
    return jnp.concatenate([part] * 4, axis=0) * heads


def attention_kernel(
    core, x_ref, ids_ref, attn_gain, attn_shift, wqkv_wide, bqkv, bias, place, place_t, heads, segment,
    wproj_wide, bproj, moe_gain, moe_shift, router, out_bias,
    hidden_ref, base_ref, second_ref, gate_ref, mixed_ref, qkv_ref, prob_ref, window_ref,
    low_scr, raster_scr, wqkv, wproj, power_scr,
):
    @pl.when(pl.program_id(0) == 0)
    def _():
        wqkv[...] = wqkv_wide[...].T.astype(LOW)
        wproj[...] = wproj_wide[...].astype(LOW)

    x = x_ref[...].astype(F32)
    unit, _ = norm_parts(x)
    low_scr[...] = (unit * attn_gain[...] + attn_shift[...]).astype(LOW)
    raster_scr[...] = jnp.zeros_like(raster_scr)
    lane = lax.broadcasted_iota(jnp.int32, (64, 128), 1)
    left = lane < 64

    def project(k, carry):
        start = pl.multiple_of(k * 192, 64)
        rows = nn(place[k], low_scr[pl.ds(start, SLICE), :]).astype(LOW)
        qkv = (nn(rows, wqkv[...]) + bqkv[...]).astype(LOW)
        qkv_ref[pl.ds(pl.multiple_of(k * PADDED, PADDED), PADDED), :] = qkv
        return carry

    def scores_of(k, w, g):
        at = pl.ds(pl.multiple_of(k * PADDED + w * 64, 64), 64)
        q = qkv_ref[at, g * 128 : g * 128 + 128]
        kx = expand(qkv_ref[at, D + g * 128 : D + g * 128 + 128], heads[...])
        return nt(q, kx) * SCALE + bias[w * 3 + g]

    def finish(k):
        spot = pl.multiple_of(k * 768, 64)
        total = nn(power_scr[...], segment[...])
        prob_ref[pl.ds(spot, 768), :] = (power_scr[...].astype(F32) / total).astype(LOW)
        for w in range(4):
            at = pl.ds(pl.multiple_of(k * PADDED + w * 64, 64), 64)
            parts = []
            for g in range(3):
                vx = expand(qkv_ref[at, 2 * D + g * 128 : 2 * D + g * 128 + 128], heads[...])
                prob = prob_ref[pl.ds(pl.multiple_of(spot + (w * 3 + g) * 64, 64), 64), :]
                parts.append(nn(prob, vx).astype(LOW))
            window_ref[at, :] = jnp.concatenate(parts, axis=1)
        mixed = window_ref[pl.ds(pl.multiple_of(k * PADDED, PADDED), PADDED), :]
        raster_scr[pl.ds(pl.multiple_of(k * 192, 64), SLICE), :] += nn(place_t[k], mixed)
        return total

    def image(k, bounds):
        project(k, 0)
        for w in range(4):
            for g in range(3):
                power_scr[(w * 3 + g) * 64 : (w * 3 + g) * 64 + 64, :] = jnp.exp(scores_of(k, w, g)).astype(LOW)
        total = finish(k).reshape(96, 8, 256)
        return jnp.minimum(bounds[0], jnp.min(total, axis=0)), jnp.maximum(bounds[1], jnp.max(total, axis=0))

    def image_shifted(k, carry):
        for w in range(4):
            for g in range(3):
                scores = scores_of(k, w, g)
                power = []
                for c in range(2):
                    piece = scores[:, c * 128 : c * 128 + 128]
                    first = jnp.max(jnp.where(left, piece, 2 * MASK_FILL), axis=-1, keepdims=True)
                    other = jnp.max(jnp.where(left, 2 * MASK_FILL, piece), axis=-1, keepdims=True)
                    power.append(jnp.exp(piece - jnp.where(left, first, other)))
                power_scr[(w * 3 + g) * 64 : (w * 3 + g) * 64 + 64, :] = jnp.concatenate(power, axis=1).astype(LOW)
        finish(k)
        return carry

    least, most = lax.fori_loop(0, 4, image, (jnp.full((8, 256), 1.0, F32), jnp.full((8, 256), 1.0, F32)))
    safe = (jnp.min(least) > 1e-25) & (jnp.max(most) < 1e25)

    @pl.when(jnp.logical_not(safe))
    def _():
        raster_scr[...] = jnp.zeros_like(raster_scr)
        lax.fori_loop(0, 4, image_shifted, 0)

    mixed = raster_scr[...].astype(LOW)
    mixed_ref[...] = mixed
    hidden = x + (nn(mixed, wproj[...]) + bproj[...])
    hidden_ref[...] = hidden
    unit, _ = norm_parts(hidden)
    second = (unit * moe_gain[...] + moe_shift[...]).astype(LOW)
    second_ref[...] = second.astype(F32)
    probs, lanes = router_softmax(second, router[...])
    chosen = lanes == ids_ref[...]
    gate = jnp.sum(jnp.where(chosen, probs, 0.0), axis=-1, keepdims=True)
    gate_ref[...] = gate
    base_ref[...] = hidden + gate * nn(chosen.astype(F32).astype(LOW), out_bias[...])


def whole(shape):
    return pl.BlockSpec(shape, lambda *_: (0,) * len(shape))


def attention_forward(core, x, ids, consts, weights, bias):
    place, place_t, heads, segment, _ = consts
    at_block = lambda width: pl.BlockSpec((BLOCK, width), lambda i, s: (s[0] * BLOCKS + i, 0))
    rows = lambda height, width: pl.BlockSpec((height, width), lambda i, s: (i, 0))
    fixed = [weights[n] for n in ("attn_gain", "attn_shift", "wqkv", "bqkv")]
    tail = [weights[n] for n in ("wproj", "bproj", "moe_gain", "moe_shift", "router", "out_bias_pad")]
    operands = fixed + [bias, place, place_t, heads, segment] + tail
    return pl.pallas_call(
        attention_kernel,
        grid_spec=pltpu.PrefetchScalarGridSpec(
            num_scalar_prefetch=1,
            grid=(BLOCKS,),
            in_specs=[at_block(D), at_block(1)] + [whole(v.shape) for v in operands],
            out_specs=[
                rows(BLOCK, D),
                rows(BLOCK, D),
                rows(BLOCK, D),
                rows(BLOCK, 1),
                rows(BLOCK, D),
                rows(4 * PADDED, 3 * D),
                rows(48 * 64, 256),
                rows(4 * PADDED, D),
            ],
            scratch_shapes=[
                pltpu.VMEM((BLOCK, D), LOW),
                pltpu.VMEM((BLOCK, D), F32),
                pltpu.VMEM((D, 3 * D), LOW),
                pltpu.VMEM((D, D), LOW),
                pltpu.VMEM((768, 256), LOW),
            ],
        ),
        out_shape=[
            jax.ShapeDtypeStruct((HALF, D), F32),
            jax.ShapeDtypeStruct((HALF, D), F32),
            jax.ShapeDtypeStruct((HALF, D), F32),
            jax.ShapeDtypeStruct((HALF, 1), F32),
            jax.ShapeDtypeStruct((HALF, D), LOW),
            jax.ShapeDtypeStruct((BLOCKS * 4 * PADDED, 3 * D), LOW),
            jax.ShapeDtypeStruct((BLOCKS * 48 * 64, 256), LOW),
            jax.ShapeDtypeStruct((BLOCKS * 4 * PADDED, D), LOW),
        ],
        compiler_params=pltpu.CompilerParams(vmem_limit_bytes=VMEM),
        cost_estimate=pl.CostEstimate(flops=1_000_000, bytes_accessed=100_000, transcendentals=0),
        name="attention_forward",
    )(core, x, ids, *operands)


def gelu_parts(values):
    size = jnp.abs(values)
    decay = jnp.exp(-0.5 * values * values)
    t = 1.0 / (1.0 + (0.3275911 / math.sqrt(2.0)) * size)
    poly = t * (0.254829592 + t * (-0.284496736 + t * (1.421413741 + t * (-1.453152027 + t * 1.061405429))))
    half = 0.5 * poly * decay
    cdf = jnp.where(values >= 0.0, 1.0 - half, half)
    return values * cdf, cdf + values * decay * (1.0 / math.sqrt(2.0 * math.pi))


def experts_kernel(
    core, dest, chunks,
    own_ref, other_ref, g_ref, meta_ref, router_t, w_in, b_in, w_out,
    grad_in, grad_out, in_bias, out_bias, act_ref, gs_theirs, gg_theirs, gs_mine, gg_mine,
    store,
):
    step = pl.program_id(0)
    undo = DISPATCH + EXPERTS

    def first_tile(j, flip):
        half = jnp.where(j < STEPS_HALF, flip, 1 - flip)
        return half * HALF_TILES + j % STEPS_HALF * RUN

    @pl.when(step == 0)
    def _():
        def clear(j, carry):
            store[pl.ds(pl.multiple_of(j * CLEAR, 8), CLEAR), :] = jnp.zeros((CLEAR, 2 * D), F32)
            return carry

        lax.fori_loop(0, STORE // CLEAR, clear, 0)

    @pl.when(step < DISPATCH)
    def _():
        begin = first_tile(step, core[0])
        for r in range(RUN):
            second = jnp.where(step < STEPS_HALF, own_ref[r], other_ref[r]).astype(LOW)
            logits = nt(router_t[...], second)
            kind = lax.broadcasted_iota(jnp.int32, logits.shape, 0)
            logits = jnp.where(kind < EXPERTS, logits, MASK_FILL)
            power = jnp.exp(logits - jnp.max(logits, axis=0, keepdims=True))
            chosen = jnp.where(kind == meta_ref[r, 1:2, :], power, 0.0)
            gate = jnp.sum(chosen, axis=0, keepdims=True) / jnp.sum(power, axis=0, keepdims=True)
            high = gate.astype(LOW).astype(F32)
            spot = lax.broadcasted_iota(jnp.int32, (SORTED, TILE), 0)
            here = spot == meta_ref[r, 0:1, :]
            pick = jnp.where(here, 1.0, 0.0).astype(LOW)
            pick_high = jnp.where(here, high, 0.0).astype(LOW)
            pick_rest = jnp.where(here, gate - high, 0.0).astype(LOW)
            moved = jnp.concatenate([nn(pick, second), nn(pick_high, g_ref[r]) + nn(pick_rest, g_ref[r])], axis=1)
            for j in range(GROUPS):
                at = pl.multiple_of(dest[(begin + r) * GROUPS + j] * 8, 8)
                store[pl.ds(at, 8), :] = moved[j * 8 : j * 8 + 8, :]

    @pl.when((step >= DISPATCH) & (step < undo))
    def _():
        e = step - DISPATCH
        grad_in[...] = jnp.zeros_like(grad_in)
        grad_out[...] = jnp.zeros_like(grad_out)
        lane = lax.broadcasted_iota(jnp.int32, (CHUNK, 128), 1)

        def chunk(c, sums):
            at = pl.ds(pl.multiple_of(e * SLOTS + c * CHUNK, 16), CHUNK)
            buffer = store[at, :D].astype(LOW)
            grad = store[at, D:].astype(LOW)
            act, slope = gelu_parts(nn(buffer, w_in[0]) + b_in[pl.ds(e, 1), :].astype(F32))
            act = act.astype(LOW)
            act_ref[pl.ds(pl.multiple_of(c * CHUNK, 16), CHUNK), :] = act
            grad_act = nt(grad, w_out[0])
            gate_grad = jnp.sum(act.astype(F32) * grad_act, axis=-1, keepdims=True)
            high = gate_grad.astype(LOW).astype(F32)
            grad_pre = (grad_act * slope).astype(LOW)
            store[at, :D] = nt(grad_pre, w_in[0])
            store[at, D : D + 128] = jnp.where(lane == 0, high, gate_grad - high)
            grad_in[...] += tn(buffer, grad_pre)
            grad_out[...] += tn(act, grad)
            return sums[0] + column_sum(grad_pre.astype(F32)), sums[1] + column_sum(grad.astype(F32))

        zero = jnp.zeros((1, D), F32)
        sums = lax.fori_loop(0, chunks[e], chunk, (zero, zero))
        in_bias[pl.ds(e, 1), :] = sums[0]
        out_bias[pl.ds(e, 1), :] = sums[1]

    def collect(gs_ref, gg_ref):
        begin = first_tile(step - undo, 1 - core[0])
        ones = jnp.where(lax.broadcasted_iota(jnp.int32, (8, 128), 1) < 2, 1.0, 0.0).astype(LOW)
        for r in range(RUN):
            tile = (begin + r) * GROUPS
            rows = [store[pl.ds(pl.multiple_of(dest[tile + j] * 8, 8), 8), : D + 128] for j in range(GROUPS)]
            rows = jnp.concatenate(rows, axis=0).astype(LOW)
            spot = lax.broadcasted_iota(jnp.int32, (SORTED, TILE), 0)
            pick = jnp.where(spot == meta_ref[r, 0:1, :], 1.0, 0.0).astype(LOW)
            back = tn(pick, rows)
            gs_ref[r] = back[:, :D]
            gg_ref[r] = nt(ones, back[:, D:].astype(LOW))[0:1, :]

    @pl.when((step >= undo) & (step < undo + STEPS_HALF))
    def _():
        collect(gs_theirs, gg_theirs)

    @pl.when(step >= undo + STEPS_HALF)
    def _():
        collect(gs_mine, gg_mine)


def tile_blocks(begin, undo):
    def index(i, c, *_):
        back = i >= undo
        j = jnp.where(back, i - undo, jnp.clip(i - begin, 0, DISPATCH - 1))
        flip = jnp.where(back, 1 - c[0], c[0])
        half = jnp.where(j < STEPS_HALF, flip, 1 - flip)
        return half * STEPS_HALF + j % STEPS_HALF

    return index


def run_from(begin):
    return lambda i, *_: (jnp.clip(i - begin, 0, STEPS_HALF - 1), 0, 0)


def experts(core, dest, chunks, own, other, g, meta, router_t, w_in, b_in, w_out):
    undo = DISPATCH + EXPERTS
    tile = tile_blocks(0, undo)
    expert = lambda i, *_: (jnp.clip(i - DISPATCH, 0, EXPERTS - 1), 0, 0)
    flat = lambda i, *_: (jnp.clip(i - DISPATCH, 0, EXPERTS - 1), 0)
    out_half = lambda begin: [
        pl.BlockSpec((RUN, TILE, D), run_from(begin)),
        pl.BlockSpec((RUN, 1, TILE), run_from(begin)),
    ]
    half = [
        jax.ShapeDtypeStruct((HALF_TILES, TILE, D), F32),
        jax.ShapeDtypeStruct((HALF_TILES, 1, TILE), F32),
    ]
    return pl.pallas_call(
        experts_kernel,
        grid_spec=pltpu.PrefetchScalarGridSpec(
            num_scalar_prefetch=3,
            grid=(undo + DISPATCH,),
            in_specs=[
                pl.BlockSpec((RUN, TILE, D), run_from(0)),
                pl.BlockSpec((RUN, TILE, D), run_from(STEPS_HALF)),
                pl.BlockSpec((RUN, TILE, D), lambda i, *s: (tile(jnp.minimum(i, undo - 1), *s), 0, 0)),
                pl.BlockSpec((RUN, 2, TILE), lambda i, *s: (tile(i, *s), 0, 0)),
                whole((16, D)),
                pl.BlockSpec((1, D, D), expert),
                whole((EXPERTS, D)),
                pl.BlockSpec((1, D, D), expert),
            ],
            out_specs=[
                pl.BlockSpec((D, D), flat),
                pl.BlockSpec((D, D), flat),
                whole((EXPERTS, D)),
                whole((EXPERTS, D)),
                pl.BlockSpec((SLOTS, D), flat),
            ]
            + out_half(undo)
            + out_half(undo + STEPS_HALF),
            scratch_shapes=[pltpu.VMEM((STORE, 2 * D), F32)],
        ),
        out_shape=[
            jax.ShapeDtypeStruct((EXPERTS * D, D), F32),
            jax.ShapeDtypeStruct((EXPERTS * D, D), F32),
            jax.ShapeDtypeStruct((EXPERTS, D), F32),
            jax.ShapeDtypeStruct((EXPERTS, D), F32),
            jax.ShapeDtypeStruct((EXPERTS * SLOTS, D), LOW),
        ]
        + half
        + half,
        compiler_params=pltpu.CompilerParams(vmem_limit_bytes=VMEM),
        cost_estimate=pl.CostEstimate(flops=1_000_000, bytes_accessed=100_000, transcendentals=0),
        name="experts",
    )(core, dest, chunks, own, other, g, meta, router_t, w_in, b_in, w_out)


def output_kernel(core, dest, chunks, act_ref, meta_ref, w_out, ep_theirs, ep_mine, store):
    step = pl.program_id(0)

    @pl.when(step == 0)
    def _():
        store[EXPERTS * SLOTS :, :] = jnp.zeros((8, D), F32)

    @pl.when(step < EXPERTS)
    def _():
        def chunk(c, carry):
            rows = act_ref[pl.ds(pl.multiple_of(c * CHUNK, 16), CHUNK), :]
            store[pl.ds(pl.multiple_of(step * SLOTS + c * CHUNK, 16), CHUNK), :] = nn(rows, w_out[0])
            return carry

        lax.fori_loop(0, chunks[step], chunk, 0)

    def collect(ep_ref):
        j = step - EXPERTS
        half = jnp.where(j < STEPS_HALF, 1 - core[0], core[0])
        begin = half * HALF_TILES + j % STEPS_HALF * RUN
        for r in range(RUN):
            tile = (begin + r) * GROUPS
            rows = [store[pl.ds(pl.multiple_of(dest[tile + j] * 8, 8), 8), :] for j in range(GROUPS)]
            rows = jnp.concatenate(rows, axis=0).astype(LOW)
            spot = lax.broadcasted_iota(jnp.int32, (SORTED, TILE), 0)
            pick = jnp.where(spot == meta_ref[r, 0:1, :], 1.0, 0.0).astype(LOW)
            ep_ref[r] = tn(pick, rows)

    @pl.when((step >= EXPERTS) & (step < EXPERTS + STEPS_HALF))
    def _():
        collect(ep_theirs)

    @pl.when(step >= EXPERTS + STEPS_HALF)
    def _():
        collect(ep_mine)


def experts_output(core, dest, chunks, act, meta, w_out):
    tile = tile_blocks(-DISPATCH, EXPERTS)
    half = jax.ShapeDtypeStruct((HALF_TILES, TILE, D), F32)
    return pl.pallas_call(
        output_kernel,
        grid_spec=pltpu.PrefetchScalarGridSpec(
            num_scalar_prefetch=3,
            grid=(EXPERTS + DISPATCH,),
            in_specs=[
                pl.BlockSpec((SLOTS, D), lambda i, *_: (jnp.minimum(i, EXPERTS - 1), 0)),
                pl.BlockSpec((RUN, 2, TILE), lambda i, *s: (tile(i, *s), 0, 0)),
                pl.BlockSpec((1, D, D), lambda i, *_: (jnp.minimum(i, EXPERTS - 1), 0, 0)),
            ],
            out_specs=[
                pl.BlockSpec((RUN, TILE, D), run_from(EXPERTS)),
                pl.BlockSpec((RUN, TILE, D), run_from(EXPERTS + STEPS_HALF)),
            ],
            scratch_shapes=[pltpu.VMEM((STORE, D), F32)],
        ),
        out_shape=[half, half],
        compiler_params=pltpu.CompilerParams(vmem_limit_bytes=VMEM),
        cost_estimate=pl.CostEstimate(flops=1_000_000, bytes_accessed=100_000, transcendentals=0),
        name="experts_output",
    )(core, dest, chunks, act, meta, w_out)


def sort_plan(ids):
    named = ids.reshape(TILES, TILE)
    kinds = jnp.arange(EXPERTS, dtype=jnp.int32)
    chosen = (named[:, :, None] == kinds).astype(F32)
    before = jnp.asarray(np.tril(np.ones((TILE, TILE), np.float32), -1))
    rank = jnp.einsum("ij,tje->tie", before, chosen)
    count = jnp.sum(chosen, axis=1).astype(jnp.int32)
    groups = (count + 7) // 8
    ahead = jnp.asarray(np.tril(np.ones((EXPERTS, EXPERTS), np.int32), -1))
    first = jnp.sum(groups[:, None, :] * ahead[None], axis=-1)
    spot = jnp.sum(chosen * (rank + 8.0 * first[:, None, :].astype(F32)), axis=-1).astype(jnp.int32)
    earlier = jnp.asarray(np.tril(np.ones((TILES, TILES), np.int32), -1))
    offset = jnp.sum(earlier[:, :, None] * groups[None], axis=1)
    j = jnp.arange(GROUPS, dtype=jnp.int32)[None, :, None]
    inside = (j >= first[:, None, :]) & (j < (first + groups)[:, None, :])
    target = kinds * (SLOTS // 8) + offset[:, None, :] + j - first[:, None, :]
    dest = jnp.sum(jnp.where(inside, target, 0), axis=-1)
    dest = jnp.where(jnp.any(inside, axis=-1), dest, EXPERTS * SLOTS // 8).astype(jnp.int32)
    used = jnp.sum(groups, axis=0) * 8
    chunks = (used + CHUNK - 1) // CHUNK
    return spot, dest.reshape(-1), chunks.astype(jnp.int32)


def backward_kernel(
    first, last, core, gs_a, gs_b, hidden_ref, g_ref, x_ref, ids_ref, mixed_ref, qkv_ref, prob_ref, window_ref,
    attn_gain, attn_shift, wqkv, place, place_t, heads, spread, wproj, moe_gain, moe_shift, router, out_bias_t,
    *refs,
):
    if first:
        input_grad, grad_wqkv, grad_wproj, small, table, raster_scr, mixed_scr = refs
        turned = None
        grad_wqkv[...] = jnp.zeros_like(grad_wqkv)
        grad_wproj[...] = jnp.zeros_like(grad_wproj)
        small[...] = jnp.zeros_like(small)
        table[...] = jnp.zeros_like(table)
    else:
        before, refs = refs[:4], refs[4:]
        turned = refs[5] if last else None
        input_grad, grad_wqkv, grad_wproj, small, table, raster_scr, mixed_scr = refs[:5] + refs[-2:]
        for was, now in zip(before, (grad_wqkv, grad_wproj, small, table)):
            now[...] = was[...]

    g_low = g_ref[...]
    g = g_low.astype(F32)
    unit, inverse = norm_parts(hidden_ref[...])
    second = (unit * moe_gain[...] + moe_shift[...]).astype(LOW)
    probs, lanes = router_softmax(second, router[...])
    chosen = lanes == ids_ref[...]
    gate = jnp.sum(jnp.where(chosen, probs, 0.0), axis=-1, keepdims=True)
    with_bias = jnp.sum(jnp.where(chosen, nn(g_low, out_bias_t[...]), 0.0), axis=-1, keepdims=True)
    sums = gs_a[BLOCK:, :] + gs_b[BLOCK:, :]
    columns = []
    for piece in range(3):
        count = min(D, BLOCK - piece * D)
        same = lax.broadcasted_iota(jnp.int32, (count, D), 0) == lax.broadcasted_iota(jnp.int32, (count, D), 1)
        columns.append(jnp.sum(jnp.where(same, sums[piece : piece + 1, :], 0.0), axis=-1, keepdims=True))
    gated = jnp.concatenate(columns, axis=0)
    grad_logit = (gated + gate * with_bias) * (chosen.astype(F32) - probs)
    logit_high = grad_logit.astype(LOW)
    logit_rest = (grad_logit - logit_high.astype(F32)).astype(LOW)
    grad_router = tn(logit_high, second) + tn(logit_rest, second)
    grad_second = gs_a[:BLOCK, :] + gs_b[:BLOCK, :] + nt(logit_high, router[...]) + nt(logit_rest, router[...])
    small[3:4, :] += column_sum(grad_second * unit)
    small[4:5, :] += column_sum(grad_second)
    small[8:16, :] += grad_router[:EXPERTS, :]
    grad_hidden = g + norm_back(grad_second, unit, inverse, moe_gain[...])
    grad_low = grad_hidden.astype(LOW)
    small[2:3, :] += column_sum(grad_low.astype(F32))
    grad_wproj[...] += tn(mixed_ref[...], grad_low)
    mixed_scr[...] = nt(grad_low, wproj[...].astype(LOW)).astype(LOW)
    raster_scr[...] = jnp.zeros_like(raster_scr)

    def image(k, carry):
        start = pl.multiple_of(k * 192, 64)
        grad_mixed = nn(place[k], mixed_scr[pl.ds(start, SLICE), :])
        dots = (grad_mixed * window_ref[pl.ds(pl.multiple_of(k * PADDED, PADDED), PADDED), :].astype(F32)).astype(LOW)
        grad_mixed = grad_mixed.astype(LOW)
        weighted = [nn(dots[:, c * 128 : c * 128 + 128], spread[...]) for c in range(3)]
        outs = []
        for w in range(4):
            row = slice(w * 64, w * 64 + 64)
            at = pl.ds(pl.multiple_of(k * PADDED + w * 64, 64), 64)
            parts = [[], [], []]
            for c in range(3):
                q = qkv_ref[at, c * 128 : c * 128 + 128]
                kx = expand(qkv_ref[at, D + c * 128 : D + c * 128 + 128], heads[...])
                vx = expand(qkv_ref[at, 2 * D + c * 128 : 2 * D + c * 128 + 128], heads[...])
                prob_low = prob_ref[pl.ds(pl.multiple_of(((k * 4 + w) * 3 + c) * 64, 64), 64), :]
                prob = prob_low.astype(F32)
                upstream = grad_mixed[row, c * 128 : c * 128 + 128]
                grad_prob = nt(upstream, vx)
                grad_score = prob * (grad_prob - weighted[c][row])
                table[c * 64 : c * 64 + 64, :] += grad_score
                low = (grad_score * SCALE).astype(LOW)
                parts[0].append(nn(low, kx).astype(LOW))
                for slot, left, right in ((1, low, q), (2, prob_low, upstream)):
                    full = tn(left, right)
                    kept = [full[h * 64 : h * 64 + 64] * heads[h * 64 : h * 64 + 64, :].astype(F32) for h in range(4)]
                    parts[slot].append((kept[0] + kept[1] + kept[2] + kept[3]).astype(LOW))
            outs.append(jnp.concatenate(parts[0] + parts[1] + parts[2], axis=1))
        grads = jnp.concatenate(outs, axis=0)
        raster_scr[pl.ds(start, SLICE), :] += nn(place_t[k], grads)
        return carry

    lax.fori_loop(0, 4, image, 0)
    if last:
        for c in range(3):
            turned[c * 256 : c * 256 + 256, :] = table[c * 64 : c * 64 + 64, :].T
    unit, inverse = norm_parts(x_ref[...].astype(F32))
    attn_low = (unit * attn_gain[...] + attn_shift[...]).astype(LOW)
    raster = raster_scr[...]
    small[5:6, :] += column_sum(raster[:, :D])
    small[6:7, :] += column_sum(raster[:, 2 * D :])
    grads = raster.astype(LOW)
    grad_wqkv[...] += tn(grads, attn_low)
    grad_in = nn(grads, wqkv[...].astype(LOW))
    small[0:1, :] += column_sum(grad_in * unit)
    small[1:2, :] += column_sum(grad_in)
    input_grad[...] = grad_hidden + norm_back(grad_in, unit, inverse, attn_gain[...])


def attention_backward(block, core, gs_a, gs_b, hidden, g, x, ids, mixed, qkv, prob, window, consts, weights, sums):
    place, place_t, heads, _, spread = consts
    at_block = lambda width: pl.BlockSpec((BLOCK, width), lambda i, s: (s[0] * BLOCKS + block, 0))
    rows = lambda height, width: pl.BlockSpec((height, width), lambda i, s: (block, 0))
    fixed = [weights[n] for n in ("attn_gain", "attn_shift", "wqkv")] + [place, place_t, heads, spread]
    fixed = fixed + [weights[n] for n in ("wproj", "moe_gain", "moe_shift", "router", "out_bias_t")]
    totals = [(3 * D, D), (D, D), (16, D), (192, 256)]
    before = [] if sums is None else list(sums)
    last = block == BLOCKS - 1
    extra = [(768, 64)] if last else []
    return pl.pallas_call(
        functools.partial(backward_kernel, sums is None, last),
        grid_spec=pltpu.PrefetchScalarGridSpec(
            num_scalar_prefetch=1,
            grid=(1,),
            in_specs=[
                whole((BLOCK + 8, D)),
                whole((BLOCK + 8, D)),
                rows(BLOCK, D),
                at_block(D),
                at_block(D),
                at_block(1),
                rows(BLOCK, D),
                rows(4 * PADDED, 3 * D),
                rows(48 * 64, 256),
                rows(4 * PADDED, D),
            ]
            + [whole(v.shape) for v in fixed + before],
            out_specs=[whole((BLOCK, D))] + [whole(v) for v in totals + extra],
            scratch_shapes=[pltpu.VMEM((BLOCK, 3 * D), F32), pltpu.VMEM((BLOCK, D), LOW)],
        ),
        out_shape=[jax.ShapeDtypeStruct(v, F32) for v in [(BLOCK, D)] + totals + extra],
        compiler_params=pltpu.CompilerParams(vmem_limit_bytes=VMEM),
        cost_estimate=pl.CostEstimate(flops=1_000_000, bytes_accessed=100_000, transcendentals=0),
        name="attention_backward",
    )(core, gs_a, gs_b, hidden, g, x, ids, mixed, qkv, prob, window, *fixed, *before)


def head_bias(table, lookup):
    rows = lax.dot_general(table.astype(LOW), jnp.asarray(lookup).astype(LOW), (((0,), (1,)), ((), ())), preferred_element_type=F32)
    return rows.reshape(32, D)


def position_bias(heads, fill):
    rows = heads.reshape(3, 4, 64, 64).transpose(0, 2, 1, 3).reshape(1, 3, 64, 256)
    return (rows + fill[:, None]).reshape(12, 64, 256)


def table_gradient(sums, lookup):
    rows = sums.reshape(HEADS, 4096)
    high = rows.astype(LOW)
    rest = (rows - high.astype(F32)).astype(LOW)
    turned = lookup.reshape(64, 64, 169).transpose(1, 0, 2).reshape(4096, 169)
    turned = jnp.asarray(turned).astype(LOW)
    found = nn(jnp.concatenate([high, rest]), turned)
    return (found[:HEADS] + found[HEADS:]).T


AXES = ("dp", "tensor")


def device_index(x, y, z, core):
    return (x % 2 * 16 + y % 4 * 4 + z % 4) * 4 + x // 2 % 2 * 2 + core


def pairs(move):
    places = [(x, y, z, c) for x in range(4) for y in range(4) for z in range(4) for c in range(2)]
    return [(device_index(*p), device_index(*move(*p))) for p in places]


CORE_SWAP = pairs(lambda x, y, z, c: (x, y, z, 1 - c))
FAR_SWAP = pairs(lambda x, y, z, c: ((x + 2) % 4, y, z, c))
NEAR_SWAP = pairs(lambda x, y, z, c: (x ^ 1, y, z, c))
TURN = {
    "y": [pairs(lambda x, y, z, c, s=s: (x, y + s, z, c)) for s in range(4)],
    "z": [pairs(lambda x, y, z, c, s=s: (x, y, z + s, c)) for s in range(4)],
}


PAIR = {
    "y": pairs(lambda x, y, z, c: (x, y ^ 1, z, c)),
    "z": pairs(lambda x, y, z, c: (x, y, z ^ 1, c)),
}


def send(values, table):
    return lax.ppermute(values, AXES, table)


def after(values, *others):
    return lax.optimization_barrier((values,) + others)[0]


def near_pieces(parts):
    return [quarter(v, at + shift, dim) for shift in (1, 3) for v, axis, at, dim in parts]


def near_sends(parts, pieces):
    tables = [TURN[axis][shift] for shift in (1, 3) for v, axis, at, dim in parts]
    return [send(piece, table) for piece, table in zip(pieces, tables)]


def quarter(values, index, dim):
    return lax.dynamic_index_in_dim(values, index % 4, dim, False)


def scatter_across(parts, near):
    return [
        send(after(quarter(v, at + 2, dim), near[n]), TURN[axis][2]) for n, (v, axis, at, dim) in enumerate(parts)
    ]


def scatter_total(parts, near, across):
    return [
        quarter(v, at, dim) + near[n] + near[n + len(parts)] + across[n]
        for n, (v, axis, at, dim) in enumerate(parts)
    ]


def scatter_sums(parts):
    near = [send(quarter(v, at + shift, dim), TURN[axis][shift]) for shift in (1, 3, 2) for v, axis, at, dim in parts]
    sums = scatter_total(parts, near, near[2 * len(parts) :])
    return [v.reshape((4, v.shape[0] // 4) + v.shape[1:]) for v in sums]


def gather_rows(parts):
    got = []
    for shift in (1, 3, 2):
        for n, (values, axis, place) in enumerate(parts):
            piece = after(values, got[n]) if shift == 2 and len(parts) > 1 else values
            got.append(send(piece, TURN[axis][shift]))
    fulls = []
    for n, (values, axis, place) in enumerate(parts):
        rows = values.shape[0]
        full = jnp.zeros((4 * rows,) + values.shape[1:], values.dtype)
        for shift, piece in ((0, values), (1, got[n]), (3, got[n + len(parts)]), (2, got[n + 2 * len(parts)])):
            full = lax.dynamic_update_slice_in_dim(full, piece, (place - shift) % 4 * rows, 0)
        fulls.append(full)
    return fulls


def assemble_kernel(core, mine, other, *refs):
    refs[-1][...] = jnp.where(pl.program_id(0) == 0, mine[...], other[...]).astype(refs[-1].dtype)


def assemble(core, size, first, mine, other, kind, before):
    def spot(i, j, c):
        return (jnp.where(i == 0, c[0], 1 - c[0]) * (HALF // size) + first // size + j, 0)

    kept = [] if before is None else [before]
    rows = pl.BlockSpec((size, D), lambda i, j, c: (j, 0))
    return pl.pallas_call(
        assemble_kernel,
        grid_spec=pltpu.PrefetchScalarGridSpec(
            num_scalar_prefetch=1,
            grid=(2, mine.shape[0] // size),
            in_specs=[rows, rows] + [pl.BlockSpec(memory_space=pl.ANY)] * len(kept),
            out_specs=pl.BlockSpec((size, D), spot),
        ),
        out_shape=jax.ShapeDtypeStruct((2 * HALF, D), kind),
        input_output_aliases={3: 0} if kept else {},
        cost_estimate=pl.CostEstimate(flops=1_000_000, bytes_accessed=100_000, transcendentals=0),
        name="assemble",
    )(core, mine, other, *kept)


def gather_shards(far, core, own):
    over = send(own, FAR_SWAP)
    near = send(own, CORE_SWAP)
    last = send(over, CORE_SWAP)
    pick = lambda flag, a, b: jnp.where(flag == 1, a, b)
    low = (pick(core, near, own), pick(core, own, near))
    high = (pick(core, last, over), pick(core, over, last))
    return [pick(far, high[i], low[i]) for i in (0, 1)] + [pick(far, low[i], high[i]) for i in (0, 1)]


def gather_weights(far, core, qkv_weight, qv_bias, rel_table, proj_weight, lookup):
    own = jnp.concatenate(
        [
            qkv_weight.astype(F32).transpose(0, 2, 1).reshape(3 * 96, D),
            proj_weight.astype(F32),
            head_bias(rel_table, lookup),
            jnp.pad(qv_bias.astype(F32), ((0, 6), (0, D - 96))),
        ]
    )
    shards = gather_shards(far, core, own)
    wqkv = jnp.stack([v[:288].reshape(3, 96, D) for v in shards], axis=1).reshape(3 * D, D)
    wproj = jnp.concatenate([v[288:384] for v in shards])
    heads = jnp.stack([v[384:416].reshape(3, 64, 64) for v in shards]).reshape(HEADS, 64, 64)
    bias = jnp.concatenate([v[416:418, :96] for v in shards], axis=1)
    return wqkv, wproj, bias, heads


def pack_rest(shard, sums, in_bias, out_bias, lookup):
    grad_wqkv, grad_wproj, small, _, pair_sums = sums
    rows = jnp.pad(table_gradient(pair_sums, lookup).reshape(-1), (0, 8 * D - 169 * HEADS)).reshape(8, D)
    by_shard = jnp.concatenate([grad_wqkv.reshape(3, 4, 96, D), grad_wproj.reshape(1, 4, 96, D)])

    def pack(index):
        return jnp.concatenate([lax.dynamic_index_in_dim(by_shard, index, 1, False).reshape(D, D), small, rows])

    packed = pack(shard) + send(pack(shard ^ 1), CORE_SWAP)
    return jnp.concatenate([packed, in_bias, out_bias, jnp.zeros((88, D), F32)]).reshape(4, 128, D)


def shards(
    tokens_in, attn_gain, attn_shift, qkv_weight, qv_bias, rel_table, proj_weight, proj_bias, moe_gain, moe_shift,
    router_weight, expert_in, expert_in_bias, expert_out, expert_out_bias, expert_ids, cotangent,
):
    group, shard = lax.axis_index("dp"), lax.axis_index("tensor")
    at_x, at_y, at_z = group // 16, group // 4 % 4, group % 4
    far, side = shard // 2, shard % 2
    core = side.astype(jnp.int32).reshape(1)
    place, fill, lookup, heads, segment = layout_consts()
    consts = (place, place.transpose(0, 2, 1), heads, segment, heads.T)
    consts = tuple(jnp.asarray(v).astype(LOW) for v in consts)
    wide = lambda v: v.astype(F32).reshape(1, -1)

    wqkv, wproj, bias_qv, table = gather_weights(
        far, side, qkv_weight, qv_bias, rel_table, proj_weight, lookup
    )
    router = jnp.pad(router_weight, ((0, 0), (0, 128 - EXPERTS)))
    weights = dict(
        attn_gain=wide(attn_gain),
        attn_shift=wide(attn_shift),
        wqkv=wqkv,
        bqkv=jnp.concatenate([bias_qv[0:1], jnp.zeros((1, D), F32), bias_qv[1:2]], axis=1),
        wproj=wproj,
        bproj=wide(proj_bias),
        moe_gain=wide(moe_gain),
        moe_shift=wide(moe_shift),
        router=router,
        out_bias_pad=jnp.pad(expert_out_bias, ((0, 128 - EXPERTS), (0, 0))),
        out_bias_t=jnp.pad(expert_out_bias, ((0, 128 - EXPERTS), (0, 0))).T,
    )
    bias = position_bias(table, jnp.asarray(fill))
    spot, dest, chunks = sort_plan(expert_ids)
    meta = jnp.stack([spot, expert_ids.reshape(TILES, TILE)], axis=1)
    hidden, base, second, gate, mixed, qkv, prob, window = attention_forward(
        core, tokens_in, expert_ids, consts, weights, bias
    )
    second = second.reshape(HALF_TILES, TILE, D)
    grad_in, grad_out, in_bias, out_bias, act, gs_theirs, gg_theirs, gs_mine, gg_mine = experts(
        core, dest, chunks, second, send(second, CORE_SWAP), cotangent.reshape(TILES, TILE, D), meta,
        router[:, :16].T, expert_in, expert_in_bias.astype(F32), expert_out,
    )

    sixteen = [[i * 16 + j for j in range(16)] for i in range(2)]
    gather = lambda v: lax.all_gather(v, "dp", axis=0, axis_index_groups=sixteen, tiled=True)
    sum_out = lax.psum_scatter(grad_out, "dp", scatter_dimension=0, axis_index_groups=sixteen, tiled=True)
    cells = grad_in.reshape(4, 4, 2, 96, D)
    first = [(cells[:, :, 0], "y", at_y, 0), (cells[:, :, 1], "z", at_z, 1)]
    pieces = near_pieces(first)

    gs_theirs = send(gs_theirs, CORE_SWAP).reshape(HALF, D)
    gg = gg_mine.reshape(HALF) + send(gg_theirs.reshape(HALF), CORE_SWAP)
    gg = jnp.pad(gg.reshape(BLOCKS, BLOCK), ((0, 0), (0, 8 * D - BLOCK))).reshape(BLOCKS, 8, D)
    gs_mine = gs_mine.reshape(HALF, D)
    pieces, gs_theirs, gs_mine = lax.optimization_barrier((pieces, gs_theirs, gs_mine))
    near = near_sends(first, pieces)

    def chip_block(b, mine, theirs):
        return jnp.concatenate([mine[b * BLOCK : (b + 1) * BLOCK] + theirs[b * BLOCK : (b + 1) * BLOCK], gg[b]])

    gs = [chip_block(0, gs_mine, gs_theirs)]
    gs_far = [send(gs[0], FAR_SWAP)]
    later = lax.optimization_barrier((gs_mine, gs_theirs, gs[0]))
    gs = gs + [chip_block(b, later[0], later[1]) for b in (1, 2)]

    def attend(b, sums):
        return attention_backward(
            b, core, gs[b], gs_far[b], hidden, cotangent, tokens_in, expert_ids, mixed, qkv, prob, window,
            consts, weights, sums,
        )

    act, gs[1], gs[2] = lax.optimization_barrier((act, gs[1], gs[2]))
    ep_theirs, ep_mine = experts_output(core, dest, chunks, act, meta, expert_out)
    ep_mine, ep_theirs, near = lax.optimization_barrier((ep_mine, ep_theirs, near))
    gs_far.append(send(after(gs[1], near[0]), FAR_SWAP))
    across = scatter_across(first, near)
    gs_far.append(send(after(gs[2], near[0]), FAR_SWAP))
    ep_theirs, gs_far[0] = lax.optimization_barrier((ep_theirs, gs_far[0]))
    ep_theirs = send(ep_theirs, CORE_SWAP)
    grad_0, *sums = attend(0, None)
    across, gs_far[1], grad_0, ep_theirs = lax.optimization_barrier((across, gs_far[1], grad_0, ep_theirs))
    halves = scatter_total(first, near, across)
    second = [(halves[0], "z", at_z), (halves[1], "y", at_y)]
    fold = [send(jnp.stack([quarter(v, at ^ 1, 0), quarter(v, at ^ 3, 0)]), PAIR[axis]) for v, axis, at in second]
    ep = (ep_mine + ep_theirs).reshape(HALF, D)
    ep = [ep[a:b] for a, b in zip(CUTS, CUTS[1:])]
    gs_far[1], halves, ep = lax.optimization_barrier((gs_far[1], halves, ep))
    ep_far = [send(ep[0], FAR_SWAP)]
    grad_1, *sums = attend(1, sums)
    fold, sum_out, gs_far[2], grad_1, ep_far[0] = lax.optimization_barrier((fold, sum_out, gs_far[2], grad_1, ep_far[0]))
    near_out = send(sum_out, NEAR_SWAP)
    kept = [quarter(v, at, 0) + got[0] for (v, axis, at), got in zip(second, fold)]
    over = [send(quarter(v, at ^ 2, 0) + got[1], TURN[axis][2]) for (v, axis, at), got in zip(second, fold)]
    near_out, over, gs_far[2] = lax.optimization_barrier((near_out, over, gs_far[2]))
    sum_out = gather(sum_out + near_out)
    sum_in = jnp.concatenate([v + got for v, got in zip(kept, over)])
    near_in = send(sum_in, NEAR_SWAP)
    ep_far.append(send(after(ep[1], sum_in), FAR_SWAP))
    gs_far[2], sum_in = lax.optimization_barrier((gs_far[2], sum_in))
    grad_2, *sums = attend(2, sums)
    near_in, grad_2, sums, ep_far[1] = lax.optimization_barrier((near_in, grad_2, sums, ep_far[1]))
    sum_in = gather(sum_in + near_in)
    ep_far.append(send(after(ep[2], ep_far[1]), FAR_SWAP))
    packed = pack_rest(shard, sums, in_bias, out_bias, lookup)
    (packed,) = scatter_sums([(packed, "y", at_y, 0)])
    (packed,) = scatter_sums([(packed, "z", at_z, 0)])
    packed, ep_far[2] = lax.optimization_barrier((packed.reshape(32, D), ep_far[2]))
    packed_near = send(packed, NEAR_SWAP)
    ep_far.append(send(after(ep[3], packed_near), FAR_SWAP))
    packed = packed + packed_near

    (packed,) = gather_rows([(packed, "z", at_z)])
    (packed,) = gather_rows([(packed, "y", at_y)])
    ep_far[3], packed = lax.optimization_barrier((ep_far[3], packed))

    block_out, input_grad = None, None
    for n, block in enumerate(slice(a, b) for a, b in zip(CUTS, CUTS[1:])):
        block_half = base[block] + gate[block] * (ep[n] + ep_far[n])
        block_out = assemble(core, PIECES[n], block.start, block_half, send(block_half, CORE_SWAP), LOW, block_out)
    for n, grad in enumerate((grad_0, grad_1, grad_2)):
        input_grad = assemble(core, BLOCK, n * BLOCK, grad, send(grad, CORE_SWAP), F32, input_grad)

    few = packed[D : D + 24]
    grad_table = few[16:24].reshape(-1)[: 169 * HEADS].reshape(169, HEADS)
    return (
        block_out,
        input_grad,
        few[0],
        few[1],
        packed[:288].reshape(3, 96, D).transpose(0, 2, 1),
        lax.dynamic_slice_in_dim(few[5:7], shard * 96, 96, 1),
        lax.dynamic_slice_in_dim(grad_table, shard * 3, 3, 1),
        packed[288:384],
        few[2],
        few[3],
        few[4],
        few[8:16].T,
        sum_in.reshape(EXPERTS, D, D),
        packed[408:416],
        sum_out.reshape(EXPERTS, D, D),
        packed[416:424],
    )


def solution(mesh):
    placed = (
        P("dp", None),
        P(),
        P(),
        P(None, None, "tensor"),
        P(None, "tensor"),
        P(None, "tensor"),
        P("tensor", None),
        P(),
        P(),
        P(),
        P(),
        P(None, None, "tensor"),
        P(None, "tensor"),
        P(None, "tensor", None),
        P(),
        P("dp", None),
        P("dp", None),
    )
    return jax.shard_map(
        shards,
        mesh=mesh,
        in_specs=placed,
        out_specs=(
            P("dp", None),
            P("dp", None),
            P(),
            P(),
            P(None, None, "tensor"),
            P(None, "tensor"),
            P(None, "tensor"),
            P("tensor", None),
            P(),
            P(),
            P(),
            P(),
            P(None, None, "tensor"),
            P(None, "tensor"),
            P(None, "tensor", None),
            P(),
        ),
        check_vma=False,
    )
```

```python
import functools
import math

import jax
import jax.numpy as jnp
import numpy as np
from jax import lax
from jax.experimental import pallas as pl
from jax.experimental.pallas import tpu as pltpu
from jax.sharding import PartitionSpec as P

F32 = jnp.float32
LOW = jnp.bfloat16
D = 384
HEADS = 12
EXPERTS = 8
SIDE = 14
WINDOW = 7
IMAGE = 196
HALF = 2352
BLOCK = 784
BLOCKS = 3
PADDED = 256
SLICE = 208
TILE = 168
TILES = 28
HALF_TILES = 14
GROUPS = 28
SORTED = 224
RUN = 7
STEPS_HALF = HALF_TILES // RUN
DISPATCH = 2 * STEPS_HALF
SLOTS = 960
CHUNK = 240
STORE = EXPERTS * SLOTS + 8
CLEAR = 248
PIECE = 336
CUTS = (0, 336, 1008, 1680, 2352)
MASK_FILL = -1e30
SCALE = 32 ** (-0.5)
VMEM = 60 * 1024 * 1024


def layout_consts():
    cell = np.arange(IMAGE)
    row = (cell // SIDE - WINDOW // 2) % SIDE
    col = (cell % SIDE - WINDOW // 2) % SIDE
    slot = (row // WINDOW * 2 + col // WINDOW) * 64 + row % WINDOW * WINDOW + col % WINDOW
    place = np.zeros((4, PADDED, SLICE), np.float32)
    for k in range(4):
        place[k, slot, 4 * k + cell] = 1.0
    part = lambda v: (v >= SIDE - WINDOW) * 1 + (v >= SIDE - WINDOW // 2) * 1
    label = np.full((PADDED,), -1)
    label[slot] = part(row) * 3 + part(col)
    label = label.reshape(4, 64)
    real = np.arange(64) < WINDOW * WINDOW
    meet = (label[:, :, None] == label[:, None, :]) | ~real[None, :, None]
    fill = np.where(meet & real[None, None, :], 0.0, MASK_FILL).astype(np.float32)
    fill = np.tile(fill, (1, 1, 4))
    spot = np.arange(49)
    entry = (spot[:, None] // 7 - spot[None, :] // 7 + 6) * 13 + spot[:, None] % 7 - spot[None, :] % 7 + 6
    lookup = np.zeros((64, 64, 169), np.float32)
    lookup[spot[:, None], spot[None, :], entry] = 1.0
    heads = (np.arange(256)[:, None] // 64 == np.arange(128)[None, :] // 32).astype(np.float32)
    segment = (np.arange(256)[:, None] // 64 == np.arange(256)[None, :] // 64).astype(np.float32)
    return place, fill, lookup.reshape(4096, 169), heads, segment


def nn(a, b):
    return lax.dot_general(a, b, (((1,), (0,)), ((), ())), preferred_element_type=F32)


def nt(a, b):
    return lax.dot_general(a, b, (((1,), (1,)), ((), ())), preferred_element_type=F32)


def tn(a, b):
    return lax.dot_general(a, b, (((0,), (0,)), ((), ())), preferred_element_type=F32)


def norm_parts(values):
    centre = values - jnp.mean(values, axis=-1, keepdims=True)
    inverse = lax.rsqrt(jnp.mean(centre * centre, axis=-1, keepdims=True) + 1e-5)
    return centre * inverse, inverse


def norm_back(upstream, unit, inverse, gain):
    scaled = upstream * gain
    return inverse * (
        scaled
        - jnp.mean(scaled, axis=-1, keepdims=True)
        - unit * jnp.mean(scaled * unit, axis=-1, keepdims=True)
    )


def column_sum(values):
    return jnp.sum(values, axis=0, keepdims=True)


def router_softmax(second, router):
    logits = nn(second, router)
    lane = lax.broadcasted_iota(jnp.int32, logits.shape, 1)
    logits = jnp.where(lane < EXPERTS, logits, MASK_FILL)
    power = jnp.exp(logits - jnp.max(logits, axis=-1, keepdims=True))
    return power / jnp.sum(power, axis=-1, keepdims=True), lane


def expand(part, heads):
    return jnp.concatenate([part] * 4, axis=0) * heads


def attention_kernel(
    core, x_ref, ids_ref, attn_gain, attn_shift, own, near, over, last, bqkv, bias, place, place_t, heads, segment,
    bproj, moe_gain, moe_shift, router, out_bias,
    hidden_ref, base_ref, second_ref, gate_ref, mixed_ref, qkv_ref, prob_ref, window_ref, wqkv_rows, wproj,
    low_scr, raster_scr, wqkv, power_scr,
):
    @pl.when(pl.program_id(0) == 0)
    def _():
        for j in range(4):
            found = last[:D, :]
            for step, shard in ((2, over), (1, near), (0, own)):
                found = jnp.where(core[1] == j ^ step, shard[:D, :], found)
            found = found.astype(LOW)
            for k in range(3):
                wqkv_rows[k * D + j * 96 : k * D + j * 96 + 96, :] = found[k * 96 : k * 96 + 96, :]
            wproj[j * 96 : j * 96 + 96, :] = found[288:, :]
        wqkv[...] = wqkv_rows[...].astype(F32).T.astype(LOW)

    x = x_ref[...].astype(F32)
    unit, _ = norm_parts(x)
    low_scr[...] = (unit * attn_gain[...] + attn_shift[...]).astype(LOW)
    raster_scr[...] = jnp.zeros_like(raster_scr)
    lane = lax.broadcasted_iota(jnp.int32, (64, 128), 1)
    left = lane < 64

    def project(k, carry):
        start = pl.multiple_of(k * 192, 64)
        rows = nn(place[k], low_scr[pl.ds(start, SLICE), :]).astype(LOW)
        qkv = (nn(rows, wqkv[...]) + bqkv[...]).astype(LOW)
        qkv_ref[pl.ds(pl.multiple_of(k * PADDED, PADDED), PADDED), :] = qkv
        return carry

    def scores_of(k, w, g):
        at = pl.ds(pl.multiple_of(k * PADDED + w * 64, 64), 64)
        q = qkv_ref[at, g * 128 : g * 128 + 128]
        kx = expand(qkv_ref[at, D + g * 128 : D + g * 128 + 128], heads[...])
        return nt(q, kx) * SCALE + bias[w * 3 + g]

    def finish(k):
        spot = pl.multiple_of(k * 768, 64)
        total = nn(power_scr[...], segment[...])
        prob_ref[pl.ds(spot, 768), :] = (power_scr[...].astype(F32) / total).astype(LOW)
        for w in range(4):
            at = pl.ds(pl.multiple_of(k * PADDED + w * 64, 64), 64)
            parts = []
            for g in range(3):
                vx = expand(qkv_ref[at, 2 * D + g * 128 : 2 * D + g * 128 + 128], heads[...])
                prob = prob_ref[pl.ds(pl.multiple_of(spot + (w * 3 + g) * 64, 64), 64), :]
                parts.append(nn(prob, vx).astype(LOW))
            window_ref[at, :] = jnp.concatenate(parts, axis=1)
        mixed = window_ref[pl.ds(pl.multiple_of(k * PADDED, PADDED), PADDED), :]
        raster_scr[pl.ds(pl.multiple_of(k * 192, 64), SLICE), :] += nn(place_t[k], mixed)
        return total

    def image(k, bounds):
        project(k, 0)
        for w in range(4):
            for g in range(3):
                power_scr[(w * 3 + g) * 64 : (w * 3 + g) * 64 + 64, :] = jnp.exp(scores_of(k, w, g)).astype(LOW)
        total = finish(k).reshape(96, 8, 256)
        return jnp.minimum(bounds[0], jnp.min(total, axis=0)), jnp.maximum(bounds[1], jnp.max(total, axis=0))

    def image_shifted(k, carry):
        for w in range(4):
            for g in range(3):
                scores = scores_of(k, w, g)
                power = []
                for c in range(2):
                    piece = scores[:, c * 128 : c * 128 + 128]
                    first = jnp.max(jnp.where(left, piece, 2 * MASK_FILL), axis=-1, keepdims=True)
                    other = jnp.max(jnp.where(left, 2 * MASK_FILL, piece), axis=-1, keepdims=True)
                    power.append(jnp.exp(piece - jnp.where(left, first, other)))
                power_scr[(w * 3 + g) * 64 : (w * 3 + g) * 64 + 64, :] = jnp.concatenate(power, axis=1).astype(LOW)
        finish(k)
        return carry

    least, most = lax.fori_loop(0, 4, image, (jnp.full((8, 256), 1.0, F32), jnp.full((8, 256), 1.0, F32)))
    safe = (jnp.min(least) > 1e-25) & (jnp.max(most) < 1e25)

    @pl.when(jnp.logical_not(safe))
    def _():
        raster_scr[...] = jnp.zeros_like(raster_scr)
        lax.fori_loop(0, 4, image_shifted, 0)

    mixed = raster_scr[...].astype(LOW)
    mixed_ref[...] = mixed
    hidden = x + (nn(mixed, wproj[...]) + bproj[...])
    hidden_ref[...] = hidden
    unit, _ = norm_parts(hidden)
    second = (unit * moe_gain[...] + moe_shift[...]).astype(LOW)
    second_ref[...] = second.astype(F32)
    probs, lanes = router_softmax(second, router[...])
    chosen = lanes == ids_ref[...]
    gate = jnp.sum(jnp.where(chosen, probs, 0.0), axis=-1, keepdims=True)
    gate_ref[...] = gate
    base_ref[...] = hidden + gate * nn(chosen.astype(F32).astype(LOW), out_bias[...])


def whole(shape):
    return pl.BlockSpec(shape, lambda *_: (0,) * len(shape))


def attention_forward(core, x, ids, shards, consts, weights, bias):
    place, place_t, heads, segment, _ = consts
    at_block = lambda width: pl.BlockSpec((BLOCK, width), lambda i, s: (s[0] * BLOCKS + i, 0))
    rows = lambda height, width: pl.BlockSpec((height, width), lambda i, s: (i, 0))
    fixed = [weights[n] for n in ("attn_gain", "attn_shift")] + list(shards) + [weights["bqkv"]]
    tail = [weights[n] for n in ("bproj", "moe_gain", "moe_shift", "router", "out_bias_pad")]
    operands = fixed + [bias, place, place_t, heads, segment] + tail
    return pl.pallas_call(
        attention_kernel,
        grid_spec=pltpu.PrefetchScalarGridSpec(
            num_scalar_prefetch=1,
            grid=(BLOCKS,),
            in_specs=[at_block(D), at_block(1)] + [whole(v.shape) for v in operands],
            out_specs=[
                rows(BLOCK, D),
                rows(BLOCK, D),
                rows(BLOCK, D),
                rows(BLOCK, 1),
                rows(BLOCK, D),
                rows(4 * PADDED, 3 * D),
                rows(48 * 64, 256),
                rows(4 * PADDED, D),
                whole((3 * D, D)),
                whole((D, D)),
            ],
            scratch_shapes=[
                pltpu.VMEM((BLOCK, D), LOW),
                pltpu.VMEM((BLOCK, D), F32),
                pltpu.VMEM((D, 3 * D), LOW),
                pltpu.VMEM((768, 256), LOW),
            ],
        ),
        out_shape=[
            jax.ShapeDtypeStruct((HALF, D), F32),
            jax.ShapeDtypeStruct((HALF, D), F32),
            jax.ShapeDtypeStruct((HALF, D), F32),
            jax.ShapeDtypeStruct((HALF, 1), F32),
            jax.ShapeDtypeStruct((HALF, D), LOW),
            jax.ShapeDtypeStruct((BLOCKS * 4 * PADDED, 3 * D), LOW),
            jax.ShapeDtypeStruct((BLOCKS * 48 * 64, 256), LOW),
            jax.ShapeDtypeStruct((BLOCKS * 4 * PADDED, D), LOW),
            jax.ShapeDtypeStruct((3 * D, D), LOW),
            jax.ShapeDtypeStruct((D, D), LOW),
        ],
        compiler_params=pltpu.CompilerParams(vmem_limit_bytes=VMEM),
        cost_estimate=pl.CostEstimate(flops=1_000_000, bytes_accessed=100_000, transcendentals=0),
        name="attention_forward",
    )(core, x, ids, *operands)


def gelu_parts(values):
    size = jnp.abs(values)
    decay = jnp.exp(-0.5 * values * values)
    t = 1.0 / (1.0 + (0.3275911 / math.sqrt(2.0)) * size)
    poly = t * (0.254829592 + t * (-0.284496736 + t * (1.421413741 + t * (-1.453152027 + t * 1.061405429))))
    half = 0.5 * poly * decay
    cdf = jnp.where(values >= 0.0, 1.0 - half, half)
    return values * cdf, cdf + values * decay * (1.0 / math.sqrt(2.0 * math.pi))


def experts_kernel(
    core, dest, chunks,
    own_ref, other_ref, g_ref, meta_ref, router_t, w_in, b_in, w_out,
    grad_in, grad_out, in_bias, out_bias, act_ref, gs_theirs, gg_theirs, gs_mine, gg_mine,
    store,
):
    step = pl.program_id(0)
    undo = DISPATCH + EXPERTS

    def first_tile(j, flip):
        half = jnp.where(j < STEPS_HALF, flip, 1 - flip)
        return half * HALF_TILES + j % STEPS_HALF * RUN

    @pl.when(step == 0)
    def _():
        def clear(j, carry):
            store[pl.ds(pl.multiple_of(j * CLEAR, 8), CLEAR), :] = jnp.zeros((CLEAR, 2 * D), F32)
            return carry

        lax.fori_loop(0, STORE // CLEAR, clear, 0)

    @pl.when(step < DISPATCH)
    def _():
        begin = first_tile(step, core[0])
        for r in range(RUN):
            second = jnp.where(step < STEPS_HALF, own_ref[r], other_ref[r]).astype(LOW)
            logits = nt(router_t[...], second)
            kind = lax.broadcasted_iota(jnp.int32, logits.shape, 0)
            logits = jnp.where(kind < EXPERTS, logits, MASK_FILL)
            power = jnp.exp(logits - jnp.max(logits, axis=0, keepdims=True))
            chosen = jnp.where(kind == meta_ref[r, 1:2, :], power, 0.0)
            gate = jnp.sum(chosen, axis=0, keepdims=True) / jnp.sum(power, axis=0, keepdims=True)
            high = gate.astype(LOW).astype(F32)
            spot = lax.broadcasted_iota(jnp.int32, (SORTED, TILE), 0)
            here = spot == meta_ref[r, 0:1, :]
            pick = jnp.where(here, 1.0, 0.0).astype(LOW)
            pick_high = jnp.where(here, high, 0.0).astype(LOW)
            pick_rest = jnp.where(here, gate - high, 0.0).astype(LOW)
            moved = jnp.concatenate([nn(pick, second), nn(pick_high, g_ref[r]) + nn(pick_rest, g_ref[r])], axis=1)
            for j in range(GROUPS):
                at = pl.multiple_of(dest[(begin + r) * GROUPS + j] * 8, 8)
                store[pl.ds(at, 8), :] = moved[j * 8 : j * 8 + 8, :]

    @pl.when((step >= DISPATCH) & (step < undo))
    def _():
        e = step - DISPATCH
        grad_in[...] = jnp.zeros_like(grad_in)
        grad_out[...] = jnp.zeros_like(grad_out)
        lane = lax.broadcasted_iota(jnp.int32, (CHUNK, 128), 1)

        def chunk(c, sums):
            at = pl.ds(pl.multiple_of(e * SLOTS + c * CHUNK, 16), CHUNK)
            buffer = store[at, :D].astype(LOW)
            grad = store[at, D:].astype(LOW)
            act, slope = gelu_parts(nn(buffer, w_in[0]) + b_in[pl.ds(e, 1), :].astype(F32))
            act = act.astype(LOW)
            act_ref[pl.ds(pl.multiple_of(c * CHUNK, 16), CHUNK), :] = act
            grad_act = nt(grad, w_out[0])
            gate_grad = jnp.sum(act.astype(F32) * grad_act, axis=-1, keepdims=True)
            high = gate_grad.astype(LOW).astype(F32)
            grad_pre = (grad_act * slope).astype(LOW)
            store[at, :D] = nt(grad_pre, w_in[0])
            store[at, D : D + 128] = jnp.where(lane == 0, high, gate_grad - high)
            grad_in[...] += tn(buffer, grad_pre)
            grad_out[...] += tn(act, grad)
            return sums[0] + column_sum(grad_pre.astype(F32)), sums[1] + column_sum(grad.astype(F32))

        zero = jnp.zeros((1, D), F32)
        sums = lax.fori_loop(0, chunks[e], chunk, (zero, zero))
        in_bias[pl.ds(e, 1), :] = sums[0]
        out_bias[pl.ds(e, 1), :] = sums[1]

    def collect(gs_ref, gg_ref):
        begin = first_tile(step - undo, 1 - core[0])
        ones = jnp.where(lax.broadcasted_iota(jnp.int32, (8, 128), 1) < 2, 1.0, 0.0).astype(LOW)
        for r in range(RUN):
            tile = (begin + r) * GROUPS
            rows = [store[pl.ds(pl.multiple_of(dest[tile + j] * 8, 8), 8), : D + 128] for j in range(GROUPS)]
            rows = jnp.concatenate(rows, axis=0).astype(LOW)
            spot = lax.broadcasted_iota(jnp.int32, (SORTED, TILE), 0)
            pick = jnp.where(spot == meta_ref[r, 0:1, :], 1.0, 0.0).astype(LOW)
            back = tn(pick, rows)
            gs_ref[r] = back[:, :D]
            gg_ref[r] = nt(ones, back[:, D:].astype(LOW))[0:1, :]

    @pl.when((step >= undo) & (step < undo + STEPS_HALF))
    def _():
        collect(gs_theirs, gg_theirs)

    @pl.when(step >= undo + STEPS_HALF)
    def _():
        collect(gs_mine, gg_mine)


def tile_blocks(begin, undo):
    def index(i, c, *_):
        back = i >= undo
        j = jnp.where(back, i - undo, jnp.clip(i - begin, 0, DISPATCH - 1))
        flip = jnp.where(back, 1 - c[0], c[0])
        half = jnp.where(j < STEPS_HALF, flip, 1 - flip)
        return half * STEPS_HALF + j % STEPS_HALF

    return index


def run_from(begin):
    return lambda i, *_: (jnp.clip(i - begin, 0, STEPS_HALF - 1), 0, 0)


def experts(core, dest, chunks, own, other, g, meta, router_t, w_in, b_in, w_out):
    undo = DISPATCH + EXPERTS
    tile = tile_blocks(0, undo)
    expert = lambda i, *_: (jnp.clip(i - DISPATCH, 0, EXPERTS - 1), 0, 0)
    flat = lambda i, *_: (jnp.clip(i - DISPATCH, 0, EXPERTS - 1), 0)
    out_half = lambda begin: [
        pl.BlockSpec((RUN, TILE, D), run_from(begin)),
        pl.BlockSpec((RUN, 1, TILE), run_from(begin)),
    ]
    half = [
        jax.ShapeDtypeStruct((HALF_TILES, TILE, D), F32),
        jax.ShapeDtypeStruct((HALF_TILES, 1, TILE), F32),
    ]
    return pl.pallas_call(
        experts_kernel,
        grid_spec=pltpu.PrefetchScalarGridSpec(
            num_scalar_prefetch=3,
            grid=(undo + DISPATCH,),
            in_specs=[
                pl.BlockSpec((RUN, TILE, D), run_from(0)),
                pl.BlockSpec((RUN, TILE, D), run_from(STEPS_HALF)),
                pl.BlockSpec((RUN, TILE, D), lambda i, *s: (tile(jnp.minimum(i, undo - 1), *s), 0, 0)),
                pl.BlockSpec((RUN, 2, TILE), lambda i, *s: (tile(i, *s), 0, 0)),
                whole((16, D)),
                pl.BlockSpec((1, D, D), expert),
                whole((EXPERTS, D)),
                pl.BlockSpec((1, D, D), expert),
            ],
            out_specs=[
                pl.BlockSpec((D, D), flat),
                pl.BlockSpec((D, D), flat),
                whole((EXPERTS, D)),
                whole((EXPERTS, D)),
                pl.BlockSpec((SLOTS, D), flat),
            ]
            + out_half(undo)
            + out_half(undo + STEPS_HALF),
            scratch_shapes=[pltpu.VMEM((STORE, 2 * D), F32)],
        ),
        out_shape=[
            jax.ShapeDtypeStruct((EXPERTS * D, D), F32),
            jax.ShapeDtypeStruct((EXPERTS * D, D), F32),
            jax.ShapeDtypeStruct((EXPERTS, D), F32),
            jax.ShapeDtypeStruct((EXPERTS, D), F32),
            jax.ShapeDtypeStruct((EXPERTS * SLOTS, D), LOW),
        ]
        + half
        + half,
        compiler_params=pltpu.CompilerParams(vmem_limit_bytes=VMEM),
        cost_estimate=pl.CostEstimate(flops=1_000_000, bytes_accessed=100_000, transcendentals=0),
        name="experts",
    )(core, dest, chunks, own, other, g, meta, router_t, w_in, b_in, w_out)


def output_kernel(core, dest, chunks, act_ref, meta_ref, w_out, ep_theirs, ep_mine, store):
    step = pl.program_id(0)

    @pl.when(step == 0)
    def _():
        store[EXPERTS * SLOTS :, :] = jnp.zeros((8, D), F32)

    @pl.when(step < EXPERTS)
    def _():
        def chunk(c, carry):
            rows = act_ref[pl.ds(pl.multiple_of(c * CHUNK, 16), CHUNK), :]
            store[pl.ds(pl.multiple_of(step * SLOTS + c * CHUNK, 16), CHUNK), :] = nn(rows, w_out[0])
            return carry

        lax.fori_loop(0, chunks[step], chunk, 0)

    def collect(ep_ref):
        j = step - EXPERTS
        half = jnp.where(j < STEPS_HALF, 1 - core[0], core[0])
        begin = half * HALF_TILES + j % STEPS_HALF * RUN
        for r in range(RUN):
            tile = (begin + r) * GROUPS
            rows = [store[pl.ds(pl.multiple_of(dest[tile + j] * 8, 8), 8), :] for j in range(GROUPS)]
            rows = jnp.concatenate(rows, axis=0).astype(LOW)
            spot = lax.broadcasted_iota(jnp.int32, (SORTED, TILE), 0)
            pick = jnp.where(spot == meta_ref[r, 0:1, :], 1.0, 0.0).astype(LOW)
            ep_ref[r] = tn(pick, rows)

    @pl.when((step >= EXPERTS) & (step < EXPERTS + STEPS_HALF))
    def _():
        collect(ep_theirs)

    @pl.when(step >= EXPERTS + STEPS_HALF)
    def _():
        collect(ep_mine)


def experts_output(core, dest, chunks, act, meta, w_out):
    tile = tile_blocks(-DISPATCH, EXPERTS)
    half = jax.ShapeDtypeStruct((HALF_TILES, TILE, D), F32)
    return pl.pallas_call(
        output_kernel,
        grid_spec=pltpu.PrefetchScalarGridSpec(
            num_scalar_prefetch=3,
            grid=(EXPERTS + DISPATCH,),
            in_specs=[
                pl.BlockSpec((SLOTS, D), lambda i, *_: (jnp.minimum(i, EXPERTS - 1), 0)),
                pl.BlockSpec((RUN, 2, TILE), lambda i, *s: (tile(i, *s), 0, 0)),
                pl.BlockSpec((1, D, D), lambda i, *_: (jnp.minimum(i, EXPERTS - 1), 0, 0)),
            ],
            out_specs=[
                pl.BlockSpec((RUN, TILE, D), run_from(EXPERTS)),
                pl.BlockSpec((RUN, TILE, D), run_from(EXPERTS + STEPS_HALF)),
            ],
            scratch_shapes=[pltpu.VMEM((STORE, D), F32)],
        ),
        out_shape=[half, half],
        compiler_params=pltpu.CompilerParams(vmem_limit_bytes=VMEM),
        cost_estimate=pl.CostEstimate(flops=1_000_000, bytes_accessed=100_000, transcendentals=0),
        name="experts_output",
    )(core, dest, chunks, act, meta, w_out)


def sort_plan(ids):
    named = ids.reshape(TILES, TILE)
    kinds = jnp.arange(EXPERTS, dtype=jnp.int32)
    chosen = (named[:, :, None] == kinds).astype(F32)
    before = jnp.asarray(np.tril(np.ones((TILE, TILE), np.float32), -1))
    rank = jnp.einsum("ij,tje->tie", before, chosen)
    count = jnp.sum(chosen, axis=1).astype(jnp.int32)
    groups = (count + 7) // 8
    ahead = jnp.asarray(np.tril(np.ones((EXPERTS, EXPERTS), np.int32), -1))
    first = jnp.sum(groups[:, None, :] * ahead[None], axis=-1)
    spot = jnp.sum(chosen * (rank + 8.0 * first[:, None, :].astype(F32)), axis=-1).astype(jnp.int32)
    earlier = jnp.asarray(np.tril(np.ones((TILES, TILES), np.int32), -1))
    offset = jnp.sum(earlier[:, :, None] * groups[None], axis=1)
    j = jnp.arange(GROUPS, dtype=jnp.int32)[None, :, None]
    inside = (j >= first[:, None, :]) & (j < (first + groups)[:, None, :])
    target = kinds * (SLOTS // 8) + offset[:, None, :] + j - first[:, None, :]
    dest = jnp.sum(jnp.where(inside, target, 0), axis=-1)
    dest = jnp.where(jnp.any(inside, axis=-1), dest, EXPERTS * SLOTS // 8).astype(jnp.int32)
    used = jnp.sum(groups, axis=0) * 8
    chunks = (used + CHUNK - 1) // CHUNK
    return spot, dest.reshape(-1), chunks.astype(jnp.int32)


def backward_kernel(
    block, core, gs_a, gs_b, hidden_ref, g_ref, ids_ref,
    attn_gain, attn_shift, place, place_t, heads, spread, moe_gain, moe_shift, router, out_bias_t,
    x_hbm, mixed_hbm, qkv_hbm, prob_hbm, window_hbm, wqkv_hbm, wproj_hbm,
    *refs,
):
    first, last = block == 0, block == BLOCKS - 1
    if first:
        before = ()
    else:
        before, refs = refs[:4], refs[4:]
    input_grad, totals, refs = refs[0], refs[1:5], refs[5:]
    turned = refs[0] if last else None
    raster_scr, mixed_scr, x_ref, mixed_ref, qkv_ref, prob_ref, window_ref, wqkv, wproj, sems = refs[-10:]
    grad_wqkv, grad_wproj, small, table = totals

    def part(ref, rows):
        return ref.at[pl.ds(block * rows, rows), :]

    here = pl.multiple_of((core[0] * BLOCKS + block) * BLOCK, 16)
    moves = [
        (wproj_hbm, wproj),
        (part(mixed_hbm, BLOCK), mixed_ref),
        (part(window_hbm, 4 * PADDED), window_ref),
        (part(qkv_hbm, 4 * PADDED), qkv_ref),
        (part(prob_hbm, 48 * 64), prob_ref),
        (x_hbm.at[pl.ds(here, BLOCK), :], x_ref),
        (wqkv_hbm, wqkv),
    ] + list(zip(before, totals))
    moves = [pltpu.make_async_copy(source, target, sems.at[n]) for n, (source, target) in enumerate(moves)]
    for move in moves[7:] + moves[:7]:
        move.start()
    if first:
        for total in totals:
            total[...] = jnp.zeros_like(total)
    g_low = g_ref[...]
    g = g_low.astype(F32)
    unit, inverse = norm_parts(hidden_ref[...])
    second = (unit * moe_gain[...] + moe_shift[...]).astype(LOW)
    probs, lanes = router_softmax(second, router[...])
    chosen = lanes == ids_ref[...]
    gate = jnp.sum(jnp.where(chosen, probs, 0.0), axis=-1, keepdims=True)
    with_bias = jnp.sum(jnp.where(chosen, nn(g_low, out_bias_t[...]), 0.0), axis=-1, keepdims=True)
    sums = gs_a[BLOCK:, :] + gs_b[BLOCK:, :]
    columns = []
    for piece in range(3):
        count = min(D, BLOCK - piece * D)
        same = lax.broadcasted_iota(jnp.int32, (count, D), 0) == lax.broadcasted_iota(jnp.int32, (count, D), 1)
        columns.append(jnp.sum(jnp.where(same, sums[piece : piece + 1, :], 0.0), axis=-1, keepdims=True))
    gated = jnp.concatenate(columns, axis=0)
    grad_logit = (gated + gate * with_bias) * (chosen.astype(F32) - probs)
    logit_high = grad_logit.astype(LOW)
    logit_rest = (grad_logit - logit_high.astype(F32)).astype(LOW)
    grad_router = tn(logit_high, second) + tn(logit_rest, second)
    grad_second = gs_a[:BLOCK, :] + gs_b[:BLOCK, :] + nt(logit_high, router[...]) + nt(logit_rest, router[...])
    for move in moves[7:]:
        move.wait()
    small[3:4, :] += column_sum(grad_second * unit)
    small[4:5, :] += column_sum(grad_second)
    small[8:16, :] += grad_router[:EXPERTS, :]
    grad_hidden = g + norm_back(grad_second, unit, inverse, moe_gain[...])
    grad_low = grad_hidden.astype(LOW)
    small[2:3, :] += column_sum(grad_low.astype(F32))
    for move in moves[:2]:
        move.wait()
    grad_wproj[...] += tn(mixed_ref[...], grad_low)
    mixed_scr[...] = nt(grad_low, wproj[...]).astype(LOW)
    raster_scr[...] = jnp.zeros_like(raster_scr)
    for move in moves[2:5]:
        move.wait()

    def image(k, carry):
        start = pl.multiple_of(k * 192, 64)
        grad_mixed = nn(place[k], mixed_scr[pl.ds(start, SLICE), :])
        dots = (grad_mixed * window_ref[pl.ds(pl.multiple_of(k * PADDED, PADDED), PADDED), :].astype(F32)).astype(LOW)
        grad_mixed = grad_mixed.astype(LOW)
        weighted = [nn(dots[:, c * 128 : c * 128 + 128], spread[...]) for c in range(3)]
        outs = []
        for w in range(4):
            row = slice(w * 64, w * 64 + 64)
            at = pl.ds(pl.multiple_of(k * PADDED + w * 64, 64), 64)
            parts = [[], [], []]
            for c in range(3):
                q = qkv_ref[at, c * 128 : c * 128 + 128]
                kx = expand(qkv_ref[at, D + c * 128 : D + c * 128 + 128], heads[...])
                vx = expand(qkv_ref[at, 2 * D + c * 128 : 2 * D + c * 128 + 128], heads[...])
                prob_low = prob_ref[pl.ds(pl.multiple_of(((k * 4 + w) * 3 + c) * 64, 64), 64), :]
                prob = prob_low.astype(F32)
                upstream = grad_mixed[row, c * 128 : c * 128 + 128]
                grad_prob = nt(upstream, vx)
                grad_score = prob * (grad_prob - weighted[c][row])
                table[c * 64 : c * 64 + 64, :] += grad_score
                low = (grad_score * SCALE).astype(LOW)
                parts[0].append(nn(low, kx).astype(LOW))
                for slot, left, right in ((1, low, q), (2, prob_low, upstream)):
                    full = tn(left, right)
                    kept = [full[h * 64 : h * 64 + 64] * heads[h * 64 : h * 64 + 64, :].astype(F32) for h in range(4)]
                    parts[slot].append((kept[0] + kept[1] + kept[2] + kept[3]).astype(LOW))
            outs.append(jnp.concatenate(parts[0] + parts[1] + parts[2], axis=1))
        grads = jnp.concatenate(outs, axis=0)
        raster_scr[pl.ds(start, SLICE), :] += nn(place_t[k], grads)
        return carry

    lax.fori_loop(0, 4, image, 0)
    if last:
        for c in range(3):
            turned[c * 256 : c * 256 + 256, :] = table[c * 64 : c * 64 + 64, :].T
    for move in moves[5:7]:
        move.wait()
    unit, inverse = norm_parts(x_ref[...].astype(F32))
    attn_low = (unit * attn_gain[...] + attn_shift[...]).astype(LOW)
    raster = raster_scr[...]
    small[5:6, :] += column_sum(raster[:, :D])
    small[6:7, :] += column_sum(raster[:, 2 * D :])
    grads = raster.astype(LOW)
    grad_wqkv[...] += tn(grads, attn_low)
    grad_in = nn(grads, wqkv[...])
    small[0:1, :] += column_sum(grad_in * unit)
    small[1:2, :] += column_sum(grad_in)
    input_grad[...] = grad_hidden + norm_back(grad_in, unit, inverse, attn_gain[...])


def attention_backward(block, core, gs_a, gs_b, hidden, g, x, ids, mixed, qkv, prob, window, consts, weights, sums):
    place, place_t, heads, _, spread = consts
    at_block = lambda width: pl.BlockSpec((BLOCK, width), lambda i, s: (s[0] * BLOCKS + block, 0))
    rows = lambda height, width: pl.BlockSpec((height, width), lambda i, s: (block, 0))
    fixed = [weights[n] for n in ("attn_gain", "attn_shift")] + [place, place_t, heads, spread]
    fixed = fixed + [weights[n] for n in ("moe_gain", "moe_shift", "router", "out_bias_t")]
    totals = [(3 * D, D), (D, D), (16, D), (192, 256)]
    before = [] if sums is None else list(sums)
    late = [x, mixed, qkv, prob, window, weights["wqkv"], weights["wproj"]] + before
    extra = [(768, 64)] if block == BLOCKS - 1 else []
    return pl.pallas_call(
        functools.partial(backward_kernel, block),
        grid_spec=pltpu.PrefetchScalarGridSpec(
            num_scalar_prefetch=1,
            grid=(1,),
            in_specs=[
                whole((BLOCK + 8, D)),
                whole((BLOCK + 8, D)),
                rows(BLOCK, D),
                at_block(D),
                at_block(1),
            ]
            + [whole(v.shape) for v in fixed]
            + [pl.BlockSpec(memory_space=pl.ANY) for v in late],
            out_specs=[whole((BLOCK, D))] + [whole(v) for v in totals + extra],
            scratch_shapes=[
                pltpu.VMEM((BLOCK, 3 * D), F32),
                pltpu.VMEM((BLOCK, D), LOW),
                pltpu.VMEM((BLOCK, D), LOW),
                pltpu.VMEM((BLOCK, D), LOW),
                pltpu.VMEM((4 * PADDED, 3 * D), LOW),
                pltpu.VMEM((48 * 64, 256), LOW),
                pltpu.VMEM((4 * PADDED, D), LOW),
                pltpu.VMEM((3 * D, D), LOW),
                pltpu.VMEM((D, D), LOW),
                pltpu.SemaphoreType.DMA((len(late),)),
            ],
        ),
        out_shape=[jax.ShapeDtypeStruct(v, F32) for v in [(BLOCK, D)] + totals + extra],
        compiler_params=pltpu.CompilerParams(vmem_limit_bytes=VMEM),
        cost_estimate=pl.CostEstimate(flops=1_000_000, bytes_accessed=100_000, transcendentals=0),
        name="attention_backward",
    )(core, gs_a, gs_b, hidden, g, ids, *fixed, *late)


def head_bias(table, lookup):
    rows = lax.dot_general(table.astype(LOW), jnp.asarray(lookup).astype(LOW), (((0,), (1,)), ((), ())), preferred_element_type=F32)
    return rows.reshape(32, D)


def position_bias(heads, fill):
    rows = heads.reshape(3, 4, 64, 64).transpose(0, 2, 1, 3).reshape(1, 3, 64, 256)
    return (rows + fill[:, None]).reshape(12, 64, 256)


def table_gradient(sums, lookup):
    rows = sums.reshape(HEADS, 4096)
    high = rows.astype(LOW)
    rest = (rows - high.astype(F32)).astype(LOW)
    turned = lookup.reshape(64, 64, 169).transpose(1, 0, 2).reshape(4096, 169)
    turned = jnp.asarray(turned).astype(LOW)
    found = nn(jnp.concatenate([high, rest]), turned)
    return (found[:HEADS] + found[HEADS:]).T


AXES = ("dp", "tensor")


def device_index(x, y, z, core):
    return (x % 2 * 16 + y % 4 * 4 + z % 4) * 4 + x // 2 % 2 * 2 + core


def pairs(move):
    places = [(x, y, z, c) for x in range(4) for y in range(4) for z in range(4) for c in range(2)]
    return [(device_index(*p), device_index(*move(*p))) for p in places]


CORE_SWAP = pairs(lambda x, y, z, c: (x, y, z, 1 - c))
FAR_SWAP = pairs(lambda x, y, z, c: ((x + 2) % 4, y, z, c))
NEAR_SWAP = pairs(lambda x, y, z, c: (x ^ 1, y, z, c))
TURN = {
    "y": [pairs(lambda x, y, z, c, s=s: (x, y + s, z, c)) for s in range(4)],
    "z": [pairs(lambda x, y, z, c, s=s: (x, y, z + s, c)) for s in range(4)],
}


PAIR = {
    "y": pairs(lambda x, y, z, c: (x, y ^ 1, z, c)),
    "z": pairs(lambda x, y, z, c: (x, y, z ^ 1, c)),
}


def send(values, table):
    return lax.ppermute(values, AXES, table)


def after(values, *others):
    return lax.optimization_barrier((values,) + others)[0]


def near_pieces(parts):
    return [quarter(v, at + shift, dim) for shift in (1, 3) for v, axis, at, dim in parts]


def near_sends(parts, pieces):
    tables = [TURN[axis][shift] for shift in (1, 3) for v, axis, at, dim in parts]
    return [send(piece, table) for piece, table in zip(pieces, tables)]


def quarter(values, index, dim):
    return lax.dynamic_index_in_dim(values, index % 4, dim, False)


def scatter_across(parts, near):
    return [
        send(after(quarter(v, at + 2, dim), near[n]), TURN[axis][2]) for n, (v, axis, at, dim) in enumerate(parts)
    ]


def scatter_total(parts, near, across):
    return [
        quarter(v, at, dim) + near[n] + near[n + len(parts)] + across[n]
        for n, (v, axis, at, dim) in enumerate(parts)
    ]


def scatter_sums(parts):
    near = [send(quarter(v, at + shift, dim), TURN[axis][shift]) for shift in (1, 3, 2) for v, axis, at, dim in parts]
    sums = scatter_total(parts, near, near[2 * len(parts) :])
    return [v.reshape((4, v.shape[0] // 4) + v.shape[1:]) for v in sums]


def gather_rows(parts):
    got = []
    for shift in (1, 3, 2):
        for n, (values, axis, place) in enumerate(parts):
            piece = after(values, got[n]) if shift == 2 and len(parts) > 1 else values
            got.append(send(piece, TURN[axis][shift]))
    fulls = []
    for n, (values, axis, place) in enumerate(parts):
        rows = values.shape[0]
        full = jnp.zeros((4 * rows,) + values.shape[1:], values.dtype)
        for shift, piece in ((0, values), (1, got[n]), (3, got[n + len(parts)]), (2, got[n + 2 * len(parts)])):
            full = lax.dynamic_update_slice_in_dim(full, piece, (place - shift) % 4 * rows, 0)
        fulls.append(full)
    return fulls


def assemble_kernel(core, mine, other, *refs):
    refs[-1][...] = jnp.where(pl.program_id(0) == 0, mine[...], other[...]).astype(refs[-1].dtype)


def assemble(core, size, first, mine, other, kind, before):
    def spot(i, j, c):
        return (jnp.where(i == 0, c[0], 1 - c[0]) * (HALF // size) + first // size + j, 0)

    kept = [] if before is None else [before]
    rows = pl.BlockSpec((size, D), lambda i, j, c: (j, 0))
    return pl.pallas_call(
        assemble_kernel,
        grid_spec=pltpu.PrefetchScalarGridSpec(
            num_scalar_prefetch=1,
            grid=(2, mine.shape[0] // size),
            in_specs=[rows, rows] + [pl.BlockSpec(memory_space=pl.ANY)] * len(kept),
            out_specs=pl.BlockSpec((size, D), spot),
        ),
        out_shape=jax.ShapeDtypeStruct((2 * HALF, D), kind),
        input_output_aliases={3: 0} if kept else {},
        cost_estimate=pl.CostEstimate(flops=1_000_000, bytes_accessed=100_000, transcendentals=0),
        name="assemble",
    )(core, mine, other, *kept)


def gather_shards(far, core, own):
    over = send(own, FAR_SWAP)
    near = send(own, CORE_SWAP)
    last = send(over, CORE_SWAP)
    pick = lambda flag, a, b: jnp.where(flag == 1, a, b)
    few = [v[D:] for v in (own, near, over, last)]
    low = (pick(core, few[1], few[0]), pick(core, few[0], few[1]))
    high = (pick(core, few[3], few[2]), pick(core, few[2], few[3]))
    few = [pick(far, high[i], low[i]) for i in (0, 1)] + [pick(far, low[i], high[i]) for i in (0, 1)]
    return (own, near, over, last), few


def gather_weights(far, core, qkv_weight, qv_bias, rel_table, proj_weight, lookup):
    own = jnp.concatenate(
        [
            qkv_weight.astype(F32).transpose(0, 2, 1).reshape(3 * 96, D),
            proj_weight.astype(F32),
            head_bias(rel_table, lookup),
            jnp.pad(qv_bias.astype(F32), ((0, 6), (0, D - 96))),
        ]
    )
    whole_shards, shards = gather_shards(far, core, own)
    heads = jnp.stack([v[:32].reshape(3, 64, 64) for v in shards]).reshape(HEADS, 64, 64)
    bias = jnp.concatenate([v[32:34, :96] for v in shards], axis=1)
    return whole_shards, bias, heads


def pack_rest(shard, sums, in_bias, out_bias, lookup):
    grad_wqkv, grad_wproj, small, _, pair_sums = sums
    rows = jnp.pad(table_gradient(pair_sums, lookup).reshape(-1), (0, 8 * D - 169 * HEADS)).reshape(8, D)
    by_shard = jnp.concatenate([grad_wqkv.reshape(3, 4, 96, D), grad_wproj.reshape(1, 4, 96, D)])

    def pack(index):
        return jnp.concatenate([lax.dynamic_index_in_dim(by_shard, index, 1, False).reshape(D, D), small, rows])

    packed = pack(shard) + send(pack(shard ^ 1), CORE_SWAP)
    return jnp.concatenate([packed, in_bias, out_bias, jnp.zeros((88, D), F32)]).reshape(4, 128, D)


def shards(
    tokens_in, attn_gain, attn_shift, qkv_weight, qv_bias, rel_table, proj_weight, proj_bias, moe_gain, moe_shift,
    router_weight, expert_in, expert_in_bias, expert_out, expert_out_bias, expert_ids, cotangent,
):
    group, shard = lax.axis_index("dp"), lax.axis_index("tensor")
    at_x, at_y, at_z = group // 16, group // 4 % 4, group % 4
    far, side = shard // 2, shard % 2
    core = side.astype(jnp.int32).reshape(1)
    place, fill, lookup, heads, segment = layout_consts()
    consts = (place, place.transpose(0, 2, 1), heads, segment, heads.T)
    consts = tuple(jnp.asarray(v).astype(LOW) for v in consts)
    wide = lambda v: v.astype(F32).reshape(1, -1)

    weight_shards, bias_qv, table = gather_weights(
        far, side, qkv_weight, qv_bias, rel_table, proj_weight, lookup
    )
    router = jnp.pad(router_weight, ((0, 0), (0, 128 - EXPERTS)))
    weights = dict(
        attn_gain=wide(attn_gain),
        attn_shift=wide(attn_shift),
        bqkv=jnp.concatenate([bias_qv[0:1], jnp.zeros((1, D), F32), bias_qv[1:2]], axis=1),
        bproj=wide(proj_bias),
        moe_gain=wide(moe_gain),
        moe_shift=wide(moe_shift),
        router=router,
        out_bias_pad=jnp.pad(expert_out_bias, ((0, 128 - EXPERTS), (0, 0))),
        out_bias_t=jnp.pad(expert_out_bias, ((0, 128 - EXPERTS), (0, 0))).T,
    )
    bias = position_bias(table, jnp.asarray(fill))
    spot, dest, chunks = sort_plan(expert_ids)
    meta = jnp.stack([spot, expert_ids.reshape(TILES, TILE)], axis=1)
    place_here = jnp.stack([side, shard]).astype(jnp.int32)
    hidden, base, second, gate, mixed, qkv, prob, window, weights["wqkv"], weights["wproj"] = attention_forward(
        place_here, tokens_in, expert_ids, weight_shards, consts, weights, bias
    )
    second = second.reshape(HALF_TILES, TILE, D)
    second_other = send(second, CORE_SWAP)
    gate, second_other = lax.optimization_barrier((gate.reshape(HALF), second_other))
    grad_in, grad_out, in_bias, out_bias, act, gs_theirs, gg_theirs, gs_mine, gg_mine = experts(
        core, dest, chunks, second, second_other, cotangent.reshape(TILES, TILE, D), meta,
        router[:, :16].T, expert_in, expert_in_bias.astype(F32), expert_out,
    )

    sixteen = [[i * 16 + j for j in range(16)] for i in range(2)]
    gather = lambda v: lax.all_gather(v, "dp", axis=0, axis_index_groups=sixteen, tiled=True)
    sum_out = lax.psum_scatter(grad_out, "dp", scatter_dimension=0, axis_index_groups=sixteen, tiled=True)
    cells = grad_in.reshape(4, 4, 2, 96, D)
    first = [(cells[:, :, 0], "y", at_y, 0), (cells[:, :, 1], "z", at_z, 1)]
    pieces = near_pieces(first)

    gs_theirs = send(gs_theirs, CORE_SWAP).reshape(HALF, D)
    gg = gg_mine.reshape(HALF) + send(gg_theirs.reshape(HALF), CORE_SWAP)
    gg = jnp.pad(gg.reshape(BLOCKS, BLOCK), ((0, 0), (0, 8 * D - BLOCK))).reshape(BLOCKS, 8, D)
    gs_mine = gs_mine.reshape(HALF, D)
    pieces, gs_theirs, gs_mine = lax.optimization_barrier((pieces, gs_theirs, gs_mine))
    near = near_sends(first, pieces)

    def chip_block(b, mine, theirs):
        return jnp.concatenate([mine[b * BLOCK : (b + 1) * BLOCK] + theirs[b * BLOCK : (b + 1) * BLOCK], gg[b]])

    gs = [chip_block(0, gs_mine, gs_theirs)]
    gs_far = [send(gs[0], FAR_SWAP)]
    later = lax.optimization_barrier((gs_mine, gs_theirs, gs[0]))
    gs = gs + [chip_block(b, later[0], later[1]) for b in (1, 2)]

    def attend(b, sums):
        return attention_backward(
            b, core, gs[b], gs_far[b], hidden, cotangent, tokens_in, expert_ids, mixed, qkv, prob, window,
            consts, weights, sums,
        )

    act, gs[1], gs[2] = lax.optimization_barrier((act, gs[1], gs[2]))
    ep_theirs, ep_mine = experts_output(core, dest, chunks, act, meta, expert_out)
    ep_mine, ep_theirs, near = lax.optimization_barrier((ep_mine, ep_theirs, near))
    gs_far.append(send(after(gs[1], near[0]), FAR_SWAP))
    across = scatter_across(first, near)
    gs_far.append(send(after(gs[2], near[0]), FAR_SWAP))
    ep_theirs, gs_far[0] = lax.optimization_barrier((ep_theirs, gs_far[0]))
    ep_theirs = send(ep_theirs, CORE_SWAP)
    grad_0, *sums = attend(0, None)
    across, gs_far[1], grad_0, ep_theirs = lax.optimization_barrier((across, gs_far[1], grad_0, ep_theirs))
    halves = scatter_total(first, near, across)
    second = [(halves[0], "z", at_z), (halves[1], "y", at_y)]
    fold = [send(jnp.stack([quarter(v, at ^ 1, 0), quarter(v, at ^ 3, 0)]), PAIR[axis]) for v, axis, at in second]
    ep = (ep_mine + ep_theirs).reshape(HALF, D)
    ep = [ep[a:b] for a, b in zip(CUTS, CUTS[1:])]
    gs_far[1], halves, ep = lax.optimization_barrier((gs_far[1], halves, ep))
    sum_out, halves = lax.optimization_barrier((sum_out, halves))
    near_out = send(sum_out, NEAR_SWAP)
    ep_far = [send(ep[0], FAR_SWAP)]
    gs_far[1], sum_out = lax.optimization_barrier((gs_far[1], sum_out))
    grad_1, *sums = attend(1, sums)
    fold, near_out, gs_far[2], grad_1, ep_far[0] = lax.optimization_barrier(
        (fold, near_out, gs_far[2], grad_1, ep_far[0])
    )
    sum_out = gather(sum_out + near_out)
    kept = [quarter(v, at, 0) + got[0] for (v, axis, at), got in zip(second, fold)]
    over = [send(quarter(v, at ^ 2, 0) + got[1], TURN[axis][2]) for (v, axis, at), got in zip(second, fold)]
    over, gs_far[2] = lax.optimization_barrier((over, gs_far[2]))
    sum_in = jnp.concatenate([v + got for v, got in zip(kept, over)])
    near_in = send(sum_in, NEAR_SWAP)
    ep_far.append(send(after(ep[1], sum_in), FAR_SWAP))
    gs_far[2], sum_in = lax.optimization_barrier((gs_far[2], sum_in))
    grad_2, *sums = attend(2, sums)
    near_in, grad_2, sums, ep_far[1] = lax.optimization_barrier((near_in, grad_2, sums, ep_far[1]))
    sum_in = gather(sum_in + near_in)
    ep_far.append(send(after(ep[2], ep_far[1]), FAR_SWAP))
    hold = lax.optimization_barrier

    def half_of(n):
        block = slice(CUTS[n], CUTS[n + 1])
        return base[block] + gate[block][:, None] * (ep[n] + ep_far[n])

    def put_grad(n, grad, other, whole_grad):
        return assemble(core, BLOCK, n * BLOCK, grad, other, F32, whole_grad)

    def put_out(n, half, other, whole_out):
        return assemble(core, PIECE, CUTS[n], half, other, LOW, whole_out)

    halves_out = [half_of(0), half_of(1)]
    packed = pack_rest(shard, sums, in_bias, out_bias, lookup)
    others = [send(v, CORE_SWAP) for v in (grad_0, grad_1, halves_out[0])]
    packed, others, halves_out = hold((packed, others, halves_out))
    (packed,) = scatter_sums([(packed, "y", at_y, 0)])
    input_grad = put_grad(1, grad_1, others[1], put_grad(0, grad_0, others[0], None))
    block_out = put_out(0, halves_out[0], others[2], None)
    packed, input_grad, block_out, half_1, grad_2 = hold((packed, input_grad, block_out, halves_out[1], grad_2))
    (packed,) = scatter_sums([(packed, "z", at_z, 0)])
    other_out = send(half_1, CORE_SWAP)
    packed, other_out, ep_far[2], grad_2 = hold((packed.reshape(32, D), other_out, ep_far[2], grad_2))
    packed_near = send(packed, NEAR_SWAP)
    other_grad = send(grad_2, CORE_SWAP)
    ep_far.append(send(after(ep[3], packed_near), FAR_SWAP))
    half_2 = half_of(2)
    packed, other_grad, half_2 = hold((packed + packed_near, other_grad, half_2))
    (packed,) = gather_rows([(packed, "z", at_z)])
    other_half = send(half_2, CORE_SWAP)
    packed, other_half = hold((packed, other_half))
    (packed,) = gather_rows([(packed, "y", at_y)])
    block_out = put_out(1, half_1, other_out, block_out)
    ep_far[3], packed, block_out, other_half, other_grad = hold((ep_far[3], packed, block_out, other_half, other_grad))
    half_3 = half_of(3)
    other_last = send(half_3, CORE_SWAP)
    input_grad = put_grad(2, grad_2, other_grad, input_grad)
    block_out = put_out(2, half_2, other_half, block_out)
    block_out = put_out(3, half_3, other_last, block_out)

    few = packed[D : D + 24]
    grad_table = few[16:24].reshape(-1)[: 169 * HEADS].reshape(169, HEADS)
    return (
        block_out,
        input_grad,
        few[0],
        few[1],
        packed[:288].reshape(3, 96, D).transpose(0, 2, 1),
        lax.dynamic_slice_in_dim(few[5:7], shard * 96, 96, 1),
        lax.dynamic_slice_in_dim(grad_table, shard * 3, 3, 1),
        packed[288:384],
        few[2],
        few[3],
        few[4],
        few[8:16].T,
        sum_in.reshape(EXPERTS, D, D),
        packed[408:416],
        sum_out.reshape(EXPERTS, D, D),
        packed[416:424],
    )


def solution(mesh):
    placed = (
        P("dp", None),
        P(),
        P(),
        P(None, None, "tensor"),
        P(None, "tensor"),
        P(None, "tensor"),
        P("tensor", None),
        P(),
        P(),
        P(),
        P(),
        P(None, None, "tensor"),
        P(None, "tensor"),
        P(None, "tensor", None),
        P(),
        P("dp", None),
        P("dp", None),
    )
    return jax.shard_map(
        shards,
        mesh=mesh,
        in_specs=placed,
        out_specs=(
            P("dp", None),
            P("dp", None),
            P(),
            P(),
            P(None, None, "tensor"),
            P(None, "tensor"),
            P(None, "tensor"),
            P("tensor", None),
            P(),
            P(),
            P(),
            P(),
            P(None, None, "tensor"),
            P(None, "tensor"),
            P(None, "tensor", None),
            P(),
        ),
        check_vma=False,
    )
```

```python
import functools
import math

import jax
import jax.numpy as jnp
import numpy as np
from jax import lax
from jax.experimental import pallas as pl
from jax.experimental.pallas import tpu as pltpu
from jax.sharding import PartitionSpec as P

F32 = jnp.float32
LOW = jnp.bfloat16
D = 384
HEADS = 12
EXPERTS = 8
SIDE = 14
WINDOW = 7
IMAGE = 196
HALF = 2352
BLOCK = 784
BLOCKS = 3
PADDED = 256
SLICE = 208
TILE = 168
TILES = 28
HALF_TILES = 14
GROUPS = 28
SORTED = 224
RUN = 7
STEPS_HALF = HALF_TILES // RUN
DISPATCH = 2 * STEPS_HALF
SLOTS = 960
CHUNK = 240
STORE = EXPERTS * SLOTS + 8
CLEAR = 248
CUTS = (0, 336, 1008, 1568, 2352)
MASK_FILL = -1e30
SCALE = 32 ** (-0.5)
VMEM = 60 * 1024 * 1024


def layout_consts():
    cell = np.arange(IMAGE)
    row = (cell // SIDE - WINDOW // 2) % SIDE
    col = (cell % SIDE - WINDOW // 2) % SIDE
    slot = (row // WINDOW * 2 + col // WINDOW) * 64 + row % WINDOW * WINDOW + col % WINDOW
    place = np.zeros((4, PADDED, SLICE), np.float32)
    for k in range(4):
        place[k, slot, 4 * k + cell] = 1.0
    part = lambda v: (v >= SIDE - WINDOW) * 1 + (v >= SIDE - WINDOW // 2) * 1
    label = np.full((PADDED,), -1)
    label[slot] = part(row) * 3 + part(col)
    label = label.reshape(4, 64)
    real = np.arange(64) < WINDOW * WINDOW
    meet = (label[:, :, None] == label[:, None, :]) | ~real[None, :, None]
    fill = np.where(meet & real[None, None, :], 0.0, MASK_FILL).astype(np.float32)
    fill = np.tile(fill, (1, 1, 4))
    spot = np.arange(49)
    entry = (spot[:, None] // 7 - spot[None, :] // 7 + 6) * 13 + spot[:, None] % 7 - spot[None, :] % 7 + 6
    lookup = np.zeros((64, 64, 169), np.float32)
    lookup[spot[:, None], spot[None, :], entry] = 1.0
    heads = (np.arange(256)[:, None] // 64 == np.arange(128)[None, :] // 32).astype(np.float32)
    segment = (np.arange(256)[:, None] // 64 == np.arange(256)[None, :] // 64).astype(np.float32)
    return place, fill, lookup.reshape(4096, 169), heads, segment


def nn(a, b):
    return lax.dot_general(a, b, (((1,), (0,)), ((), ())), preferred_element_type=F32)


def nt(a, b):
    return lax.dot_general(a, b, (((1,), (1,)), ((), ())), preferred_element_type=F32)


def tn(a, b):
    return lax.dot_general(a, b, (((0,), (0,)), ((), ())), preferred_element_type=F32)


def norm_parts(values):
    centre = values - jnp.mean(values, axis=-1, keepdims=True)
    inverse = lax.rsqrt(jnp.mean(centre * centre, axis=-1, keepdims=True) + 1e-5)
    return centre * inverse, inverse


def norm_back(upstream, unit, inverse, gain):
    scaled = upstream * gain
    return inverse * (
        scaled
        - jnp.mean(scaled, axis=-1, keepdims=True)
        - unit * jnp.mean(scaled * unit, axis=-1, keepdims=True)
    )


def column_sum(values):
    return jnp.sum(values, axis=0, keepdims=True)


def router_softmax(second, router):
    logits = nn(second, router)
    lane = lax.broadcasted_iota(jnp.int32, logits.shape, 1)
    logits = jnp.where(lane < EXPERTS, logits, MASK_FILL)
    power = jnp.exp(logits - jnp.max(logits, axis=-1, keepdims=True))
    return power / jnp.sum(power, axis=-1, keepdims=True), lane


def expand(part, heads):
    return jnp.concatenate([part] * 4, axis=0) * heads


def attention_kernel(
    core, x_ref, ids_ref, attn_gain, attn_shift, own, near, over, last, bqkv, bias, place, place_t, heads, segment,
    bproj, moe_gain, moe_shift, router, out_bias,
    hidden_ref, base_ref, second_ref, gate_ref, mixed_ref, qkv_ref, prob_ref, window_ref, wqkv_rows, wproj,
    low_scr, raster_scr, wqkv, power_scr,
):
    @pl.when(pl.program_id(0) == 0)
    def _():
        for j in range(4):
            found = last[:D, :]
            for step, shard in ((2, over), (1, near), (0, own)):
                found = jnp.where(core[1] == j ^ step, shard[:D, :], found)
            found = found.astype(LOW)
            for k in range(3):
                wqkv_rows[k * D + j * 96 : k * D + j * 96 + 96, :] = found[k * 96 : k * 96 + 96, :]
            wproj[j * 96 : j * 96 + 96, :] = found[288:, :]
        wqkv[...] = wqkv_rows[...].astype(F32).T.astype(LOW)

    x = x_ref[...].astype(F32)
    unit, _ = norm_parts(x)
    low_scr[...] = (unit * attn_gain[...] + attn_shift[...]).astype(LOW)
    raster_scr[...] = jnp.zeros_like(raster_scr)
    lane = lax.broadcasted_iota(jnp.int32, (64, 128), 1)
    left = lane < 64

    def project(k, carry):
        start = pl.multiple_of(k * 192, 64)
        rows = nn(place[k], low_scr[pl.ds(start, SLICE), :]).astype(LOW)
        qkv = (nn(rows, wqkv[...]) + bqkv[...]).astype(LOW)
        qkv_ref[pl.ds(pl.multiple_of(k * PADDED, PADDED), PADDED), :] = qkv
        return carry

    def scores_of(k, w, g):
        at = pl.ds(pl.multiple_of(k * PADDED + w * 64, 64), 64)
        q = qkv_ref[at, g * 128 : g * 128 + 128]
        kx = expand(qkv_ref[at, D + g * 128 : D + g * 128 + 128], heads[...])
        return nt(q, kx) * SCALE + bias[w * 3 + g]

    def finish(k):
        spot = pl.multiple_of(k * 768, 64)
        total = nn(power_scr[...], segment[...])
        prob_ref[pl.ds(spot, 768), :] = (power_scr[...].astype(F32) / total).astype(LOW)
        for w in range(4):
            at = pl.ds(pl.multiple_of(k * PADDED + w * 64, 64), 64)
            parts = []
            for g in range(3):
                vx = expand(qkv_ref[at, 2 * D + g * 128 : 2 * D + g * 128 + 128], heads[...])
                prob = prob_ref[pl.ds(pl.multiple_of(spot + (w * 3 + g) * 64, 64), 64), :]
                parts.append(nn(prob, vx).astype(LOW))
            window_ref[at, :] = jnp.concatenate(parts, axis=1)
        mixed = window_ref[pl.ds(pl.multiple_of(k * PADDED, PADDED), PADDED), :]
        raster_scr[pl.ds(pl.multiple_of(k * 192, 64), SLICE), :] += nn(place_t[k], mixed)
        return total

    def image(k, bounds):
        project(k, 0)
        for w in range(4):
            for g in range(3):
                power_scr[(w * 3 + g) * 64 : (w * 3 + g) * 64 + 64, :] = jnp.exp(scores_of(k, w, g)).astype(LOW)
        total = finish(k).reshape(96, 8, 256)
        return jnp.minimum(bounds[0], jnp.min(total, axis=0)), jnp.maximum(bounds[1], jnp.max(total, axis=0))

    def image_shifted(k, carry):
        for w in range(4):
            for g in range(3):
                scores = scores_of(k, w, g)
                power = []
                for c in range(2):
                    piece = scores[:, c * 128 : c * 128 + 128]
                    first = jnp.max(jnp.where(left, piece, 2 * MASK_FILL), axis=-1, keepdims=True)
                    other = jnp.max(jnp.where(left, 2 * MASK_FILL, piece), axis=-1, keepdims=True)
                    power.append(jnp.exp(piece - jnp.where(left, first, other)))
                power_scr[(w * 3 + g) * 64 : (w * 3 + g) * 64 + 64, :] = jnp.concatenate(power, axis=1).astype(LOW)
        finish(k)
        return carry

    least, most = lax.fori_loop(0, 4, image, (jnp.full((8, 256), 1.0, F32), jnp.full((8, 256), 1.0, F32)))
    safe = (jnp.min(least) > 1e-25) & (jnp.max(most) < 1e25)

    @pl.when(jnp.logical_not(safe))
    def _():
        raster_scr[...] = jnp.zeros_like(raster_scr)
        lax.fori_loop(0, 4, image_shifted, 0)

    mixed = raster_scr[...].astype(LOW)
    mixed_ref[...] = mixed
    hidden = x + (nn(mixed, wproj[...]) + bproj[...])
    hidden_ref[...] = hidden
    unit, _ = norm_parts(hidden)
    second = (unit * moe_gain[...] + moe_shift[...]).astype(LOW)
    second_ref[...] = second.astype(F32)
    probs, lanes = router_softmax(second, router[...])
    chosen = lanes == ids_ref[...]
    gate = jnp.sum(jnp.where(chosen, probs, 0.0), axis=-1, keepdims=True)
    gate_ref[...] = gate
    base_ref[...] = hidden + gate * nn(chosen.astype(F32).astype(LOW), out_bias[...])


def whole(shape):
    return pl.BlockSpec(shape, lambda *_: (0,) * len(shape))


def attention_forward(core, x, ids, shards, consts, weights, bias):
    place, place_t, heads, segment, _ = consts
    at_block = lambda width: pl.BlockSpec((BLOCK, width), lambda i, s: (s[0] * BLOCKS + i, 0))
    rows = lambda height, width: pl.BlockSpec((height, width), lambda i, s: (i, 0))
    fixed = [weights[n] for n in ("attn_gain", "attn_shift")] + list(shards) + [weights["bqkv"]]
    tail = [weights[n] for n in ("bproj", "moe_gain", "moe_shift", "router", "out_bias_pad")]
    operands = fixed + [bias, place, place_t, heads, segment] + tail
    return pl.pallas_call(
        attention_kernel,
        grid_spec=pltpu.PrefetchScalarGridSpec(
            num_scalar_prefetch=1,
            grid=(BLOCKS,),
            in_specs=[at_block(D), at_block(1)] + [whole(v.shape) for v in operands],
            out_specs=[
                rows(BLOCK, D),
                rows(BLOCK, D),
                rows(BLOCK, D),
                rows(BLOCK, 1),
                rows(BLOCK, D),
                rows(4 * PADDED, 3 * D),
                rows(48 * 64, 256),
                rows(4 * PADDED, D),
                whole((3 * D, D)),
                whole((D, D)),
            ],
            scratch_shapes=[
                pltpu.VMEM((BLOCK, D), LOW),
                pltpu.VMEM((BLOCK, D), F32),
                pltpu.VMEM((D, 3 * D), LOW),
                pltpu.VMEM((768, 256), LOW),
            ],
        ),
        out_shape=[
            jax.ShapeDtypeStruct((HALF, D), F32),
            jax.ShapeDtypeStruct((HALF, D), F32),
            jax.ShapeDtypeStruct((HALF, D), F32),
            jax.ShapeDtypeStruct((HALF, 1), F32),
            jax.ShapeDtypeStruct((HALF, D), LOW),
            jax.ShapeDtypeStruct((BLOCKS * 4 * PADDED, 3 * D), LOW),
            jax.ShapeDtypeStruct((BLOCKS * 48 * 64, 256), LOW),
            jax.ShapeDtypeStruct((BLOCKS * 4 * PADDED, D), LOW),
            jax.ShapeDtypeStruct((3 * D, D), LOW),
            jax.ShapeDtypeStruct((D, D), LOW),
        ],
        compiler_params=pltpu.CompilerParams(vmem_limit_bytes=VMEM),
        cost_estimate=pl.CostEstimate(flops=1_000_000, bytes_accessed=100_000, transcendentals=0),
        name="attention_forward",
    )(core, x, ids, *operands)


def gelu_parts(values):
    size = jnp.abs(values)
    decay = jnp.exp(-0.5 * values * values)
    t = 1.0 / (1.0 + (0.3275911 / math.sqrt(2.0)) * size)
    poly = t * (0.254829592 + t * (-0.284496736 + t * (1.421413741 + t * (-1.453152027 + t * 1.061405429))))
    half = 0.5 * poly * decay
    cdf = jnp.where(values >= 0.0, 1.0 - half, half)
    return values * cdf, cdf + values * decay * (1.0 / math.sqrt(2.0 * math.pi))


def experts_kernel(
    core, dest, chunks,
    own_ref, other_ref, g_ref, meta_ref, router_t, w_in, b_in, w_out,
    grad_in, grad_out, in_bias, out_bias, act_ref, gs_theirs, gg_theirs, gs_mine, gg_mine,
    store,
):
    step = pl.program_id(0)
    undo = DISPATCH + EXPERTS

    def first_tile(j, flip):
        half = jnp.where(j < STEPS_HALF, flip, 1 - flip)
        return half * HALF_TILES + j % STEPS_HALF * RUN

    @pl.when(step == 0)
    def _():
        def clear(j, carry):
            store[pl.ds(pl.multiple_of(j * CLEAR, 8), CLEAR), :] = jnp.zeros((CLEAR, 2 * D), F32)
            return carry

        lax.fori_loop(0, STORE // CLEAR, clear, 0)

    @pl.when(step < DISPATCH)
    def _():
        begin = first_tile(step, core[0])
        for r in range(RUN):
            second = jnp.where(step < STEPS_HALF, own_ref[r], other_ref[r]).astype(LOW)
            logits = nt(router_t[...], second)
            kind = lax.broadcasted_iota(jnp.int32, logits.shape, 0)
            logits = jnp.where(kind < EXPERTS, logits, MASK_FILL)
            power = jnp.exp(logits - jnp.max(logits, axis=0, keepdims=True))
            chosen = jnp.where(kind == meta_ref[r, 1:2, :], power, 0.0)
            gate = jnp.sum(chosen, axis=0, keepdims=True) / jnp.sum(power, axis=0, keepdims=True)
            high = gate.astype(LOW).astype(F32)
            spot = lax.broadcasted_iota(jnp.int32, (SORTED, TILE), 0)
            here = spot == meta_ref[r, 0:1, :]
            pick = jnp.where(here, 1.0, 0.0).astype(LOW)
            pick_high = jnp.where(here, high, 0.0).astype(LOW)
            pick_rest = jnp.where(here, gate - high, 0.0).astype(LOW)
            moved = jnp.concatenate([nn(pick, second), nn(pick_high, g_ref[r]) + nn(pick_rest, g_ref[r])], axis=1)
            for j in range(GROUPS):
                at = pl.multiple_of(dest[(begin + r) * GROUPS + j] * 8, 8)
                store[pl.ds(at, 8), :] = moved[j * 8 : j * 8 + 8, :]

    @pl.when((step >= DISPATCH) & (step < undo))
    def _():
        e = step - DISPATCH
        grad_in[...] = jnp.zeros_like(grad_in)
        grad_out[...] = jnp.zeros_like(grad_out)
        lane = lax.broadcasted_iota(jnp.int32, (CHUNK, 128), 1)

        def chunk(c, sums):
            at = pl.ds(pl.multiple_of(e * SLOTS + c * CHUNK, 16), CHUNK)
            buffer = store[at, :D].astype(LOW)
            grad = store[at, D:].astype(LOW)
            act, slope = gelu_parts(nn(buffer, w_in[0]) + b_in[pl.ds(e, 1), :].astype(F32))
            act = act.astype(LOW)
            act_ref[pl.ds(pl.multiple_of(c * CHUNK, 16), CHUNK), :] = act
            grad_act = nt(grad, w_out[0])
            gate_grad = jnp.sum(act.astype(F32) * grad_act, axis=-1, keepdims=True)
            high = gate_grad.astype(LOW).astype(F32)
            grad_pre = (grad_act * slope).astype(LOW)
            store[at, :D] = nt(grad_pre, w_in[0])
            store[at, D : D + 128] = jnp.where(lane == 0, high, gate_grad - high)
            grad_in[...] += tn(buffer, grad_pre)
            grad_out[...] += tn(act, grad)
            return sums[0] + column_sum(grad_pre.astype(F32)), sums[1] + column_sum(grad.astype(F32))

        zero = jnp.zeros((1, D), F32)
        sums = lax.fori_loop(0, chunks[e], chunk, (zero, zero))
        in_bias[pl.ds(e, 1), :] = sums[0]
        out_bias[pl.ds(e, 1), :] = sums[1]

    def collect(gs_ref, gg_ref):
        begin = first_tile(step - undo, 1 - core[0])
        ones = jnp.where(lax.broadcasted_iota(jnp.int32, (8, 128), 1) < 2, 1.0, 0.0).astype(LOW)
        for r in range(RUN):
            tile = (begin + r) * GROUPS
            rows = [store[pl.ds(pl.multiple_of(dest[tile + j] * 8, 8), 8), : D + 128] for j in range(GROUPS)]
            rows = jnp.concatenate(rows, axis=0).astype(LOW)
            spot = lax.broadcasted_iota(jnp.int32, (SORTED, TILE), 0)
            pick = jnp.where(spot == meta_ref[r, 0:1, :], 1.0, 0.0).astype(LOW)
            back = tn(pick, rows)
            gs_ref[r] = back[:, :D]
            gg_ref[r] = nt(ones, back[:, D:].astype(LOW))[0:1, :]

    @pl.when((step >= undo) & (step < undo + STEPS_HALF))
    def _():
        collect(gs_theirs, gg_theirs)

    @pl.when(step >= undo + STEPS_HALF)
    def _():
        collect(gs_mine, gg_mine)


def tile_blocks(begin, undo):
    def index(i, c, *_):
        back = i >= undo
        j = jnp.where(back, i - undo, jnp.clip(i - begin, 0, DISPATCH - 1))
        flip = jnp.where(back, 1 - c[0], c[0])
        half = jnp.where(j < STEPS_HALF, flip, 1 - flip)
        return half * STEPS_HALF + j % STEPS_HALF

    return index


def run_from(begin):
    return lambda i, *_: (jnp.clip(i - begin, 0, STEPS_HALF - 1), 0, 0)


def experts(core, dest, chunks, own, other, g, meta, router_t, w_in, b_in, w_out):
    undo = DISPATCH + EXPERTS
    tile = tile_blocks(0, undo)
    expert = lambda i, *_: (jnp.clip(i - DISPATCH, 0, EXPERTS - 1), 0, 0)
    flat = lambda i, *_: (jnp.clip(i - DISPATCH, 0, EXPERTS - 1), 0)
    out_half = lambda begin: [
        pl.BlockSpec((RUN, TILE, D), run_from(begin)),
        pl.BlockSpec((RUN, 1, TILE), run_from(begin)),
    ]
    half = [
        jax.ShapeDtypeStruct((HALF_TILES, TILE, D), F32),
        jax.ShapeDtypeStruct((HALF_TILES, 1, TILE), F32),
    ]
    return pl.pallas_call(
        experts_kernel,
        grid_spec=pltpu.PrefetchScalarGridSpec(
            num_scalar_prefetch=3,
            grid=(undo + DISPATCH,),
            in_specs=[
                pl.BlockSpec((RUN, TILE, D), run_from(0)),
                pl.BlockSpec((RUN, TILE, D), run_from(STEPS_HALF)),
                pl.BlockSpec((RUN, TILE, D), lambda i, *s: (tile(jnp.minimum(i, undo - 1), *s), 0, 0)),
                pl.BlockSpec((RUN, 2, TILE), lambda i, *s: (tile(i, *s), 0, 0)),
                whole((16, D)),
                pl.BlockSpec((1, D, D), expert),
                whole((EXPERTS, D)),
                pl.BlockSpec((1, D, D), expert),
            ],
            out_specs=[
                pl.BlockSpec((D, D), flat),
                pl.BlockSpec((D, D), flat),
                whole((EXPERTS, D)),
                whole((EXPERTS, D)),
                pl.BlockSpec((SLOTS, D), flat),
            ]
            + out_half(undo)
            + out_half(undo + STEPS_HALF),
            scratch_shapes=[pltpu.VMEM((STORE, 2 * D), F32)],
        ),
        out_shape=[
            jax.ShapeDtypeStruct((EXPERTS * D, D), F32),
            jax.ShapeDtypeStruct((EXPERTS * D, D), F32),
            jax.ShapeDtypeStruct((EXPERTS, D), F32),
            jax.ShapeDtypeStruct((EXPERTS, D), F32),
            jax.ShapeDtypeStruct((EXPERTS * SLOTS, D), LOW),
        ]
        + half
        + half,
        compiler_params=pltpu.CompilerParams(vmem_limit_bytes=VMEM),
        cost_estimate=pl.CostEstimate(flops=1_000_000, bytes_accessed=100_000, transcendentals=0),
        name="experts",
    )(core, dest, chunks, own, other, g, meta, router_t, w_in, b_in, w_out)


def output_kernel(core, dest, chunks, act_ref, meta_ref, w_out, ep_theirs, ep_mine, store):
    step = pl.program_id(0)

    @pl.when(step == 0)
    def _():
        store[EXPERTS * SLOTS :, :] = jnp.zeros((8, D), F32)

    @pl.when(step < EXPERTS)
    def _():
        def chunk(c, carry):
            rows = act_ref[pl.ds(pl.multiple_of(c * CHUNK, 16), CHUNK), :]
            store[pl.ds(pl.multiple_of(step * SLOTS + c * CHUNK, 16), CHUNK), :] = nn(rows, w_out[0])
            return carry

        lax.fori_loop(0, chunks[step], chunk, 0)

    def collect(ep_ref):
        j = step - EXPERTS
        half = jnp.where(j < STEPS_HALF, 1 - core[0], core[0])
        begin = half * HALF_TILES + j % STEPS_HALF * RUN
        for r in range(RUN):
            tile = (begin + r) * GROUPS
            rows = [store[pl.ds(pl.multiple_of(dest[tile + j] * 8, 8), 8), :] for j in range(GROUPS)]
            rows = jnp.concatenate(rows, axis=0).astype(LOW)
            spot = lax.broadcasted_iota(jnp.int32, (SORTED, TILE), 0)
            pick = jnp.where(spot == meta_ref[r, 0:1, :], 1.0, 0.0).astype(LOW)
            ep_ref[r] = tn(pick, rows)

    @pl.when((step >= EXPERTS) & (step < EXPERTS + STEPS_HALF))
    def _():
        collect(ep_theirs)

    @pl.when(step >= EXPERTS + STEPS_HALF)
    def _():
        collect(ep_mine)


def experts_output(core, dest, chunks, act, meta, w_out):
    tile = tile_blocks(-DISPATCH, EXPERTS)
    half = jax.ShapeDtypeStruct((HALF_TILES, TILE, D), F32)
    return pl.pallas_call(
        output_kernel,
        grid_spec=pltpu.PrefetchScalarGridSpec(
            num_scalar_prefetch=3,
            grid=(EXPERTS + DISPATCH,),
            in_specs=[
                pl.BlockSpec((SLOTS, D), lambda i, *_: (jnp.minimum(i, EXPERTS - 1), 0)),
                pl.BlockSpec((RUN, 2, TILE), lambda i, *s: (tile(i, *s), 0, 0)),
                pl.BlockSpec((1, D, D), lambda i, *_: (jnp.minimum(i, EXPERTS - 1), 0, 0)),
            ],
            out_specs=[
                pl.BlockSpec((RUN, TILE, D), run_from(EXPERTS)),
                pl.BlockSpec((RUN, TILE, D), run_from(EXPERTS + STEPS_HALF)),
            ],
            scratch_shapes=[pltpu.VMEM((STORE, D), F32)],
        ),
        out_shape=[half, half],
        compiler_params=pltpu.CompilerParams(vmem_limit_bytes=VMEM),
        cost_estimate=pl.CostEstimate(flops=1_000_000, bytes_accessed=100_000, transcendentals=0),
        name="experts_output",
    )(core, dest, chunks, act, meta, w_out)


def sort_plan(ids):
    named = ids.reshape(TILES, TILE)
    kinds = jnp.arange(EXPERTS, dtype=jnp.int32)
    chosen = (named[:, :, None] == kinds).astype(F32)
    before = jnp.asarray(np.tril(np.ones((TILE, TILE), np.float32), -1))
    rank = jnp.einsum("ij,tje->tie", before, chosen)
    count = jnp.sum(chosen, axis=1).astype(jnp.int32)
    groups = (count + 7) // 8
    ahead = jnp.asarray(np.tril(np.ones((EXPERTS, EXPERTS), np.int32), -1))
    first = jnp.sum(groups[:, None, :] * ahead[None], axis=-1)
    spot = jnp.sum(chosen * (rank + 8.0 * first[:, None, :].astype(F32)), axis=-1).astype(jnp.int32)
    earlier = jnp.asarray(np.tril(np.ones((TILES, TILES), np.int32), -1))
    offset = jnp.sum(earlier[:, :, None] * groups[None], axis=1)
    j = jnp.arange(GROUPS, dtype=jnp.int32)[None, :, None]
    inside = (j >= first[:, None, :]) & (j < (first + groups)[:, None, :])
    target = kinds * (SLOTS // 8) + offset[:, None, :] + j - first[:, None, :]
    dest = jnp.sum(jnp.where(inside, target, 0), axis=-1)
    dest = jnp.where(jnp.any(inside, axis=-1), dest, EXPERTS * SLOTS // 8).astype(jnp.int32)
    used = jnp.sum(groups, axis=0) * 8
    chunks = (used + CHUNK - 1) // CHUNK
    return spot, dest.reshape(-1), chunks.astype(jnp.int32)


def backward_kernel(
    block, core, gs_a, gs_b, hidden_ref, g_ref, ids_ref,
    attn_gain, attn_shift, place, place_t, heads, spread, moe_gain, moe_shift, router, out_bias_t,
    x_hbm, mixed_hbm, qkv_hbm, prob_hbm, window_hbm, wqkv_hbm, wproj_hbm,
    *refs,
):
    first, last = block == 0, block == BLOCKS - 1
    if first:
        before = ()
    else:
        before, refs = refs[:4], refs[4:]
    input_grad, totals, refs = refs[0], refs[1:5], refs[5:]
    turned = refs[0] if last else None
    raster_scr, mixed_scr, x_ref, mixed_ref, qkv_ref, prob_ref, window_ref, wqkv, wproj, sems = refs[-10:]
    grad_wqkv, grad_wproj, small, table = totals

    def part(ref, rows):
        return ref.at[pl.ds(block * rows, rows), :]

    here = pl.multiple_of((core[0] * BLOCKS + block) * BLOCK, 16)
    moves = [
        (wproj_hbm, wproj),
        (part(mixed_hbm, BLOCK), mixed_ref),
        (part(window_hbm, 4 * PADDED), window_ref),
        (part(qkv_hbm, 4 * PADDED), qkv_ref),
        (part(prob_hbm, 48 * 64), prob_ref),
        (x_hbm.at[pl.ds(here, BLOCK), :], x_ref),
        (wqkv_hbm, wqkv),
    ] + list(zip(before, totals))
    moves = [pltpu.make_async_copy(source, target, sems.at[n]) for n, (source, target) in enumerate(moves)]
    for move in moves[7:] + moves[:7]:
        move.start()
    if first:
        for total in totals:
            total[...] = jnp.zeros_like(total)
    g_low = g_ref[...]
    g = g_low.astype(F32)
    unit, inverse = norm_parts(hidden_ref[...])
    second = (unit * moe_gain[...] + moe_shift[...]).astype(LOW)
    probs, lanes = router_softmax(second, router[...])
    chosen = lanes == ids_ref[...]
    gate = jnp.sum(jnp.where(chosen, probs, 0.0), axis=-1, keepdims=True)
    with_bias = jnp.sum(jnp.where(chosen, nn(g_low, out_bias_t[...]), 0.0), axis=-1, keepdims=True)
    sums = gs_a[BLOCK:, :] + gs_b[BLOCK:, :]
    columns = []
    for piece in range(3):
        count = min(D, BLOCK - piece * D)
        same = lax.broadcasted_iota(jnp.int32, (count, D), 0) == lax.broadcasted_iota(jnp.int32, (count, D), 1)
        columns.append(jnp.sum(jnp.where(same, sums[piece : piece + 1, :], 0.0), axis=-1, keepdims=True))
    gated = jnp.concatenate(columns, axis=0)
    grad_logit = (gated + gate * with_bias) * (chosen.astype(F32) - probs)
    logit_high = grad_logit.astype(LOW)
    logit_rest = (grad_logit - logit_high.astype(F32)).astype(LOW)
    grad_router = tn(logit_high, second) + tn(logit_rest, second)
    grad_second = gs_a[:BLOCK, :] + gs_b[:BLOCK, :] + nt(logit_high, router[...]) + nt(logit_rest, router[...])
    for move in moves[7:]:
        move.wait()
    small[3:4, :] += column_sum(grad_second * unit)
    small[4:5, :] += column_sum(grad_second)
    small[8:16, :] += grad_router[:EXPERTS, :]
    grad_hidden = g + norm_back(grad_second, unit, inverse, moe_gain[...])
    grad_low = grad_hidden.astype(LOW)
    small[2:3, :] += column_sum(grad_low.astype(F32))
    for move in moves[:2]:
        move.wait()
    grad_wproj[...] += tn(mixed_ref[...], grad_low)
    mixed_scr[...] = nt(grad_low, wproj[...]).astype(LOW)
    raster_scr[...] = jnp.zeros_like(raster_scr)
    for move in moves[2:5]:
        move.wait()

    def image(k, carry):
        start = pl.multiple_of(k * 192, 64)
        grad_mixed = nn(place[k], mixed_scr[pl.ds(start, SLICE), :])
        dots = (grad_mixed * window_ref[pl.ds(pl.multiple_of(k * PADDED, PADDED), PADDED), :].astype(F32)).astype(LOW)
        grad_mixed = grad_mixed.astype(LOW)
        weighted = [nn(dots[:, c * 128 : c * 128 + 128], spread[...]) for c in range(3)]
        outs = []
        for w in range(4):
            row = slice(w * 64, w * 64 + 64)
            at = pl.ds(pl.multiple_of(k * PADDED + w * 64, 64), 64)
            parts = [[], [], []]
            for c in range(3):
                q = qkv_ref[at, c * 128 : c * 128 + 128]
                kx = expand(qkv_ref[at, D + c * 128 : D + c * 128 + 128], heads[...])
                vx = expand(qkv_ref[at, 2 * D + c * 128 : 2 * D + c * 128 + 128], heads[...])
                prob_low = prob_ref[pl.ds(pl.multiple_of(((k * 4 + w) * 3 + c) * 64, 64), 64), :]
                prob = prob_low.astype(F32)
                upstream = grad_mixed[row, c * 128 : c * 128 + 128]
                grad_prob = nt(upstream, vx)
                grad_score = prob * (grad_prob - weighted[c][row])
                table[c * 64 : c * 64 + 64, :] += grad_score
                low = (grad_score * SCALE).astype(LOW)
                parts[0].append(nn(low, kx).astype(LOW))
                for slot, left, right in ((1, low, q), (2, prob_low, upstream)):
                    full = tn(left, right)
                    kept = [full[h * 64 : h * 64 + 64] * heads[h * 64 : h * 64 + 64, :].astype(F32) for h in range(4)]
                    parts[slot].append((kept[0] + kept[1] + kept[2] + kept[3]).astype(LOW))
            outs.append(jnp.concatenate(parts[0] + parts[1] + parts[2], axis=1))
        grads = jnp.concatenate(outs, axis=0)
        raster_scr[pl.ds(start, SLICE), :] += nn(place_t[k], grads)
        return carry

    lax.fori_loop(0, 4, image, 0)
    if last:
        for c in range(3):
            turned[c * 256 : c * 256 + 256, :] = table[c * 64 : c * 64 + 64, :].T
    for move in moves[5:7]:
        move.wait()
    unit, inverse = norm_parts(x_ref[...].astype(F32))
    attn_low = (unit * attn_gain[...] + attn_shift[...]).astype(LOW)
    raster = raster_scr[...]
    small[5:6, :] += column_sum(raster[:, :D])
    small[6:7, :] += column_sum(raster[:, 2 * D :])
    grads = raster.astype(LOW)
    grad_wqkv[...] += tn(grads, attn_low)
    grad_in = nn(grads, wqkv[...])
    small[0:1, :] += column_sum(grad_in * unit)
    small[1:2, :] += column_sum(grad_in)
    input_grad[...] = grad_hidden + norm_back(grad_in, unit, inverse, attn_gain[...])


def attention_backward(block, core, gs_a, gs_b, hidden, g, x, ids, mixed, qkv, prob, window, consts, weights, sums):
    place, place_t, heads, _, spread = consts
    at_block = lambda width: pl.BlockSpec((BLOCK, width), lambda i, s: (s[0] * BLOCKS + block, 0))
    rows = lambda height, width: pl.BlockSpec((height, width), lambda i, s: (block, 0))
    fixed = [weights[n] for n in ("attn_gain", "attn_shift")] + [place, place_t, heads, spread]
    fixed = fixed + [weights[n] for n in ("moe_gain", "moe_shift", "router", "out_bias_t")]
    totals = [(3 * D, D), (D, D), (16, D), (192, 256)]
    before = [] if sums is None else list(sums)
    late = [x, mixed, qkv, prob, window, weights["wqkv"], weights["wproj"]] + before
    extra = [(768, 64)] if block == BLOCKS - 1 else []
    return pl.pallas_call(
        functools.partial(backward_kernel, block),
        grid_spec=pltpu.PrefetchScalarGridSpec(
            num_scalar_prefetch=1,
            grid=(1,),
            in_specs=[
                whole((BLOCK + 8, D)),
                whole((BLOCK + 8, D)),
                rows(BLOCK, D),
                at_block(D),
                at_block(1),
            ]
            + [whole(v.shape) for v in fixed]
            + [pl.BlockSpec(memory_space=pl.ANY) for v in late],
            out_specs=[whole((BLOCK, D))] + [whole(v) for v in totals + extra],
            scratch_shapes=[
                pltpu.VMEM((BLOCK, 3 * D), F32),
                pltpu.VMEM((BLOCK, D), LOW),
                pltpu.VMEM((BLOCK, D), LOW),
                pltpu.VMEM((BLOCK, D), LOW),
                pltpu.VMEM((4 * PADDED, 3 * D), LOW),
                pltpu.VMEM((48 * 64, 256), LOW),
                pltpu.VMEM((4 * PADDED, D), LOW),
                pltpu.VMEM((3 * D, D), LOW),
                pltpu.VMEM((D, D), LOW),
                pltpu.SemaphoreType.DMA((len(late),)),
            ],
        ),
        out_shape=[jax.ShapeDtypeStruct(v, F32) for v in [(BLOCK, D)] + totals + extra],
        compiler_params=pltpu.CompilerParams(vmem_limit_bytes=VMEM),
        cost_estimate=pl.CostEstimate(flops=1_000_000, bytes_accessed=100_000, transcendentals=0),
        name="attention_backward",
    )(core, gs_a, gs_b, hidden, g, ids, *fixed, *late)


def head_bias(table, lookup):
    rows = lax.dot_general(table.astype(LOW), jnp.asarray(lookup).astype(LOW), (((0,), (1,)), ((), ())), preferred_element_type=F32)
    return rows.reshape(32, D)


def position_bias(heads, fill):
    rows = heads.reshape(3, 4, 64, 64).transpose(0, 2, 1, 3).reshape(1, 3, 64, 256)
    return (rows + fill[:, None]).reshape(12, 64, 256)


def table_gradient(sums, lookup):
    rows = sums.reshape(HEADS, 4096)
    high = rows.astype(LOW)
    rest = (rows - high.astype(F32)).astype(LOW)
    turned = lookup.reshape(64, 64, 169).transpose(1, 0, 2).reshape(4096, 169)
    turned = jnp.asarray(turned).astype(LOW)
    found = nn(jnp.concatenate([high, rest]), turned)
    return (found[:HEADS] + found[HEADS:]).T


AXES = ("dp", "tensor")


def device_index(x, y, z, core):
    return (x % 2 * 16 + y % 4 * 4 + z % 4) * 4 + x // 2 % 2 * 2 + core


def pairs(move):
    places = [(x, y, z, c) for x in range(4) for y in range(4) for z in range(4) for c in range(2)]
    return [(device_index(*p), device_index(*move(*p))) for p in places]


CORE_SWAP = pairs(lambda x, y, z, c: (x, y, z, 1 - c))
FAR_SWAP = pairs(lambda x, y, z, c: ((x + 2) % 4, y, z, c))
NEAR_SWAP = pairs(lambda x, y, z, c: (x ^ 1, y, z, c))
TURN = {
    "y": [pairs(lambda x, y, z, c, s=s: (x, y + s, z, c)) for s in range(4)],
    "z": [pairs(lambda x, y, z, c, s=s: (x, y, z + s, c)) for s in range(4)],
}


PAIR = {
    "y": pairs(lambda x, y, z, c: (x, y ^ 1, z, c)),
    "z": pairs(lambda x, y, z, c: (x, y, z ^ 1, c)),
}


def send(values, table):
    return lax.ppermute(values, AXES, table)


def after(values, *others):
    return lax.optimization_barrier((values,) + others)[0]


def near_pieces(parts):
    return [quarter(v, at + shift, dim) for shift in (1, 3) for v, axis, at, dim in parts]


def near_sends(parts, pieces):
    tables = [TURN[axis][shift] for shift in (1, 3) for v, axis, at, dim in parts]
    return [send(piece, table) for piece, table in zip(pieces, tables)]


def quarter(values, index, dim):
    return lax.dynamic_index_in_dim(values, index % 4, dim, False)


def scatter_across(parts, near):
    return [
        send(after(quarter(v, at + 2, dim), near[n]), TURN[axis][2]) for n, (v, axis, at, dim) in enumerate(parts)
    ]


def scatter_total(parts, near, across):
    return [
        quarter(v, at, dim) + near[n] + near[n + len(parts)] + across[n]
        for n, (v, axis, at, dim) in enumerate(parts)
    ]


def scatter_sums(parts):
    near = [send(quarter(v, at + shift, dim), TURN[axis][shift]) for shift in (1, 3, 2) for v, axis, at, dim in parts]
    sums = scatter_total(parts, near, near[2 * len(parts) :])
    return [v.reshape((4, v.shape[0] // 4) + v.shape[1:]) for v in sums]


def gather_rows(parts):
    got = []
    for shift in (1, 3, 2):
        for n, (values, axis, place) in enumerate(parts):
            piece = after(values, got[n]) if shift == 2 and len(parts) > 1 else values
            got.append(send(piece, TURN[axis][shift]))
    fulls = []
    for n, (values, axis, place) in enumerate(parts):
        rows = values.shape[0]
        full = jnp.zeros((4 * rows,) + values.shape[1:], values.dtype)
        for shift, piece in ((0, values), (1, got[n]), (3, got[n + len(parts)]), (2, got[n + 2 * len(parts)])):
            full = lax.dynamic_update_slice_in_dim(full, piece, (place - shift) % 4 * rows, 0)
        fulls.append(full)
    return fulls


def assemble_kernel(first, core, mine, other, *refs):
    out, ready, sems = refs[-3:]
    rows = mine.shape[0]
    moves = []
    for n, (source, half) in enumerate(((mine, core[0]), (other, 1 - core[0]))):
        ready[n] = source[...].astype(out.dtype)
        target = out.at[pl.ds(pl.multiple_of(half * HALF + first, 16), rows), :]
        moves.append(pltpu.make_async_copy(ready.at[n], target, sems.at[n]))
        moves[n].start()
    for move in moves:
        move.wait()


def assemble(core, first, mine, other, kind, before):
    kept = [] if before is None else [before]
    return pl.pallas_call(
        functools.partial(assemble_kernel, first),
        grid_spec=pltpu.PrefetchScalarGridSpec(
            num_scalar_prefetch=1,
            grid=(1,),
            in_specs=[whole(mine.shape), whole(other.shape)] + [pl.BlockSpec(memory_space=pl.ANY)] * len(kept),
            out_specs=pl.BlockSpec(memory_space=pl.ANY),
            scratch_shapes=[pltpu.VMEM((2,) + mine.shape, kind), pltpu.SemaphoreType.DMA((2,))],
        ),
        out_shape=jax.ShapeDtypeStruct((2 * HALF, D), kind),
        input_output_aliases={3: 0} if kept else {},
        compiler_params=pltpu.CompilerParams(vmem_limit_bytes=VMEM),
        cost_estimate=pl.CostEstimate(flops=1_000_000, bytes_accessed=100_000, transcendentals=0),
        name="assemble",
    )(core, mine, other, *kept)


def gather_shards(far, core, own):
    over = send(own, FAR_SWAP)
    near = send(own, CORE_SWAP)
    last = send(over, CORE_SWAP)
    pick = lambda flag, a, b: jnp.where(flag == 1, a, b)
    few = [v[D:] for v in (own, near, over, last)]
    low = (pick(core, few[1], few[0]), pick(core, few[0], few[1]))
    high = (pick(core, few[3], few[2]), pick(core, few[2], few[3]))
    few = [pick(far, high[i], low[i]) for i in (0, 1)] + [pick(far, low[i], high[i]) for i in (0, 1)]
    return (own, near, over, last), few


def gather_weights(far, core, qkv_weight, qv_bias, rel_table, proj_weight, lookup):
    own = jnp.concatenate(
        [
            qkv_weight.astype(F32).transpose(0, 2, 1).reshape(3 * 96, D),
            proj_weight.astype(F32),
            head_bias(rel_table, lookup),
            jnp.pad(qv_bias.astype(F32), ((0, 6), (0, D - 96))),
        ]
    )
    whole_shards, shards = gather_shards(far, core, own)
    heads = jnp.stack([v[:32].reshape(3, 64, 64) for v in shards]).reshape(HEADS, 64, 64)
    bias = jnp.concatenate([v[32:34, :96] for v in shards], axis=1)
    return whole_shards, bias, heads


def pack_rest(shard, sums, in_bias, out_bias, lookup):
    grad_wqkv, grad_wproj, small, _, pair_sums = sums
    rows = jnp.pad(table_gradient(pair_sums, lookup).reshape(-1), (0, 8 * D - 169 * HEADS)).reshape(8, D)
    by_shard = jnp.concatenate([grad_wqkv.reshape(3, 4, 96, D), grad_wproj.reshape(1, 4, 96, D)])

    def pack(index):
        return jnp.concatenate([lax.dynamic_index_in_dim(by_shard, index, 1, False).reshape(D, D), small, rows])

    packed = pack(shard) + send(pack(shard ^ 1), CORE_SWAP)
    return jnp.concatenate([packed, in_bias, out_bias, jnp.zeros((88, D), F32)]).reshape(4, 128, D)


def shards(
    tokens_in, attn_gain, attn_shift, qkv_weight, qv_bias, rel_table, proj_weight, proj_bias, moe_gain, moe_shift,
    router_weight, expert_in, expert_in_bias, expert_out, expert_out_bias, expert_ids, cotangent,
):
    group, shard = lax.axis_index("dp"), lax.axis_index("tensor")
    at_x, at_y, at_z = group // 16, group // 4 % 4, group % 4
    far, side = shard // 2, shard % 2
    core = side.astype(jnp.int32).reshape(1)
    place, fill, lookup, heads, segment = layout_consts()
    consts = (place, place.transpose(0, 2, 1), heads, segment, heads.T)
    consts = tuple(jnp.asarray(v).astype(LOW) for v in consts)
    wide = lambda v: v.astype(F32).reshape(1, -1)

    weight_shards, bias_qv, table = gather_weights(
        far, side, qkv_weight, qv_bias, rel_table, proj_weight, lookup
    )
    router = jnp.pad(router_weight, ((0, 0), (0, 128 - EXPERTS)))
    weights = dict(
        attn_gain=wide(attn_gain),
        attn_shift=wide(attn_shift),
        bqkv=jnp.concatenate([bias_qv[0:1], jnp.zeros((1, D), F32), bias_qv[1:2]], axis=1),
        bproj=wide(proj_bias),
        moe_gain=wide(moe_gain),
        moe_shift=wide(moe_shift),
        router=router,
        out_bias_pad=jnp.pad(expert_out_bias, ((0, 128 - EXPERTS), (0, 0))),
        out_bias_t=jnp.pad(expert_out_bias, ((0, 128 - EXPERTS), (0, 0))).T,
    )
    bias = position_bias(table, jnp.asarray(fill))
    spot, dest, chunks = sort_plan(expert_ids)
    meta = jnp.stack([spot, expert_ids.reshape(TILES, TILE)], axis=1)
    place_here = jnp.stack([side, shard]).astype(jnp.int32)
    hidden, base, second, gate, mixed, qkv, prob, window, weights["wqkv"], weights["wproj"] = attention_forward(
        place_here, tokens_in, expert_ids, weight_shards, consts, weights, bias
    )
    second = second.reshape(HALF_TILES, TILE, D)
    second_other = send(second, CORE_SWAP)
    gate, second_other = lax.optimization_barrier((gate.reshape(HALF), second_other))
    grad_in, grad_out, in_bias, out_bias, act, gs_theirs, gg_theirs, gs_mine, gg_mine = experts(
        core, dest, chunks, second, second_other, cotangent.reshape(TILES, TILE, D), meta,
        router[:, :16].T, expert_in, expert_in_bias.astype(F32), expert_out,
    )

    sixteen = [[i * 16 + j for j in range(16)] for i in range(2)]
    gather = lambda v: lax.all_gather(v, "dp", axis=0, axis_index_groups=sixteen, tiled=True)
    sum_out = lax.psum_scatter(grad_out, "dp", scatter_dimension=0, axis_index_groups=sixteen, tiled=True)
    cells = grad_in.reshape(4, 4, 2, 96, D)
    first = [(cells[:, :, 0], "y", at_y, 0), (cells[:, :, 1], "z", at_z, 1)]
    pieces = near_pieces(first)

    gs_theirs = send(gs_theirs, CORE_SWAP).reshape(HALF, D)
    gg = gg_mine.reshape(HALF) + send(gg_theirs.reshape(HALF), CORE_SWAP)
    gg = jnp.pad(gg.reshape(BLOCKS, BLOCK), ((0, 0), (0, 8 * D - BLOCK))).reshape(BLOCKS, 8, D)
    gs_mine = gs_mine.reshape(HALF, D)
    pieces, gs_theirs, gs_mine = lax.optimization_barrier((pieces, gs_theirs, gs_mine))
    near = near_sends(first, pieces)

    def chip_block(b, mine, theirs):
        return jnp.concatenate([mine[b * BLOCK : (b + 1) * BLOCK] + theirs[b * BLOCK : (b + 1) * BLOCK], gg[b]])

    gs = [chip_block(0, gs_mine, gs_theirs)]
    gs_far = [send(gs[0], FAR_SWAP)]
    later = lax.optimization_barrier((gs_mine, gs_theirs, gs[0]))
    gs = gs + [chip_block(b, later[0], later[1]) for b in (1, 2)]

    def attend(b, sums):
        return attention_backward(
            b, core, gs[b], gs_far[b], hidden, cotangent, tokens_in, expert_ids, mixed, qkv, prob, window,
            consts, weights, sums,
        )

    act, gs[1], gs[2] = lax.optimization_barrier((act, gs[1], gs[2]))
    ep_theirs, ep_mine = experts_output(core, dest, chunks, act, meta, expert_out)
    ep_mine, ep_theirs, near = lax.optimization_barrier((ep_mine, ep_theirs, near))
    gs_far.append(send(after(gs[1], near[0]), FAR_SWAP))
    gs_far.append(send(after(gs[2], near[0]), FAR_SWAP))
    ep_theirs, gs_far[0] = lax.optimization_barrier((ep_theirs, gs_far[0]))
    ep_theirs = send(ep_theirs, CORE_SWAP)
    grad_0, *sums = attend(0, None)
    near, gs_far[1], grad_0, ep_theirs = lax.optimization_barrier((near, gs_far[1], grad_0, ep_theirs))
    across = scatter_across(first, near)
    ep = (ep_mine + ep_theirs).reshape(HALF, D)
    ep = [ep[a:b] for a, b in zip(CUTS, CUTS[1:])]
    gs_far[1], ep = lax.optimization_barrier((gs_far[1], ep))
    ep_far = [send(ep[0], FAR_SWAP)]
    grad_1, *sums = attend(1, sums)
    across, sum_out, gs_far[2], grad_1 = lax.optimization_barrier((across, sum_out, gs_far[2], grad_1))
    near_out = send(sum_out, NEAR_SWAP)
    halves = scatter_total(first, near, across)
    second = [(halves[0], "z", at_z), (halves[1], "y", at_y)]
    fold = [send(jnp.stack([quarter(v, at ^ 1, 0), quarter(v, at ^ 3, 0)]), PAIR[axis]) for v, axis, at in second]
    ep_far.append(send(ep[1], FAR_SWAP))
    gs_far[2], halves = lax.optimization_barrier((gs_far[2], halves))
    grad_2, *sums = attend(2, sums)
    fold, near_out, grad_2, sums, ep_far[0] = lax.optimization_barrier((fold, near_out, grad_2, sums, ep_far[0]))
    sum_out = gather(sum_out + near_out)
    kept = [quarter(v, at, 0) + got[0] for (v, axis, at), got in zip(second, fold)]
    over = [send(quarter(v, at ^ 2, 0) + got[1], TURN[axis][2]) for (v, axis, at), got in zip(second, fold)]

    hold = lax.optimization_barrier

    def half_of(n):
        block = slice(CUTS[n], CUTS[n + 1])
        return base[block] + gate[block][:, None] * (ep[n] + ep_far[n])

    def put_grad(n, grad, other, whole_grad):
        return assemble(core, n * BLOCK, grad, other, F32, whole_grad)

    def put_out(n, half, other, whole_out):
        return assemble(core, CUTS[n], half, other, LOW, whole_out)

    halves_out = [half_of(0)]
    packed = pack_rest(shard, sums, in_bias, out_bias, lookup)
    packed, over, ep_far[1] = hold((packed, over, ep_far[1]))
    sum_in = jnp.concatenate([v + got for v, got in zip(kept, over)])
    near_in = send(sum_in, NEAR_SWAP)
    ep_far.append(send(after(ep[2], sum_in), FAR_SWAP))
    halves_out.append(half_of(1))
    others = [send(v, CORE_SWAP) for v in (grad_0, grad_1, halves_out[0])]
    others, near_in = hold((others, near_in))
    sum_in = gather(sum_in + near_in)
    (packed,) = scatter_sums([(packed, "y", at_y, 0)])
    input_grad = put_grad(1, grad_1, others[1], put_grad(0, grad_0, others[0], None))
    block_out = put_out(0, halves_out[0], others[2], None)
    packed, input_grad, block_out, half_1, grad_2 = hold((packed, input_grad, block_out, halves_out[1], grad_2))
    (packed,) = scatter_sums([(packed, "z", at_z, 0)])
    other_out = send(half_1, CORE_SWAP)
    packed, other_out, ep_far[2], grad_2 = hold((packed.reshape(32, D), other_out, ep_far[2], grad_2))
    packed_near = send(packed, NEAR_SWAP)
    other_grad = send(grad_2, CORE_SWAP)
    ep_far.append(send(after(ep[3], packed_near), FAR_SWAP))
    half_2 = half_of(2)
    packed, other_grad, half_2 = hold((packed + packed_near, other_grad, half_2))
    (packed,) = gather_rows([(packed, "z", at_z)])
    other_half = send(half_2, CORE_SWAP)
    packed, other_half = hold((packed, other_half))
    (packed,) = gather_rows([(packed, "y", at_y)])
    block_out = put_out(1, half_1, other_out, block_out)
    ep_far[3], packed, block_out, other_half, other_grad = hold((ep_far[3], packed, block_out, other_half, other_grad))
    half_3 = half_of(3)
    other_last = send(half_3, CORE_SWAP)
    input_grad = put_grad(2, grad_2, other_grad, input_grad)
    block_out = put_out(2, half_2, other_half, block_out)
    block_out = put_out(3, half_3, other_last, block_out)

    few = packed[D : D + 24]
    grad_table = few[16:24].reshape(-1)[: 169 * HEADS].reshape(169, HEADS)
    return (
        block_out,
        input_grad,
        few[0],
        few[1],
        packed[:288].reshape(3, 96, D).transpose(0, 2, 1),
        lax.dynamic_slice_in_dim(few[5:7], shard * 96, 96, 1),
        lax.dynamic_slice_in_dim(grad_table, shard * 3, 3, 1),
        packed[288:384],
        few[2],
        few[3],
        few[4],
        few[8:16].T,
        sum_in.reshape(EXPERTS, D, D),
        packed[408:416],
        sum_out.reshape(EXPERTS, D, D),
        packed[416:424],
    )


def solution(mesh):
    placed = (
        P("dp", None),
        P(),
        P(),
        P(None, None, "tensor"),
        P(None, "tensor"),
        P(None, "tensor"),
        P("tensor", None),
        P(),
        P(),
        P(),
        P(),
        P(None, None, "tensor"),
        P(None, "tensor"),
        P(None, "tensor", None),
        P(),
        P("dp", None),
        P("dp", None),
    )
    return jax.shard_map(
        shards,
        mesh=mesh,
        in_specs=placed,
        out_specs=(
            P("dp", None),
            P("dp", None),
            P(),
            P(),
            P(None, None, "tensor"),
            P(None, "tensor"),
            P(None, "tensor"),
            P("tensor", None),
            P(),
            P(),
            P(),
            P(),
            P(None, None, "tensor"),
            P(None, "tensor"),
            P(None, "tensor", None),
            P(),
        ),
        check_vma=False,
    )
```
